32 devices in a mesh: seq: 8 (over y, x, core), fsdp: 4 (over z).
Axes of the slice: x: 2, y: 2, z: 4, core: 2. Of those that a mesh axis runs over, the one named last changes fastest.
Arguments:
- tokens: bfloat16 [4, 2048, 2048], P('fsdp', 'seq'), may hold values from -6 to 6
- w_in: bfloat16 [2048, 2304], P('fsdp'), may hold values from -0.125 to 0.125
- log_decay: float32 [4, 32, 2048], P('fsdp', None, 'seq'), may hold values from -2 to 0, as said below
- grad_out: bfloat16 [4, 2048, 2048], P('fsdp', 'seq'), may hold values from -6 to 6
Outputs:
- mixer_out: bfloat16 [4, 2048, 2048], P('fsdp', 'seq')
- grad_tokens: bfloat16 [4, 2048, 2048], P('fsdp', 'seq')
- grad_weights: float32 [2048, 2304], P(('seq', 'fsdp'))
The draws below stay inside these ranges and needn't reach their ends.
Inputs may be any that keep to these rules, and one draw needn't show every extreme that they name: `log_decay`: each entry is the logarithm of a decay factor below one.
All inputs are finite; a program needn't handle non-finite values.
Results may differ from the reference program's by a relative error of at most 0.015.
Values may be sent and summed in bfloat16 or wider, within the bound.
No kernel may reach another device: no remote copies, remote signals or barrier semaphores. Data moves between devices by JAX's collectives and lax.ppermute only.
A program may use at most 192 MiB of HBM per device.

```python
import math
import jax
import jax.numpy as jnp
from jax import lax

D = 2048
H = 32
P_SIZE = 64
N = 128
BLOCK = 256
TOK_DEV = 256
LENGTH = 2048
SEQS = 4
COLS = 2304


def draw_log_decay(key, part):
    streams = jax.random.split(key, 7)
    fast_share = 0.5
    slow_rate = jnp.exp(jax.random.uniform(streams[1], (SEQS, H, 1), minval=math.log(0.05), maxval=math.log(0.3))) / LENGTH
    fast_heads = jax.random.bernoulli(streams[0], fast_share, (SEQS, H, 1))
    fast_rate = jnp.exp(jax.random.uniform(streams[2], (SEQS, H, 1), minval=math.log(1.0 / 50.0), maxval=math.log(1.0 / 30.0)))
    head_rate = jnp.where(fast_heads, fast_rate, slow_rate)
    spans = LENGTH // TOK_DEV
    device_factor = jnp.exp(jax.random.uniform(streams[3], (SEQS, H, spans, 1), minval=-math.log(2.0), maxval=math.log(2.0)))
    device_factor = jnp.broadcast_to(device_factor, (SEQS, H, spans, TOK_DEV)).reshape(SEQS, H, LENGTH)
    roughness = jax.random.uniform(streams[4], (SEQS, H, LENGTH), minval=0.7, maxval=1.4)
    final_output = -head_rate * device_factor * roughness
    token_places = jax.random.randint(streams[5], (SEQS, 2), 0, LENGTH)
    dropped_tokens = jnp.log(jax.random.uniform(streams[6], (SEQS, H, 2), minval=0.55, maxval=0.8))
    token_position = lax.broadcasted_iota(jnp.int32, (SEQS, 1, LENGTH), 2)
    for spike_amount in range(2):
        matched_entry = token_position == token_places[:, spike_amount][:, None, None]
        final_output = final_output + jnp.where(matched_entry, dropped_tokens[:, :, spike_amount][:, :, None], 0.0)
    return final_output.astype(jnp.float32)


def strengthened(values, stream_key, source, target, shards_of, factor):
    owner, partner = [(jnp.arange(values.shape[axis_at]) // (values.shape[axis_at] // shards_of)).reshape([-1 if axis == axis_at else 1 for axis in range(values.ndim)]) for axis_at in (source, target)]
    chosen = jax.random.permutation(stream_key, shards_of)[partner]
    strong = (owner == chosen) | (owner == (partner + shards_of // 2) % shards_of)
    return jnp.where(strong, factor * values, values)


def block_levels(rng, shape, shards, low, largest):
    gain = 1.0
    for dim, parts in shards:
        draws = jax.random.uniform(jax.random.fold_in(jax.random.fold_in(rng, 6), dim), (parts,), jnp.float32, low / len(shards), largest / len(shards))
        gain = gain * jnp.repeat(jnp.exp(draws), shape[dim] // parts).reshape((-1,) + (1,) * (len(shape) - 1 - dim))
    return gain


def bell_draw(rng, shape, deviation, reach, cuts=(), kind=jnp.bfloat16):
    loudness = block_levels(rng, shape, cuts, -0.22, 0.18) if cuts else 1.0
    result = jax.random.normal(rng, shape, jnp.float32) * deviation * loudness
    return jnp.minimum(jnp.maximum(result, -reach), reach).astype(kind)


def noise_with(stream_key, dims, width, reach, cuts, heavy, dtype=jnp.bfloat16):
    result = width * jax.random.normal(stream_key, dims, jnp.float32)
    if cuts:
        result = result * block_levels(stream_key, dims, cuts, -0.22, 0.18)
    return jnp.clip(strengthened(result, jax.random.fold_in(stream_key, 3), *heavy), -reach, reach).astype(dtype)


def setup_inputs(seed: int = 0) -> dict:
    keys = jax.random.split(jax.random.key(seed), 5)
    return {
        "tokens": noise_with(keys[0], (SEQS, LENGTH, D), 1.0, 6.0, ((0, 4), (1, 8)), (1, 2, 8, 2.0)),
        "w_in": bell_draw(keys[1], (D, COLS), D ** -0.5, 0.125, ((0, 4),)),
        "log_decay": draw_log_decay(jax.random.fold_in(keys[4], 71), 0),
        "grad_out": bell_draw(keys[3], (SEQS, LENGTH, H * P_SIZE), 1.0, 6.0, ((0, 4), (1, 8))),
    }


highest = lax.Precision.HIGHEST
epsilon = 1e-05

def block_chain(log_rates, terms, backward, start_state):

    def advance(carried, packed):
        log_k, term_k = packed
        return (jnp.exp(log_k)[:, None, None] * carried + term_k, carried)
    finish, inputs = lax.scan(advance, start_state, (log_rates, terms), reverse=backward)
    return (inputs, finish)

def decay_matrix(cumulative, log_rates):
    extent = cumulative.shape[-1]
    row_idx = lax.broadcasted_iota(jnp.int32, (extent, extent), 0)
    col_idx = lax.broadcasted_iota(jnp.int32, (extent, extent), 1)
    later_gap = cumulative[:, :, None] - cumulative[:, None, :]
    exclusive = cumulative - log_rates
    earlier_gap = exclusive[:, None, :] - exclusive[:, :, None]
    exponent = jnp.where(row_idx > col_idx, later_gap, jnp.where(row_idx < col_idx, earlier_gap, 0.0))
    return jnp.exp(exponent) + (row_idx == col_idx).astype(jnp.float32)

def mix_sequence(xbc_float, log_rates):
    block_count = LENGTH // BLOCK
    inner_width = H * P_SIZE
    values = xbc_float[:, :inner_width].reshape(block_count, BLOCK, H, P_SIZE)
    key_rows = xbc_float[:, inner_width:inner_width + N].reshape(block_count, BLOCK, N)
    queries = xbc_float[:, inner_width + N:].reshape(block_count, BLOCK, N)
    blocked = log_rates.reshape(H, block_count, BLOCK).transpose(1, 0, 2)
    cumulative = jnp.cumsum(blocked, axis=-1)
    totals = cumulative[:, :, -1]
    to_end = jnp.exp(totals[:, :, None] - cumulative)
    from_start = jnp.exp(cumulative - blocked)
    end_terms = jnp.einsum('khq,kqhp,kqn->khpn', to_end, values, key_rows, precision=highest)
    start_terms = jnp.einsum('khq,kqhp,kqn->khpn', from_start, values, key_rows, precision=highest)
    zero_state = jnp.zeros((H, P_SIZE, N), jnp.float32)
    fwd_in, _ = block_chain(totals, end_terms, False, zero_state)
    rev_next, _ = block_chain(totals, start_terms, True, zero_state)

    def block_values(packed):
        block_vals, block_keys, block_queries, block_cumul, block_logs, block_total, state_in, state_next = packed
        affinity = jnp.dot(block_queries, block_keys.T, precision=highest)
        weighted = affinity[None] * decay_matrix(block_cumul, block_logs)
        inner_part = jnp.einsum('hij,jhp->ihp', weighted, block_vals, precision=highest)
        enter_weight = jnp.exp(block_cumul).T[:, :, None]
        leave_weight = jnp.exp(block_total[:, None] - (block_cumul - block_logs)).T[:, :, None]
        carried_in = jnp.einsum('qn,hpn->qhp', block_queries, state_in, precision=highest) * enter_weight
        carried_back = jnp.einsum('qn,hpn->qhp', block_queries, state_next, precision=highest) * leave_weight
        return inner_part + carried_in + carried_back
    mixture = lax.map(jax.checkpoint(block_values), (values, key_rows, queries, cumulative, blocked, totals, fwd_in, rev_next))
    row_scale = jnp.sqrt(lax.optimization_barrier(jnp.mean(mixture * mixture, axis=-1)) + epsilon)
    normed = mixture / row_scale[..., None]
    return normed.reshape(LENGTH, H * P_SIZE)

def forward_pass(xbc_rows, log_rates):
    return mix_sequence(xbc_rows.astype(jnp.float32), log_rates).astype(jnp.bfloat16)

def reference(tokens, w_in, log_decay, grad_out):
    flat_tokens = tokens.reshape(SEQS * LENGTH, D)
    xbc_rows = jnp.dot(flat_tokens, w_in, preferred_element_type=jnp.float32).astype(jnp.bfloat16)
    xbc_rows = lax.optimization_barrier(xbc_rows).reshape(SEQS, LENGTH, COLS)

    def per_sequence(packed):
        seq_rows, seq_logs, seq_grad = packed
        outputs, pullback = jax.vjp(lambda inputs: forward_pass(inputs, seq_logs), seq_rows)
        return (outputs, pullback(seq_grad)[0])
    mixer_out, grad_proj = lax.map(per_sequence, (xbc_rows, log_decay, grad_out))
    flat_grad = grad_proj.reshape(SEQS * LENGTH, COLS)
    grad_tokens = jnp.dot(flat_grad, w_in.T, preferred_element_type=jnp.float32).astype(jnp.bfloat16)
    grad_weights = jnp.dot(flat_tokens.T, flat_grad, preferred_element_type=jnp.float32)
    return (mixer_out, grad_tokens.reshape(SEQS, LENGTH, D), grad_weights)
```

```python
import functools

import jax
import jax.numpy as jnp
from jax import lax
from jax.experimental import pallas as pl
from jax.experimental.pallas import tpu as pltpu
from jax.sharding import PartitionSpec as P

CHUNK = 128
EPSILON = 1e-05
VMEM_LIMIT = 50 * 1024 * 1024

f32 = jnp.float32
bf16 = jnp.bfloat16


def dot_nn(a, b):
    return lax.dot_general(a, b, (((1,), (0,)), ((), ())), preferred_element_type=f32)


def dot_nt(a, b):
    return lax.dot_general(a, b, (((1,), (1,)), ((), ())), preferred_element_type=f32)


def dot_tn(a, b):
    return lax.dot_general(a, b, (((0,), (0,)), ((), ())), preferred_element_type=f32)


def by_head(rows, heads, head_size):
    if heads == 1:
        return rows
    lane = lax.broadcasted_iota(jnp.int32, rows.shape, 1)
    parts = []
    for h in range(heads):
        inside = (lane >= h * head_size) & (lane < (h + 1) * head_size)
        parts.append(jnp.where(inside, rows, jnp.zeros_like(rows)))
    return jnp.concatenate(parts, axis=0)


def decayed(affinity, decays, heads):
    tiled = jnp.concatenate([affinity] * heads, axis=1) if heads > 1 else affinity
    return (tiled * decays.astype(f32)).astype(bf16)


def forward_kernel(
    heads, head_size,
    x_ref, b_ref, c_ref, m_ref, te_ref, fs_ref, en_ref, lv_ref, dt_ref, mean_ref,
    z_ref, rs_ref, sf_ref, rn_ref,
    carry,
):
    chunks = dt_ref.shape[0]
    state_size = b_ref.shape[1]
    carry[...] = jnp.zeros_like(carry)

    def reverse_states(i, _):
        k = chunks - 1 - i
        rows = pl.ds(pl.multiple_of(k * CHUNK, CHUNK), CHUNK)
        state = pl.ds(pl.multiple_of(k * state_size, state_size), state_size)
        rn_ref[state, :] = carry[...].astype(bf16)
        term = dot_tn(b_ref[rows, :], x_ref[rows, :] * fs_ref[rows, :])
        carry[...] = dt_ref[k] * carry[...] + term
        return 0

    lax.fori_loop(0, chunks, reverse_states, 0, unroll=2)
    carry[...] = jnp.zeros_like(carry)

    def outputs(k, _):
        rows = pl.ds(pl.multiple_of(k * CHUNK, CHUNK), CHUNK)
        state = pl.ds(pl.multiple_of(k * state_size, state_size), state_size)
        x, b, c = x_ref[rows, :], b_ref[rows, :], c_ref[rows, :]
        state_in = carry[...].astype(bf16)
        sf_ref[state, :] = state_in
        weights = decayed(dot_nt(c, b), m_ref[rows, :], heads)
        y = dot_nn(weights, by_head(x, heads, head_size))
        y = y + en_ref[rows, :].astype(f32) * dot_nn(c, state_in)
        y = y + lv_ref[rows, :].astype(f32) * dot_nn(c, rn_ref[state, :])
        mean_square = dot_nn((y * y).astype(bf16), mean_ref[...])
        inverse = lax.rsqrt(mean_square + EPSILON)
        z_ref[rows, :] = (y * inverse).astype(bf16)
        rs_ref[rows, :] = inverse.astype(bf16)
        carry[...] = dt_ref[k] * carry[...] + dot_tn(b, x * te_ref[rows, :])
        return 0

    lax.fori_loop(0, chunks, outputs, 0, unroll=2)


def backward_kernel(
    heads, head_size,
    x_ref, b_ref, c_ref, m_ref, mt_ref, te_ref, fs_ref, en_ref, lv_ref, dt_ref, mean_ref,
    z_ref, rs_ref, sf_ref, rn_ref, g_ref,
    dx_ref, db_ref, dc_ref,
    carry, dy_ref, ge_ref,
):
    chunks = dt_ref.shape[0]
    state_size = b_ref.shape[1]
    carry[...] = jnp.zeros_like(carry)

    def end_adjoints(i, _):
        k = chunks - 1 - i
        rows = pl.ds(pl.multiple_of(k * CHUNK, CHUNK), CHUNK)
        state = pl.ds(pl.multiple_of(k * state_size, state_size), state_size)
        g, z = g_ref[rows, :].astype(f32), z_ref[rows, :].astype(f32)
        mean_gz = dot_nn((g * z).astype(bf16), mean_ref[...])
        dy = ((g - z * mean_gz) * rs_ref[rows, :].astype(f32)).astype(bf16)
        dy_ref[rows, :] = dy
        ge_ref[state, :] = carry[...].astype(bf16)
        carry[...] = dt_ref[k] * carry[...] + dot_tn(c_ref[rows, :], dy * en_ref[rows, :])
        return 0

    lax.fori_loop(0, chunks, end_adjoints, 0, unroll=2)
    carry[...] = jnp.zeros_like(carry)

    def gradients(k, _):
        rows = pl.ds(pl.multiple_of(k * CHUNK, CHUNK), CHUNK)
        state = pl.ds(pl.multiple_of(k * state_size, state_size), state_size)
        x, b, c, dy = x_ref[rows, :], b_ref[rows, :], c_ref[rows, :], dy_ref[rows, :]
        te, fs, en, lv = te_ref[rows, :], fs_ref[rows, :], en_ref[rows, :], lv_ref[rows, :]
        ge, gs = ge_ref[state, :], carry[...].astype(bf16)
        m = m_ref[rows, :]
        grad_weights = dot_nt(dy, by_head(x, heads, head_size)) * m.astype(f32)
        da = grad_weights[:, :CHUNK]
        for h in range(1, heads):
            da = da + grad_weights[:, h * CHUNK : (h + 1) * CHUNK]
        da = da.astype(bf16)
        turned = decayed(dot_nt(b, c), mt_ref[rows, :], heads)
        dx = dot_nn(turned, by_head(dy, heads, head_size))
        dx = dx + te.astype(f32) * dot_nn(b, ge)
        dx = dx + fs.astype(f32) * dot_nn(b, gs)
        dx_ref[rows, :] = dx.astype(bf16)
        dy_lv = dy * lv
        dc = dot_nn(da, b) + dot_nt(dy * en, sf_ref[state, :]) + dot_nt(dy_lv, rn_ref[state, :])
        dc_ref[rows, :] = dc.astype(bf16)
        db = dot_tn(da, c) + dot_nt(x * te, ge) + dot_nt(x * fs, gs)
        db_ref[rows, :] = db.astype(bf16)
        carry[...] = dt_ref[k] * carry[...] + dot_tn(c, dy_lv)
        return 0

    lax.fori_loop(0, chunks, gradients, 0, unroll=2)


def whole(count):
    return [pl.BlockSpec(memory_space=pltpu.VMEM)] * count


def decay_tables(log_rates, head_size):
    heads, length = log_rates.shape
    chunks = length // CHUNK
    logs = log_rates.reshape(heads, chunks, CHUNK)
    cumulative = jnp.cumsum(logs, axis=-1)
    totals = cumulative[:, :, -1:]
    exclusive = cumulative - logs

    def spread(a):
        rows = a.reshape(heads, length).T
        return jnp.repeat(jnp.exp(rows), head_size, axis=1).astype(bf16)

    to_end = spread(totals - cumulative)
    from_start = spread(exclusive)
    enter = spread(cumulative)
    leave = spread(totals - exclusive)
    chunk_decay = jnp.repeat(jnp.exp(totals[:, :, 0].T), head_size, axis=1)[:, None, :]
    row = lax.broadcasted_iota(jnp.int32, (1, CHUNK, 1, CHUNK), 1)
    col = lax.broadcasted_iota(jnp.int32, (1, CHUNK, 1, CHUNK), 3)
    by_row = lambda a: a.transpose(1, 2, 0)[:, :, :, None]
    by_col = lambda a: a.transpose(1, 0, 2)[:, None, :, :]
    below = by_row(cumulative) - by_col(cumulative)
    above = by_col(exclusive) - by_row(exclusive)
    diagonal = (row == col).astype(f32)
    decays = jnp.exp(jnp.where(row > col, below, jnp.where(row < col, above, 0.0))) + diagonal
    turned = jnp.exp(jnp.where(col > row, -below, jnp.where(col < row, -above, 0.0))) + diagonal
    decays = decays.astype(bf16).reshape(length, heads * CHUNK)
    turned = turned.astype(bf16).reshape(length, heads * CHUNK)
    return to_end, from_start, enter, leave, chunk_decay, decays, turned


def on_device(tokens, w_in, log_decay, grad_out):
    local_tokens = tokens[0]
    upstream = grad_out[0]
    token_count, hidden_width = local_tokens.shape
    head_count = log_decay.shape[1]
    inner_width = upstream.shape[1]
    head_size = inner_width // head_count
    state_size = (w_in.shape[1] - inner_width) // 2
    seq_count = lax.axis_size("seq")
    fsdp_count = lax.axis_size("fsdp")
    place = lax.axis_index("seq")
    heads = head_count // seq_count
    width = heads * head_size
    length = token_count * seq_count
    shared = 2 * state_size
    shared_part = shared // seq_count

    all_tokens = lax.all_gather(local_tokens, "seq", axis=0, tiled=True)
    own_columns = jnp.concatenate(
        [lax.dynamic_slice_in_dim(w_in, place * width, width, 1), w_in[:, inner_width:]], axis=1
    )
    w_columns = lax.all_gather(own_columns, "fsdp", axis=0, tiled=True)
    log_rates = lax.all_to_all(log_decay[0], "seq", 0, 1, tiled=True)
    g = lax.all_to_all(upstream, "seq", 1, 0, tiled=True)
    to_end, from_start, enter, leave, chunk_decay, decays, turned = decay_tables(
        log_rates, head_size
    )
    head_row = lax.broadcasted_iota(jnp.int32, (width, width), 0) // head_size
    head_col = lax.broadcasted_iota(jnp.int32, (width, width), 1) // head_size
    mean_over_head = jnp.where(head_row == head_col, 1.0 / head_size, 0.0).astype(bf16)

    xbc = jnp.dot(all_tokens, w_columns, preferred_element_type=f32).astype(bf16)
    x = xbc[:, :width]
    b = xbc[:, width : width + state_size]
    c = xbc[:, width + state_size :]

    chunks = length // CHUNK
    shape = jax.ShapeDtypeStruct
    params = pltpu.CompilerParams(vmem_limit_bytes=VMEM_LIMIT)
    z, inverse, states_in, states_next = pl.pallas_call(
        functools.partial(forward_kernel, heads, head_size),
        out_shape=[
            shape((length, width), bf16),
            shape((length, width), bf16),
            shape((chunks * state_size, width), bf16),
            shape((chunks * state_size, width), bf16),
        ],
        in_specs=whole(10),
        out_specs=whole(4),
        scratch_shapes=[pltpu.VMEM((state_size, width), f32)],
        compiler_params=params,
    )(x, b, c, decays, to_end, from_start, enter, leave, chunk_decay, mean_over_head)
    mixer_out = lax.all_to_all(z, "seq", 0, 1, tiled=True)

    dx, db, dc = pl.pallas_call(
        functools.partial(backward_kernel, heads, head_size),
        out_shape=[
            shape((length, width), bf16),
            shape((length, state_size), bf16),
            shape((length, state_size), bf16),
        ],
        in_specs=whole(16),
        out_specs=whole(3),
        scratch_shapes=[
            pltpu.VMEM((state_size, width), f32),
            pltpu.VMEM((length, width), bf16),
            pltpu.VMEM((chunks * state_size, width), bf16),
        ],
        compiler_params=params,
    )(
        x, b, c, decays, turned, to_end, from_start, enter, leave, chunk_decay, mean_over_head,
        z, inverse, states_in, states_next, g,
    )

    packed = jnp.concatenate([dx, db, dc], axis=1).reshape(seq_count, token_count, width + shared)
    arrived = lax.all_to_all(packed, "seq", 0, 0)
    grad_heads = arrived[:, :, :width]
    grad_shared = jnp.sum(arrived[:, :, width:].astype(f32), axis=0).astype(bf16)
    w_heads = lax.all_gather(w_columns[:, :width], "seq")
    grad_tokens = lax.dot_general(
        grad_heads, w_heads, (((0, 2), (0, 2)), ((), ())), preferred_element_type=f32
    ) + dot_nt(grad_shared, w_columns[:, width:])

    shared_columns = lax.all_to_all(grad_shared, "seq", 1, 0, tiled=True)
    grad_columns = jnp.concatenate([dx, shared_columns], axis=1)
    partial = dot_tn(all_tokens, grad_columns).astype(bf16)
    rows_each = hidden_width // (seq_count * fsdp_count)
    partial = partial.reshape(seq_count, fsdp_count, rows_each, width + shared_part)
    summed = lax.psum_scatter(partial, "fsdp", scatter_dimension=1, tiled=False)
    owned = lax.all_to_all(summed, "seq", 0, 0).astype(f32)
    grad_weights = jnp.concatenate(
        [
            owned[:, :, :width].transpose(1, 0, 2).reshape(rows_each, inner_width),
            owned[:, :, width:].transpose(1, 0, 2).reshape(rows_each, shared),
        ],
        axis=1,
    )
    return mixer_out[None], grad_tokens.astype(bf16)[None], grad_weights


def solution(mesh):
    return jax.shard_map(
        on_device,
        mesh=mesh,
        in_specs=(
            P("fsdp", "seq", None),
            P("fsdp", None),
            P("fsdp", None, "seq"),
            P("fsdp", "seq", None),
        ),
        out_specs=(P("fsdp", "seq", None), P("fsdp", "seq", None), P(("seq", "fsdp"), None)),
        check_vma=False,
    )
```

```python
import functools

import jax
import jax.numpy as jnp
from jax import lax
from jax.experimental import pallas as pl
from jax.experimental.pallas import tpu as pltpu
from jax.sharding import PartitionSpec as P

CHUNK = 128
EPSILON = 1e-05
VMEM_LIMIT = 50 * 1024 * 1024

f32 = jnp.float32
bf16 = jnp.bfloat16


def dot_nn(a, b):
    return lax.dot_general(a, b, (((1,), (0,)), ((), ())), preferred_element_type=f32)


def dot_nt(a, b):
    return lax.dot_general(a, b, (((1,), (1,)), ((), ())), preferred_element_type=f32)


def dot_tn(a, b):
    return lax.dot_general(a, b, (((0,), (0,)), ((), ())), preferred_element_type=f32)


def by_head(rows, heads, head_size):
    if heads == 1:
        return rows
    lane = lax.broadcasted_iota(jnp.int32, rows.shape, 1)
    parts = []
    for h in range(heads):
        inside = (lane >= h * head_size) & (lane < (h + 1) * head_size)
        parts.append(jnp.where(inside, rows, jnp.zeros_like(rows)))
    return jnp.concatenate(parts, axis=0)


def decayed(affinity, decays, heads):
    tiled = jnp.concatenate([affinity] * heads, axis=1) if heads > 1 else affinity
    return (tiled * decays.astype(f32)).astype(bf16)


def relative_chunk(k, place_ref, per_block):
    return lax.bitwise_xor(k // per_block, place_ref[0]) * per_block + k % per_block


def forward_kernel(
    heads, head_size, per_block,
    place_ref, x_ref, b_ref, c_ref, m_ref, te_ref, fs_ref, en_ref, lv_ref, dt_ref, mean_ref,
    z_ref, rs_ref, sf_ref, rn_ref,
    carry,
):
    chunks = dt_ref.shape[0]
    state_size = b_ref.shape[1]
    carry[...] = jnp.zeros_like(carry)

    def reverse_states(i, _):
        k = relative_chunk(chunks - 1 - i, place_ref, per_block)
        rows = pl.ds(pl.multiple_of(k * CHUNK, CHUNK), CHUNK)
        state = pl.ds(pl.multiple_of(k * state_size, state_size), state_size)
        rn_ref[state, :] = carry[...].astype(bf16)
        term = dot_tn(b_ref[rows, :], x_ref[rows, :] * fs_ref[rows, :])
        carry[...] = dt_ref[k] * carry[...] + term
        return 0

    lax.fori_loop(0, chunks, reverse_states, 0, unroll=2)
    carry[...] = jnp.zeros_like(carry)

    def outputs(i, _):
        k = relative_chunk(i, place_ref, per_block)
        rows = pl.ds(pl.multiple_of(k * CHUNK, CHUNK), CHUNK)
        state = pl.ds(pl.multiple_of(k * state_size, state_size), state_size)
        x, b, c = x_ref[rows, :], b_ref[rows, :], c_ref[rows, :]
        state_in = carry[...].astype(bf16)
        sf_ref[state, :] = state_in
        weights = decayed(dot_nt(c, b), m_ref[rows, :], heads)
        y = dot_nn(weights, by_head(x, heads, head_size))
        y = y + en_ref[rows, :].astype(f32) * dot_nn(c, state_in)
        y = y + lv_ref[rows, :].astype(f32) * dot_nn(c, rn_ref[state, :])
        mean_square = dot_nn((y * y).astype(bf16), mean_ref[...])
        inverse = lax.rsqrt(mean_square + EPSILON)
        z_ref[rows, :] = (y * inverse).astype(bf16)
        rs_ref[rows, :] = inverse.astype(bf16)
        carry[...] = dt_ref[k] * carry[...] + dot_tn(b, x * te_ref[rows, :])
        return 0

    lax.fori_loop(0, chunks, outputs, 0, unroll=2)


def backward_kernel(
    heads, head_size, per_block,
    place_ref, x_ref, b_ref, c_ref, m_ref, mt_ref, te_ref, fs_ref, en_ref, lv_ref, dt_ref, mean_ref,
    z_ref, rs_ref, sf_ref, rn_ref, g_ref,
    dx_ref, db_ref, dc_ref,
    carry, dy_ref, ge_ref,
):
    chunks = dt_ref.shape[0]
    state_size = b_ref.shape[1]
    carry[...] = jnp.zeros_like(carry)

    def end_adjoints(i, _):
        k = relative_chunk(chunks - 1 - i, place_ref, per_block)
        rows = pl.ds(pl.multiple_of(k * CHUNK, CHUNK), CHUNK)
        state = pl.ds(pl.multiple_of(k * state_size, state_size), state_size)
        g, z = g_ref[rows, :].astype(f32), z_ref[rows, :].astype(f32)
        mean_gz = dot_nn((g * z).astype(bf16), mean_ref[...])
        dy = ((g - z * mean_gz) * rs_ref[rows, :].astype(f32)).astype(bf16)
        dy_ref[rows, :] = dy
        ge_ref[state, :] = carry[...].astype(bf16)
        carry[...] = dt_ref[k] * carry[...] + dot_tn(c_ref[rows, :], dy * en_ref[rows, :])
        return 0

    lax.fori_loop(0, chunks, end_adjoints, 0, unroll=2)
    carry[...] = jnp.zeros_like(carry)

    def gradients(i, _):
        k = relative_chunk(i, place_ref, per_block)
        rows = pl.ds(pl.multiple_of(k * CHUNK, CHUNK), CHUNK)
        state = pl.ds(pl.multiple_of(k * state_size, state_size), state_size)
        x, b, c, dy = x_ref[rows, :], b_ref[rows, :], c_ref[rows, :], dy_ref[rows, :]
        te, fs, en, lv = te_ref[rows, :], fs_ref[rows, :], en_ref[rows, :], lv_ref[rows, :]
        ge, gs = ge_ref[state, :], carry[...].astype(bf16)
        m = m_ref[rows, :]
        grad_weights = dot_nt(dy, by_head(x, heads, head_size)) * m.astype(f32)
        da = grad_weights[:, :CHUNK]
        for h in range(1, heads):
            da = da + grad_weights[:, h * CHUNK : (h + 1) * CHUNK]
        da = da.astype(bf16)
        turned = decayed(dot_nt(b, c), mt_ref[rows, :], heads)
        dx = dot_nn(turned, by_head(dy, heads, head_size))
        dx = dx + te.astype(f32) * dot_nn(b, ge)
        dx = dx + fs.astype(f32) * dot_nn(b, gs)
        dx_ref[rows, :] = dx.astype(bf16)
        dy_lv = dy * lv
        dc = dot_nn(da, b) + dot_nt(dy * en, sf_ref[state, :]) + dot_nt(dy_lv, rn_ref[state, :])
        dc_ref[rows, :] = dc.astype(bf16)
        db = dot_tn(da, c) + dot_nt(x * te, ge) + dot_nt(x * fs, gs)
        db_ref[rows, :] = db.astype(bf16)
        carry[...] = dt_ref[k] * carry[...] + dot_tn(c, dy_lv)
        return 0

    lax.fori_loop(0, chunks, gradients, 0, unroll=2)


def project_kernel(pieces, slots, *refs):
    piece_refs, (w_ref, x_ref, b_ref, c_ref, held, sems) = refs[:pieces], refs[pieces:]
    rows = held.shape[1]
    width, state_size = x_ref.shape[1], b_ref.shape[1]

    def fetch(i):
        return pltpu.make_async_copy(piece_refs[i], held.at[i % slots], sems.at[i % slots])

    for i in range(min(slots, pieces)):
        fetch(i).start()
    for i in range(pieces):
        fetch(i).wait()
        result = dot_nn(held[i % slots], w_ref[...]).astype(bf16)
        if i + slots < pieces:
            fetch(i + slots).start()
        x_ref[i * rows : (i + 1) * rows, :] = result[:, :width]
        b_ref[i * rows : (i + 1) * rows, :] = result[:, width : width + state_size]
        c_ref[i * rows : (i + 1) * rows, :] = result[:, width + state_size :]


def weight_kernel(pieces, slots, *refs):
    piece_refs, (grad_ref, out_ref, held, total, sems) = refs[:pieces], refs[pieces:]
    rows = held.shape[1]
    hidden = held.shape[2]
    tile = 256 if hidden % 256 == 0 else hidden

    def fetch(i):
        return pltpu.make_async_copy(piece_refs[i], held.at[i % slots], sems.at[i % slots])

    for i in range(slots):
        fetch(i).start()
    for first in range(0, pieces, slots):
        for i in range(first, first + slots):
            fetch(i).wait()
        grad = grad_ref[:, first * rows : (first + slots) * rows]
        for t in range(0, hidden, tile):
            block = held[:, :, t : t + tile].reshape(slots * rows, tile)
            term = dot_nn(grad, block)
            if first > 0:
                term = term + total[:, t : t + tile]
            if first + slots < pieces:
                total[:, t : t + tile] = term
            else:
                out_ref[t : t + tile, :] = term.T.astype(bf16)
        for i in range(first + slots, min(first + 2 * slots, pieces)):
            fetch(i).start()


def whole(count):
    return [pl.BlockSpec(memory_space=pltpu.VMEM)] * count


def permute_xor(a, axis, mask):
    count = lax.axis_size(axis)
    return lax.ppermute(a, axis, [(i, i ^ mask) for i in range(count)])


def gather_halves(rows, axis):
    count = lax.axis_size(axis)
    bits = count.bit_length() - 1
    half = rows.shape[0] // 2
    upper = list(range(1, bits))
    orders = (upper + [0], upper[1:] + upper[:1] + [0])
    held = ({0: rows[:half]}, {0: rows[half:]})
    for step in range(bits):
        for part in range(2):
            mask = 1 << orders[part][step]
            for r in list(held[part]):
                held[part][r ^ mask] = permute_xor(held[part][r], axis, mask)
    return [held[part][r] for r in range(count) for part in range(2)]


def gather_line(rows, axis):
    count = lax.axis_size(axis)
    extent = rows.shape[0]
    up, down = [rows], [rows]
    for d in range(1, count):
        up.append(lax.ppermute(up[-1], axis, [(i, i + 1) for i in range(d - 1, count - 1)]))
        down.append(lax.ppermute(down[-1], axis, [(i, i - 1) for i in range(1, count - d + 1)]))
    line = jnp.concatenate(up[:0:-1] + [rows] + down[1:], axis=0)
    start = (count - 1 - lax.axis_index(axis)) * extent
    return lax.dynamic_slice_in_dim(line, start, count * extent, 0)


def exchange_xor(pieces, axis):
    return [pieces[0]] + [permute_xor(p, axis, r) for r, p in enumerate(pieces) if r > 0]


def in_order(pieces, place, axis):
    stacked = jnp.stack(pieces)
    ordered = [
        lax.dynamic_index_in_dim(stacked, lax.bitwise_xor(place, j), 0, False)
        for j in range(len(pieces))
    ]
    return jnp.concatenate(ordered, axis=axis)


def decay_tables(log_rates, head_size):
    heads, length = log_rates.shape
    chunks = length // CHUNK
    logs = log_rates.reshape(heads, chunks, CHUNK)
    cumulative = jnp.cumsum(logs, axis=-1)
    totals = cumulative[:, :, -1:]
    exclusive = cumulative - logs

    def spread(a):
        rows = a.reshape(heads, length).T
        return jnp.repeat(jnp.exp(rows), head_size, axis=1).astype(bf16)

    to_end = spread(totals - cumulative)
    from_start = spread(exclusive)
    enter = spread(cumulative)
    leave = spread(totals - exclusive)
    chunk_decay = jnp.repeat(jnp.exp(totals[:, :, 0].T), head_size, axis=1)[:, None, :]
    row = lax.broadcasted_iota(jnp.int32, (1, CHUNK, 1, CHUNK), 1)
    col = lax.broadcasted_iota(jnp.int32, (1, CHUNK, 1, CHUNK), 3)
    by_row = lambda a: a.transpose(1, 2, 0)[:, :, :, None]
    by_col = lambda a: a.transpose(1, 0, 2)[:, None, :, :]
    below = by_row(cumulative) - by_col(cumulative)
    above = by_col(exclusive) - by_row(exclusive)
    diagonal = (row == col).astype(f32)
    decays = jnp.exp(jnp.where(row > col, below, jnp.where(row < col, above, 0.0))) + diagonal
    turned = jnp.exp(jnp.where(col > row, -below, jnp.where(col < row, -above, 0.0))) + diagonal
    decays = decays.astype(bf16).reshape(length, heads * CHUNK)
    turned = turned.astype(bf16).reshape(length, heads * CHUNK)
    return to_end, from_start, enter, leave, chunk_decay, decays, turned


def on_device(tokens, w_in, log_decay, grad_out):
    local_tokens = tokens[0]
    upstream = grad_out[0]
    token_count, hidden_width = local_tokens.shape
    head_count = log_decay.shape[1]
    inner_width = upstream.shape[1]
    head_size = inner_width // head_count
    state_size = (w_in.shape[1] - inner_width) // 2
    seq_count = lax.axis_size("seq")
    fsdp_count = lax.axis_size("fsdp")
    place = lax.axis_index("seq")
    row_place = lax.axis_index("fsdp")
    heads = head_count // seq_count
    width = heads * head_size
    length = token_count * seq_count
    shared = 2 * state_size
    shared_part = shared // seq_count
    chunks = length // CHUNK
    per_block = token_count // CHUNK
    relative = range(seq_count)
    shape = jax.ShapeDtypeStruct
    params = pltpu.CompilerParams(vmem_limit_bytes=VMEM_LIMIT)

    def columns_of(array, r):
        return lax.dynamic_slice_in_dim(array, lax.bitwise_xor(place, r) * width, width, 1)

    pieces = gather_halves(local_tokens, "seq")
    parity = place % 2
    shared_half = lax.dynamic_slice_in_dim(w_in, inner_width + parity * state_size, state_size, 1)
    first_columns = gather_line(
        jnp.concatenate([columns_of(w_in, 0), shared_half], axis=1), "fsdp"
    )
    w_own, w_half = first_columns[:, :width], first_columns[:, width:]
    w_other = permute_xor(w_half, "seq", 1)
    w_shared = jnp.where(
        parity == 0,
        jnp.concatenate([w_half, w_other], axis=1),
        jnp.concatenate([w_other, w_half], axis=1),
    )
    w_columns = jnp.concatenate([w_own, w_shared], axis=1)

    log_pieces = lax.all_to_all(log_decay[0], "seq", 0, 0, tiled=True)
    log_pieces = log_pieces.reshape(seq_count, heads, token_count)
    log_rates = in_order([log_pieces[r] for r in relative], place, 1)
    g = jnp.concatenate(exchange_xor([columns_of(upstream, r) for r in relative], "seq"), axis=0)
    to_end, from_start, enter, leave, chunk_decay, decays, turned = decay_tables(
        log_rates, head_size
    )
    head_row = lax.broadcasted_iota(jnp.int32, (width, width), 0) // head_size
    head_col = lax.broadcasted_iota(jnp.int32, (width, width), 1) // head_size
    mean_over_head = jnp.where(head_row == head_col, 1.0 / head_size, 0.0).astype(bf16)

    count = len(pieces)
    slots = min(count, 16)
    streamed = [pl.BlockSpec(memory_space=pl.ANY)] * count
    x, b, c = pl.pallas_call(
        functools.partial(project_kernel, count, slots),
        out_shape=[
            shape((length, width), bf16),
            shape((length, state_size), bf16),
            shape((length, state_size), bf16),
        ],
        in_specs=streamed + whole(1),
        out_specs=whole(3),
        scratch_shapes=[
            pltpu.VMEM((slots,) + pieces[0].shape, bf16),
            pltpu.SemaphoreType.DMA((slots,)),
        ],
        compiler_params=params,
        cost_estimate=pl.CostEstimate(
            flops=2 * length * hidden_width * (width + shared),
            bytes_accessed=2 * length * hidden_width,
            transcendentals=0,
        ),
    )(*pieces, w_columns)

    scalar = [pl.BlockSpec(memory_space=pltpu.SMEM)]
    place_word = place.astype(jnp.int32).reshape(1)
    mixer_cost = pl.CostEstimate(
        flops=60 * length * width * CHUNK, bytes_accessed=40 * length * width, transcendentals=0
    )
    z, inverse, states_in, states_next = pl.pallas_call(
        functools.partial(forward_kernel, heads, head_size, per_block),
        out_shape=[
            shape((length, width), bf16),
            shape((length, width), bf16),
            shape((chunks * state_size, width), bf16),
            shape((chunks * state_size, width), bf16),
        ],
        in_specs=scalar + whole(10),
        out_specs=whole(4),
        scratch_shapes=[pltpu.VMEM((state_size, width), f32)],
        compiler_params=params,
        cost_estimate=mixer_cost,
    )(place_word, x, b, c, decays, to_end, from_start, enter, leave, chunk_decay, mean_over_head)
    blocks = lambda a: [a[r * token_count : (r + 1) * token_count] for r in relative]
    mixer_out = in_order(exchange_xor(blocks(z), "seq"), place, 1)

    rest = jnp.concatenate([columns_of(w_in, r) for r in relative if r % 2 == 0 and r > 0], axis=1)
    rest, first_columns = lax.optimization_barrier((rest, first_columns))
    w_even = gather_line(rest, "fsdp")
    w_even = jnp.concatenate([w_own, w_even], axis=1)
    w_odd = permute_xor(w_even, "seq", 1)

    dx, db, dc = pl.pallas_call(
        functools.partial(backward_kernel, heads, head_size, per_block),
        out_shape=[
            shape((length, width), bf16),
            shape((length, state_size), bf16),
            shape((length, state_size), bf16),
        ],
        in_specs=scalar + whole(16),
        out_specs=whole(3),
        scratch_shapes=[
            pltpu.VMEM((state_size, width), f32),
            pltpu.VMEM((length, width), bf16),
            pltpu.VMEM((chunks * state_size, width), bf16),
        ],
        compiler_params=params,
        cost_estimate=mixer_cost,
    )(
        place_word, x, b, c, decays, turned, to_end, from_start, enter, leave, chunk_decay,
        mean_over_head, z, inverse, states_in, states_next, g,
    )

    shared_grads = exchange_xor(blocks(jnp.concatenate([db, dc], axis=1)), "seq")
    head_grads = exchange_xor(blocks(dx), "seq")
    grad_shared = sum(a.astype(f32) for a in shared_grads).astype(bf16)
    even_grads = jnp.concatenate([head_grads[r] for r in relative if r % 2 == 0], axis=1)
    odd_grads = jnp.concatenate([head_grads[r] for r in relative if r % 2 == 1], axis=1)
    grad_tokens = dot_nt(even_grads, w_even) + dot_nt(odd_grads, w_odd)
    grad_tokens = grad_tokens + dot_nt(grad_shared, w_shared)

    rows_each = hidden_width // (seq_count * fsdp_count)

    def weight_columns(grad_t):
        columns = grad_t.shape[0]
        partial = pl.pallas_call(
            functools.partial(weight_kernel, count, slots),
            out_shape=shape((hidden_width, columns), bf16),
            in_specs=streamed + whole(1),
            out_specs=whole(1)[0],
            scratch_shapes=[
                pltpu.VMEM((slots,) + pieces[0].shape, bf16),
                pltpu.VMEM((columns, hidden_width), f32),
                pltpu.SemaphoreType.DMA((slots,)),
            ],
            compiler_params=params,
            cost_estimate=pl.CostEstimate(
                flops=2 * length * hidden_width * columns,
                bytes_accessed=2 * length * hidden_width,
                transcendentals=0,
            ),
        )(*pieces, grad_t)
        partial = partial.reshape(seq_count, fsdp_count, rows_each, columns)
        parts = [
            lax.dynamic_index_in_dim(partial, lax.bitwise_xor(row_place, k), 1, False)
            for k in range(fsdp_count)
        ]
        arrived = exchange_xor(parts, "fsdp")
        summed = sum(a.astype(f32) for a in arrived).astype(bf16)
        owned = lax.all_to_all(summed, "seq", 0, 0).astype(f32)
        return owned.transpose(1, 0, 2).reshape(rows_each, seq_count * columns)

    head_part = weight_columns(dx.T)
    turned_shared = grad_shared.T.reshape(seq_count, shared_part, token_count)
    sent = [
        lax.dynamic_index_in_dim(turned_shared, lax.bitwise_xor(place, r), 0, False)
        for r in relative
    ]
    shared_t = jnp.concatenate(exchange_xor(sent, "seq"), axis=1)
    grad_weights = jnp.concatenate([head_part, weight_columns(shared_t)], axis=1)
    return mixer_out[None], grad_tokens.astype(bf16)[None], grad_weights


def solution(mesh):
    return jax.shard_map(
        on_device,
        mesh=mesh,
        in_specs=(
            P("fsdp", "seq", None),
            P("fsdp", None),
            P("fsdp", None, "seq"),
            P("fsdp", "seq", None),
        ),
        out_specs=(P("fsdp", "seq", None), P("fsdp", "seq", None), P(("seq", "fsdp"), None)),
        check_vma=False,
    )
```

```python
import functools

import jax
import jax.numpy as jnp
from jax import lax
from jax.experimental import pallas as pl
from jax.experimental.pallas import tpu as pltpu
from jax.sharding import PartitionSpec as P

CHUNK = 128
EPSILON = 1e-05
VMEM_LIMIT = 60 * 1024 * 1024

f32 = jnp.float32
bf16 = jnp.bfloat16


def dot_nn(a, b):
    return lax.dot_general(a, b, (((1,), (0,)), ((), ())), preferred_element_type=f32)


def dot_nt(a, b):
    return lax.dot_general(a, b, (((1,), (1,)), ((), ())), preferred_element_type=f32)


def dot_tn(a, b):
    return lax.dot_general(a, b, (((0,), (0,)), ((), ())), preferred_element_type=f32)


def by_head(rows, heads, head_size):
    if heads == 1:
        return rows
    lane = lax.broadcasted_iota(jnp.int32, rows.shape, 1)
    parts = []
    for h in range(heads):
        inside = (lane >= h * head_size) & (lane < (h + 1) * head_size)
        parts.append(jnp.where(inside, rows, jnp.zeros_like(rows)))
    return jnp.concatenate(parts, axis=0)


def decayed(affinity, decays, heads):
    tiled = jnp.concatenate([affinity] * heads, axis=1) if heads > 1 else affinity
    return (tiled * decays.astype(f32)).astype(bf16)


def mixer_kernel(
    sources, arrays, slots, group, blocks, heads, head_size, places_ref, *refs
):
    array_refs, refs = refs[:arrays], refs[arrays:]
    w_hbm, refs = refs[:blocks], refs[blocks:]
    table_hbm, g_hbm, refs = refs[:7], refs[7], refs[8:]
    z_hbm, grads_hbm, refs = refs[0], refs[1], refs[2:]
    te_ref, fs_ref, en_ref, lv_ref, dt_ref, m_ref, mt_ref, refs = *refs[:7], refs[7:]
    g_ref, z_ref, grads_ref, held, w_ref, x_ref, b_ref, c_ref, refs = *refs[:8], refs[8:]
    rs_ref, sf_ref, rn_ref, dy_ref, ge_ref, mean_ref, carry, sems, loads, stores = refs
    pieces = len(sources)
    rows_each = held.shape[1]
    width = x_ref.shape[1]
    state_size = b_ref.shape[1]
    extent = w_ref.shape[0] // blocks
    chunks = dt_ref.shape[0]
    place, row_place = places_ref[0], places_ref[1]

    def fetch(i):
        array, start = sources[i]
        source = array_refs[array].at[pl.ds(start, rows_each)]
        return pltpu.make_async_copy(source, held.at[i % slots], sems.at[i % slots])

    w_loads = []
    for k in range(blocks):
        offset = pl.multiple_of(lax.bitwise_xor(row_place, k) * extent, extent)
        target = w_ref.at[pl.ds(offset, extent)]
        w_loads.append(pltpu.make_async_copy(w_hbm[k], target, loads.at[8 + k]))
    table_refs = (te_ref, fs_ref, en_ref, lv_ref, dt_ref, m_ref, mt_ref)
    table_loads = [
        pltpu.make_async_copy(source, target, loads.at[n])
        for n, (source, target) in enumerate(zip(table_hbm, table_refs))
    ]
    g_load = pltpu.make_async_copy(g_hbm, g_ref, loads.at[7])
    for load in w_loads:
        load.start()
    for i in range(slots):
        fetch(i).start()
    for load in table_loads:
        load.start()
    g_load.start()

    head_row = lax.broadcasted_iota(jnp.int32, (width, width), 0)
    head_col = lax.broadcasted_iota(jnp.int32, (width, width), 1)
    same = jnp.zeros((width, width), jnp.bool_)
    for h in range(heads):
        low, high = h * head_size, (h + 1) * head_size
        same |= (head_row >= low) & (head_row < high) & (head_col >= low) & (head_col < high)
    mean_ref[...] = jnp.where(same, 1.0 / head_size, 0.0).astype(bf16)

    for load in w_loads:
        load.wait()
    for first in range(0, pieces, group):
        for i in range(first, first + group):
            fetch(i).wait()
        slot = first % slots
        block = held[slot : slot + group].reshape(group * rows_each, held.shape[2])
        result = dot_nn(block, w_ref[...]).astype(bf16)
        for i in range(first, first + group):
            if i + slots < pieces:
                fetch(i + slots).start()
            offset = (2 * lax.bitwise_xor(place, i // 2) + i % 2) * rows_each
            target = pl.ds(pl.multiple_of(offset, rows_each), rows_each)
            part = result[(i - first) * rows_each : (i - first + 1) * rows_each]
            x_ref[target, :] = part[:, :width]
            b_ref[target, :] = part[:, width : width + state_size]
            c_ref[target, :] = part[:, width + state_size :]
    for load in table_loads:
        load.wait()

    def spans(k):
        rows = pl.ds(pl.multiple_of(k * CHUNK, CHUNK), CHUNK)
        return rows, pl.ds(pl.multiple_of(k * state_size, state_size), state_size)

    carry[...] = jnp.zeros_like(carry)

    def reverse_states(i, _):
        k = chunks - 1 - i
        rows, state = spans(k)
        rn_ref[state, :] = carry[...].astype(bf16)
        term = dot_tn(b_ref[rows, :], x_ref[rows, :] * fs_ref[rows, :])
        carry[...] = dt_ref[k] * carry[...] + term
        return 0

    lax.fori_loop(0, chunks, reverse_states, 0, unroll=2)
    carry[...] = jnp.zeros_like(carry)

    def outputs(k, _):
        rows, state = spans(k)
        x, b, c = x_ref[rows, :], b_ref[rows, :], c_ref[rows, :]
        state_in = carry[...].astype(bf16)
        sf_ref[state, :] = state_in
        weights = decayed(dot_nt(c, b), m_ref[rows, :], heads)
        y = dot_nn(weights, by_head(x, heads, head_size))
        y = y + en_ref[rows, :].astype(f32) * dot_nn(c, state_in)
        y = y + lv_ref[rows, :].astype(f32) * dot_nn(c, rn_ref[state, :])
        mean_square = dot_nn((y * y).astype(bf16), mean_ref[...])
        inverse = lax.rsqrt(mean_square + EPSILON)
        z_ref[rows, :] = (y * inverse).astype(bf16)
        rs_ref[rows, :] = inverse.astype(bf16)
        carry[...] = dt_ref[k] * carry[...] + dot_tn(b, x * te_ref[rows, :])
        return 0

    lax.fori_loop(0, chunks, outputs, 0, unroll=2)
    z_store = pltpu.make_async_copy(z_ref, z_hbm, stores.at[0])
    z_store.start()
    g_load.wait()
    carry[...] = jnp.zeros_like(carry)

    def end_adjoints(i, _):
        k = chunks - 1 - i
        rows, state = spans(k)
        g, z = g_ref[rows, :].astype(f32), z_ref[rows, :].astype(f32)
        mean_gz = dot_nn((g * z).astype(bf16), mean_ref[...])
        dy = ((g - z * mean_gz) * rs_ref[rows, :].astype(f32)).astype(bf16)
        dy_ref[rows, :] = dy
        ge_ref[state, :] = carry[...].astype(bf16)
        carry[...] = dt_ref[k] * carry[...] + dot_tn(c_ref[rows, :], dy * en_ref[rows, :])
        return 0

    lax.fori_loop(0, chunks, end_adjoints, 0, unroll=2)
    carry[...] = jnp.zeros_like(carry)

    def gradients(k, _):
        rows, state = spans(k)
        x, b, c, dy = x_ref[rows, :], b_ref[rows, :], c_ref[rows, :], dy_ref[rows, :]
        te, fs, en, lv = te_ref[rows, :], fs_ref[rows, :], en_ref[rows, :], lv_ref[rows, :]
        ge, gs = ge_ref[state, :], carry[...].astype(bf16)
        grad_weights = dot_nt(dy, by_head(x, heads, head_size)) * m_ref[rows, :].astype(f32)
        da = grad_weights[:, :CHUNK]
        for h in range(1, heads):
            da = da + grad_weights[:, h * CHUNK : (h + 1) * CHUNK]
        da = da.astype(bf16)
        turned = decayed(dot_nt(b, c), mt_ref[rows, :], heads)
        dx = dot_nn(turned, by_head(dy, heads, head_size))
        dx = dx + te.astype(f32) * dot_nn(b, ge)
        dx = dx + fs.astype(f32) * dot_nn(b, gs)
        grads_ref[rows, :width] = dx.astype(bf16)
        dy_lv = dy * lv
        dc = dot_nn(da, b) + dot_nt(dy * en, sf_ref[state, :]) + dot_nt(dy_lv, rn_ref[state, :])
        db = dot_tn(da, c) + dot_nt(x * te, ge) + dot_nt(x * fs, gs)
        grads_ref[rows, width : width + state_size] = db.astype(bf16)
        grads_ref[rows, width + state_size :] = dc.astype(bf16)
        carry[...] = dt_ref[k] * carry[...] + dot_tn(c, dy_lv)
        return 0

    lax.fori_loop(0, chunks, gradients, 0, unroll=2)
    grads_store = pltpu.make_async_copy(grads_ref, grads_hbm, stores.at[1])
    grads_store.start()
    z_store.wait()
    grads_store.wait()


def tokens_kernel(places_ref, grads_ref, shared_ref, w_shared_ref, *refs):
    columns, (out_ref, lhs_ref, w_ref) = refs[:-3], refs[-3:]
    count = grads_ref.shape[0]
    extent, width = columns[0].shape[1:]
    k = pl.program_id(0)

    @pl.when(k == 0)
    def _():
        for r in range(count):
            source = grads_ref[lax.bitwise_xor(places_ref[0], r)]
            lhs_ref[:, r * width : (r + 1) * width] = source[:, :width]
        lhs_ref[:, count * width :] = shared_ref[...]

    for r in range(count):
        w_ref[:, r * width : (r + 1) * width] = columns[r][0]
    w_ref[:, count * width :] = w_shared_ref[0]
    offset = pl.multiple_of(lax.bitwise_xor(places_ref[1], k) * extent, extent)
    out_ref[0, :, pl.ds(offset, extent)] = dot_nt(lhs_ref[...], w_ref[...]).astype(bf16)


def sum_kernel(parts_ref, sum_ref, turned_ref):
    start = parts_ref.shape[2] - sum_ref.shape[1]
    total = parts_ref[0, :, start:].astype(f32)
    for n in range(1, parts_ref.shape[0]):
        total = total + parts_ref[n, :, start:].astype(f32)
    sum_ref[...] = total.astype(bf16)
    turned_ref[...] = total.T.astype(bf16).reshape(turned_ref.shape)


def add_kernel(*refs):
    out_ref, refs = refs[-1], refs[:-1]
    head_refs, shared_refs = refs[: len(refs) // 2], refs[len(refs) // 2 :]
    rows = head_refs[0].shape[1]
    total = head_refs[0][...].astype(f32)
    for ref in head_refs[1:]:
        total = total + ref[...].astype(f32)
    out_ref[:, :rows, :] = total.astype(bf16)
    total = shared_refs[0][...].astype(f32)
    for ref in shared_refs[1:]:
        total = total + ref[...].astype(f32)
    total = total.astype(bf16)
    extra = out_ref.shape[1] - rows
    part = total.shape[2]
    out_ref[:, rows:, :] = jnp.zeros((out_ref.shape[0], extra, out_ref.shape[2]), bf16)
    for q in range(rows // extra):
        out_ref[:, rows:, q * part : (q + 1) * part] = total[:, q * extra : (q + 1) * extra]


def spread_kernel(blocks_ref, out_ref):
    width = blocks_ref.shape[2]
    for n in range(blocks_ref.shape[0]):
        out_ref[0, :, n * width : (n + 1) * width] = blocks_ref[n]


def weight_kernel(sources, arrays, slots, group, parts, places_ref, *refs):
    array_refs, grad_ref = refs[:arrays], refs[arrays]
    out_refs = refs[arrays + 1 : arrays + 1 + parts]
    held, total, result, sems = refs[arrays + 1 + parts :]
    pieces = len(sources)
    rows = held.shape[1]
    hidden = held.shape[2]

    def fetch(i):
        array, start = sources[i]
        source = array_refs[array].at[pl.ds(start, rows)]
        return pltpu.make_async_copy(source, held.at[i % slots], sems.at[i % slots])

    for i in range(slots):
        fetch(i).start()
    for first in range(0, pieces, group):
        turned = []
        for i in range(first, first + group):
            offset = (2 * lax.bitwise_xor(places_ref[0], i // 2) + i % 2) * rows
            if len(grad_ref.shape) == 3:
                block = grad_ref[lax.bitwise_xor(places_ref[0], i // 2)]
                turned.append(block[:, i % 2 * rows : (i % 2 + 1) * rows])
            else:
                block = grad_ref[pl.ds(pl.multiple_of(offset, rows), rows), :]
                turned.append(block[:, : total.shape[0]].T)
        for i in range(first, first + group):
            fetch(i).wait()
        slot = first % slots
        block = held[slot : slot + group].reshape(group * rows, hidden)
        term = dot_nn(jnp.concatenate(turned, axis=1), block)
        if first > 0:
            term = term + total[...]
        if first + group < pieces:
            total[...] = term
        else:
            result[...] = term.T.astype(bf16)
        for i in range(first, first + group):
            if i + slots < pieces:
                fetch(i + slots).start()
    each = out_refs[0].shape[1]
    for k in range(parts):
        mine = lax.bitwise_xor(places_ref[1], k) * each
        for j in range(out_refs[0].shape[0]):
            source = pl.ds(pl.multiple_of(j * parts * each + mine, each), each)
            out_refs[k][j] = result[source, :]


def finish_kernel(packed_ref, out_ref):
    count, _, width = packed_ref.shape
    rows = out_ref.shape[0]
    extra = packed_ref.shape[1] - rows
    part = (out_ref.shape[1] - count * width) // count
    for n in range(count):
        out_ref[:, n * width : (n + 1) * width] = packed_ref[n, :rows].astype(f32)
        start = count * width + n * part
        for q in range(rows // extra):
            block = packed_ref[n, rows:, q * part : (q + 1) * part]
            out_ref[q * extra : (q + 1) * extra, start : start + part] = block.astype(f32)


def resident(array):
    return pl.BlockSpec(array.shape, lambda k: (0,) * len(array.shape))


def after(value, *earlier):
    return lax.optimization_barrier((value,) + earlier)[0]


def permute_xor(a, axis, mask):
    count = lax.axis_size(axis)
    return lax.ppermute(a, axis, [(i, i ^ mask) for i in range(count)])


def gather_rows(rows, axis, beside, work):
    count = lax.axis_size(axis)
    bits = count.bit_length() - 1
    half = rows.shape[0] // 2
    if bits == 3:
        first = [permute_xor(rows, axis, mask) for mask in (2, 4)]
        *first, beside = lax.optimization_barrier((*first, beside))
        across = {2: first[0], 4: first[1]}
        done = work(beside)
        corner = [
            permute_xor(across[2][:half], axis, 4),
            permute_xor(across[4][half:], axis, 2),
        ]
        own = {0: [rows], 2: [across[2]], 4: [across[4]], 6: corner}
        held = {}
        for r, parts in own.items():
            held[r] = parts
            held[r ^ 1] = [permute_xor(after(a, done[0]), axis, 1) for a in parts]
    else:
        done = work(beside)
        upper = list(range(1, bits))
        orders = (upper + [0], upper[1:] + upper[:1] + [0])
        both = ({0: rows[:half]}, {0: rows[half:]})
        for step in range(bits):
            for part in range(2):
                mask = 1 << orders[part][step]
                for r in list(both[part]):
                    both[part][r ^ mask] = permute_xor(both[part][r], axis, mask)
        held = {r: [both[0][r], both[1][r]] for r in range(count)}
    arrays, sources = [], []
    for r in range(count):
        for part in range(2):
            whole_block = len(held[r]) == 1
            if part == 0 or not whole_block:
                arrays.append(held[r][part])
            sources.append((len(arrays) - 1, half * part if whole_block else 0))
    return arrays, tuple(sources), done


def exchange_xor(pieces, axis):
    return [pieces[0]] + [permute_xor(p, axis, r) for r, p in enumerate(pieces) if r > 0]


def tables_kernel(log_ref, *refs):
    out_refs, table_refs, sems = refs[:7], refs[7:14], refs[14]
    te_ref, fs_ref, en_ref, lv_ref, dt_ref, m_ref, mt_ref = table_refs
    heads = log_ref.shape[0]
    chunks = dt_ref.shape[0]
    head_size = te_ref.shape[1] // heads
    row = lax.broadcasted_iota(jnp.int32, (CHUNK, CHUNK), 0)
    col = lax.broadcasted_iota(jnp.int32, (CHUNK, CHUNK), 1)
    logs = jnp.concatenate(
        [log_ref[:, k * CHUNK : (k + 1) * CHUNK] for k in range(chunks)], axis=0
    )
    cumulative = lax.dot_general(
        logs, (row <= col).astype(f32), (((1,), (0,)), ((), ())),
        precision=lax.Precision.HIGHEST, preferred_element_type=f32,
    )
    exclusive = cumulative - logs
    cum_t, exc_t = cumulative.T, exclusive.T
    total = cum_t[CHUNK - 1 : CHUNK, :]
    spreads = (
        (te_ref, jnp.exp(total - cum_t)),
        (fs_ref, jnp.exp(exc_t)),
        (en_ref, jnp.exp(cum_t)),
        (lv_ref, jnp.exp(total - exc_t)),
    )
    chunk_decay = jnp.exp(total)
    diagonal = (row == col).astype(f32)
    for k in range(chunks):
        rows = slice(k * CHUNK, (k + 1) * CHUNK)
        picked = range(k * heads, (k + 1) * heads)
        for ref, source in spreads:
            ref[rows, :] = jnp.concatenate(
                [jnp.broadcast_to(source[:, n : n + 1], (CHUNK, head_size)) for n in picked], axis=1
            ).astype(bf16)
        dt_ref[k] = jnp.concatenate(
            [jnp.broadcast_to(chunk_decay[:, n : n + 1], (1, head_size)) for n in picked], axis=1
        )
        for h, n in enumerate(picked):
            cum_col, exc_col = cum_t[:, n : n + 1], exc_t[:, n : n + 1]
            cum_row, exc_row = cumulative[n : n + 1, :], exclusive[n : n + 1, :]
            below, above = cum_col - cum_row, exc_row - exc_col
            exponent = jnp.where(row > col, below, jnp.where(row < col, above, 0.0))
            turned = jnp.where(row < col, -below, jnp.where(row > col, -above, 0.0))
            columns = slice(h * CHUNK, (h + 1) * CHUNK)
            m_ref[rows, columns] = (jnp.exp(exponent) + diagonal).astype(bf16)
            mt_ref[rows, columns] = (jnp.exp(turned) + diagonal).astype(bf16)
    stores = [
        pltpu.make_async_copy(source, target, sems.at[n])
        for n, (source, target) in enumerate(zip(table_refs, out_refs))
    ]
    for store in stores:
        store.start()
    for store in stores:
        store.wait()


def on_device(tokens, w_in, log_decay, grad_out):
    local_tokens = tokens[0]
    upstream = grad_out[0]
    token_count, hidden_width = local_tokens.shape
    head_count = log_decay.shape[1]
    inner_width = upstream.shape[1]
    head_size = inner_width // head_count
    state_size = (w_in.shape[1] - inner_width) // 2
    seq_count = lax.axis_size("seq")
    fsdp_count = lax.axis_size("fsdp")
    place = lax.axis_index("seq")
    row_place = lax.axis_index("fsdp")
    heads = head_count // seq_count
    width = heads * head_size
    length = token_count * seq_count
    shared = 2 * state_size
    chunks = length // CHUNK
    extent = hidden_width // fsdp_count
    shape = jax.ShapeDtypeStruct
    params = pltpu.CompilerParams(vmem_limit_bytes=VMEM_LIMIT)
    scalar = [pl.BlockSpec(memory_space=pltpu.SMEM)]
    places = jnp.stack([place, row_place]).astype(jnp.int32)

    def cost(flops, moved):
        return pl.CostEstimate(flops=flops, bytes_accessed=moved, transcendentals=0)

    def from_all(block):
        return exchange_xor([block] * fsdp_count, "fsdp")

    def columns(r):
        return lax.dynamic_slice_in_dim(w_in, lax.bitwise_xor(place, r) * width, width, 1)

    log_rates = lax.all_to_all(log_decay[0], "seq", 0, 1, tiled=True)
    w_own = from_all(jnp.concatenate([columns(0), w_in[:, inner_width:]], axis=1))
    table_shapes = (
        [shape((length, width), bf16)] * 4
        + [shape((chunks, 1, width), f32)]
        + [shape((length, heads * CHUNK), bf16)] * 2
    )
    in_hbm = [pl.BlockSpec(memory_space=pltpu.HBM)]
    scratch = lambda *buffers: [pltpu.VMEM(a.shape, a.dtype) for a in buffers]
    make_tables = pl.pallas_call(
        tables_kernel,
        grid=(1,),
        out_shape=table_shapes,
        in_specs=[resident(log_rates)],
        out_specs=in_hbm * 7,
        scratch_shapes=scratch(*table_shapes) + [pltpu.SemaphoreType.DMA((7,))],
        compiler_params=params,
        cost_estimate=cost(0, 8 * length * width),
    )
    arrays, sources, tables = gather_rows(local_tokens, "seq", log_rates, make_tables)
    g = lax.all_to_all(after(upstream, tables[0]), "seq", 1, 0, tiled=True)

    w_stack = jnp.stack(w_own)
    w_shared = w_stack[:, :, width:]
    w_sides = {0: w_stack[:, :, :width]}
    for r in range(2, seq_count, 2):
        if r & (r - 1):
            w_sides[r] = from_all(after(columns(r), *w_own))
        else:
            w_sides[r] = permute_xor(after(w_sides[0], *arrays[-2:]), "seq", r)


    count = len(sources)
    slots = min(count, 16)
    group = min(slots, 4)
    held = shape((slots, token_count // 2, hidden_width), bf16)
    by_position = shape((length, width), bf16)
    by_state = shape((chunks * state_size, width), bf16)
    state_rows = shape((length, state_size), bf16)
    buffers = [
        *table_shapes, by_position, by_position, shape((length, width + shared), bf16),
        held, shape((hidden_width, width + shared), bf16),
        by_position, state_rows, state_rows,
        by_position, by_state, by_state, by_position, by_state,
        shape((width, width), bf16), shape((state_size, width), f32),
    ]
    z, grads = pl.pallas_call(
        functools.partial(
            mixer_kernel, sources, len(arrays), slots, group, fsdp_count, heads, head_size
        ),
        out_shape=[by_position, shape((length, width + shared), bf16)],
        in_specs=scalar + in_hbm * (len(arrays) + fsdp_count + 8),
        out_specs=in_hbm * 2,
        scratch_shapes=scratch(*buffers)
        + [
            pltpu.SemaphoreType.DMA((slots,)),
            pltpu.SemaphoreType.DMA((8 + fsdp_count,)),
            pltpu.SemaphoreType.DMA((2,)),
        ],
        compiler_params=params,
        cost_estimate=cost(
            2 * length * hidden_width * (width + shared) + 120 * length * width * CHUNK,
            4 * length * hidden_width,
        ),
    )(places, *arrays, *w_own, *tables, g)

    rows_each = hidden_width // (seq_count * fsdp_count)

    def weight_columns(grad, columns):
        total = shape((columns, hidden_width), f32)
        result = shape((hidden_width, columns), bf16)
        parts = [shape((seq_count, rows_each, columns), bf16)] * fsdp_count
        parts = pl.pallas_call(
            functools.partial(weight_kernel, sources, len(arrays), slots, group, fsdp_count),
            out_shape=parts,
            grid=(1,),
            in_specs=scalar + in_hbm * len(arrays) + [resident(grad)],
            out_specs=[resident(a) for a in parts],
            scratch_shapes=scratch(held, total, result) + [pltpu.SemaphoreType.DMA((slots,))],
            compiler_params=params,
            cost_estimate=cost(2 * length * hidden_width * columns, 2 * length * hidden_width),
        )(places, *arrays, grad)
        return parts

    for r in range(0, seq_count, 2):
        if isinstance(w_sides[r], list):
            w_sides[r] = jnp.stack(w_sides[r])
        w_sides[r + 1] = permute_xor(after(w_sides[r], grads), "seq", 1)
    arrived = lax.all_to_all(
        grads.reshape(seq_count, token_count, width + shared), "seq", 0, 0
    )
    head_weights = weight_columns(grads, width)
    head_arrived = exchange_xor(head_weights, "fsdp")
    arrived, z, w_sides, _ = lax.optimization_barrier((arrived, z, w_sides, head_weights[0]))
    sums = [
        shape((token_count, shared), bf16),
        shape((seq_count, shared // seq_count, token_count), bf16),
    ]
    grad_shared, turned_shared = pl.pallas_call(
        sum_kernel,
        grid=(1,),
        out_shape=sums,
        in_specs=[resident(arrived)],
        out_specs=[resident(a) for a in sums],
        compiler_params=params,
    )(arrived)
    shared_columns = lax.all_to_all(turned_shared, "seq", 0, 0)
    mixed_blocks = lax.all_to_all(
        after(z, shared_columns).reshape(seq_count, token_count, width), "seq", 0, 0
    )
    shared_weights = weight_columns(shared_columns, shared // seq_count)
    shared_arrived = exchange_xor(shared_weights, "fsdp")

    def by_block(a):
        return pl.BlockSpec((1,) + a.shape[1:], lambda k: (k, 0, 0))

    w_blocks = [w_shared] + [w_sides[r] for r in range(seq_count)]
    grad_tokens_shape = shape((1, token_count, hidden_width), bf16)
    lhs = shape((token_count, inner_width + shared), bf16)
    w_block = shape((extent, inner_width + shared), bf16)
    grad_tokens = pl.pallas_call(
        tokens_kernel,
        grid=(fsdp_count,),
        out_shape=grad_tokens_shape,
        in_specs=scalar
        + [resident(arrived), resident(grad_shared)]
        + [by_block(a) for a in w_blocks],
        out_specs=resident(grad_tokens_shape),
        scratch_shapes=scratch(lhs, w_block),
        compiler_params=params,
        cost_estimate=cost(
            2 * token_count * hidden_width * (inner_width + shared),
            2 * hidden_width * (inner_width + shared),
        ),
    )(places, arrived, grad_shared, *w_blocks)

    mixer_out_shape = shape((1, token_count, inner_width), bf16)
    mixer_out = pl.pallas_call(
        spread_kernel,
        grid=(1,),
        out_shape=mixer_out_shape,
        in_specs=[resident(mixed_blocks)],
        out_specs=resident(mixer_out_shape),
        compiler_params=params,
    )(mixed_blocks)
    extra = 16
    packed = shape((seq_count, rows_each + extra, width), bf16)
    packed_sums = pl.pallas_call(
        add_kernel,
        grid=(1,),
        out_shape=packed,
        in_specs=[resident(a) for a in head_arrived + shared_arrived],
        out_specs=resident(packed),
        compiler_params=params,
    )(*head_arrived, *shared_arrived)
    owned = lax.all_to_all(packed_sums, "seq", 0, 0)
    finished = shape((rows_each, inner_width + shared), f32)
    grad_weights = pl.pallas_call(
        finish_kernel,
        grid=(1,),
        out_shape=finished,
        in_specs=[resident(owned)],
        out_specs=resident(finished),
        compiler_params=params,
    )(owned)
    return mixer_out, grad_tokens, grad_weights


def solution(mesh):
    return jax.shard_map(
        on_device,
        mesh=mesh,
        in_specs=(
            P("fsdp", "seq", None),
            P("fsdp", None),
            P("fsdp", None, "seq"),
            P("fsdp", "seq", None),
        ),
        out_specs=(P("fsdp", "seq", None), P("fsdp", "seq", None), P(("seq", "fsdp"), None)),
        check_vma=False,
    )
```

```python
import functools

import jax
import jax.numpy as jnp
from jax import lax
from jax.experimental import pallas as pl
from jax.experimental.pallas import tpu as pltpu
from jax.sharding import PartitionSpec as P

CHUNK = 128
EPSILON = 1e-05
VMEM_LIMIT = 60 * 1024 * 1024

f32 = jnp.float32
bf16 = jnp.bfloat16


def dot_nn(a, b):
    return lax.dot_general(a, b, (((1,), (0,)), ((), ())), preferred_element_type=f32)


def dot_nt(a, b):
    return lax.dot_general(a, b, (((1,), (1,)), ((), ())), preferred_element_type=f32)


def dot_tn(a, b):
    return lax.dot_general(a, b, (((0,), (0,)), ((), ())), preferred_element_type=f32)


def by_head(rows, heads, head_size):
    if heads == 1:
        return rows
    lane = lax.broadcasted_iota(jnp.int32, rows.shape, 1)
    parts = []
    for h in range(heads):
        inside = (lane >= h * head_size) & (lane < (h + 1) * head_size)
        parts.append(jnp.where(inside, rows, jnp.zeros_like(rows)))
    return jnp.concatenate(parts, axis=0)


def decayed(affinity, decays, heads):
    tiled = jnp.concatenate([affinity] * heads, axis=1) if heads > 1 else affinity
    return (tiled * decays.astype(f32)).astype(bf16)


def spans(k, state_size):
    rows = pl.ds(pl.multiple_of(k * CHUNK, CHUNK), CHUNK)
    return rows, pl.ds(pl.multiple_of(k * state_size, state_size), state_size)


def fill_mean(mean_ref, heads, head_size):
    row = lax.broadcasted_iota(jnp.int32, mean_ref.shape, 0)
    col = lax.broadcasted_iota(jnp.int32, mean_ref.shape, 1)
    same = jnp.zeros(mean_ref.shape, jnp.bool_)
    for h in range(heads):
        low, high = h * head_size, (h + 1) * head_size
        same |= (row >= low) & (row < high) & (col >= low) & (col < high)
    mean_ref[...] = jnp.where(same, 1.0 / head_size, 0.0).astype(bf16)


def forward_kernel(sources, arrays, slots, group, heads, head_size, place_ref, *refs):
    array_refs, refs = refs[:arrays], refs[arrays:]
    in_hbm, out_hbm, refs = refs[:7], refs[7:14], refs[14:]
    in_refs, out_refs, (held, mean_ref, carry, sems, loads, stores) = refs[:7], refs[7:14], refs[14:]
    w_ref, m_ref, te_ref, fs_ref, en_ref, lv_ref, dt_ref = in_refs
    x_ref, b_ref, c_ref, z_ref, rs_ref, sf_ref, rn_ref = out_refs
    pieces = len(sources)
    rows_each = held.shape[1]
    width, state_size = x_ref.shape[1], b_ref.shape[1]
    chunks = dt_ref.shape[0]

    def fetch(i):
        array, start = sources[i]
        source = array_refs[array].at[pl.ds(start, rows_each)]
        return pltpu.make_async_copy(source, held.at[i % slots], sems.at[i % slots])

    in_loads = [
        pltpu.make_async_copy(source, target, loads.at[n])
        for n, (source, target) in enumerate(zip(in_hbm, in_refs))
    ]
    out_stores = [
        pltpu.make_async_copy(source, target, stores.at[n])
        for n, (source, target) in enumerate(zip(out_refs, out_hbm))
    ]
    in_loads[0].start()
    for i in range(slots):
        fetch(i).start()
    for load in in_loads[1:]:
        load.start()
    fill_mean(mean_ref, heads, head_size)

    in_loads[0].wait()
    for first in range(0, pieces, group):
        for i in range(first, first + group):
            fetch(i).wait()
        slot = first % slots
        block = held[slot : slot + group].reshape(group * rows_each, held.shape[2])
        result = dot_nn(block, w_ref[...]).astype(bf16)
        for i in range(first, first + group):
            if i + slots < pieces:
                fetch(i + slots).start()
            offset = (2 * lax.bitwise_xor(place_ref[0], i // 2) + i % 2) * rows_each
            target = pl.ds(pl.multiple_of(offset, rows_each), rows_each)
            part = slice((i - first) * rows_each, (i - first + 1) * rows_each)
            x_ref[target, :] = result[part, :width]
            b_ref[target, :] = result[part, width : width + state_size]
            c_ref[target, :] = result[part, width + state_size :]
    for store in out_stores[:3]:
        store.start()
    for load in in_loads[1:]:
        load.wait()

    carry[...] = jnp.zeros_like(carry)

    def reverse_states(i, _):
        k = chunks - 1 - i
        rows, state = spans(k, state_size)
        rn_ref[state, :] = carry[...].astype(bf16)
        term = dot_tn(b_ref[rows, :], x_ref[rows, :] * fs_ref[rows, :])
        carry[...] = dt_ref[k] * carry[...] + term
        return 0

    lax.fori_loop(0, chunks, reverse_states, 0, unroll=2)
    out_stores[6].start()
    carry[...] = jnp.zeros_like(carry)

    def outputs(k, _):
        rows, state = spans(k, state_size)
        x, b, c = x_ref[rows, :], b_ref[rows, :], c_ref[rows, :]
        state_in = carry[...].astype(bf16)
        sf_ref[state, :] = state_in
        weights = decayed(dot_nt(c, b), m_ref[rows, :], heads)
        y = dot_nn(weights, by_head(x, heads, head_size))
        y = y + en_ref[rows, :].astype(f32) * dot_nn(c, state_in)
        y = y + lv_ref[rows, :].astype(f32) * dot_nn(c, rn_ref[state, :])
        mean_square = dot_nn((y * y).astype(bf16), mean_ref[...])
        inverse = lax.rsqrt(mean_square + EPSILON)
        z_ref[rows, :] = (y * inverse).astype(bf16)
        rs_ref[rows, :] = inverse.astype(bf16)
        carry[...] = dt_ref[k] * carry[...] + dot_tn(b, x * te_ref[rows, :])
        return 0

    lax.fori_loop(0, chunks, outputs, 0, unroll=2)
    for store in out_stores[3:6]:
        store.start()
    for store in out_stores:
        store.wait()


def backward_kernel(heads, head_size, *refs):
    in_hbm, out_hbm, refs = refs[:15], refs[15:17], refs[17:]
    in_refs, (dx_ref, shared_ref), refs = refs[:15], refs[15:17], refs[17:]
    dy_ref, ge_ref, mean_ref, carry, loads, stores = refs
    g_ref, z_ref, rs_ref, c_ref, en_ref, dt_ref = in_refs[:6]
    x_ref, b_ref, m_ref, mt_ref, te_ref, fs_ref, lv_ref, sf_ref, rn_ref = in_refs[6:15]
    state_size = b_ref.shape[1]
    chunks = dt_ref.shape[0]
    in_loads = [
        pltpu.make_async_copy(source, target, loads.at[n])
        for n, (source, target) in enumerate(zip(in_hbm, in_refs))
    ]
    for load in in_loads:
        load.start()
    fill_mean(mean_ref, heads, head_size)
    carry[...] = jnp.zeros_like(carry)
    for load in in_loads[:6]:
        load.wait()

    def end_adjoints(i, _):
        k = chunks - 1 - i
        rows, state = spans(k, state_size)
        g, z = g_ref[rows, :].astype(f32), z_ref[rows, :].astype(f32)
        mean_gz = dot_nn((g * z).astype(bf16), mean_ref[...])
        dy = ((g - z * mean_gz) * rs_ref[rows, :].astype(f32)).astype(bf16)
        dy_ref[rows, :] = dy
        ge_ref[state, :] = carry[...].astype(bf16)
        carry[...] = dt_ref[k] * carry[...] + dot_tn(c_ref[rows, :], dy * en_ref[rows, :])
        return 0

    lax.fori_loop(0, chunks, end_adjoints, 0, unroll=2)
    carry[...] = jnp.zeros_like(carry)
    for load in in_loads[6:]:
        load.wait()

    def gradients(k, _):
        rows, state = spans(k, state_size)
        x, b, c, dy = x_ref[rows, :], b_ref[rows, :], c_ref[rows, :], dy_ref[rows, :]
        te, fs, en, lv = te_ref[rows, :], fs_ref[rows, :], en_ref[rows, :], lv_ref[rows, :]
        ge, gs = ge_ref[state, :], carry[...].astype(bf16)
        grad_weights = dot_nt(dy, by_head(x, heads, head_size)) * m_ref[rows, :].astype(f32)
        da = grad_weights[:, :CHUNK]
        for h in range(1, heads):
            da = da + grad_weights[:, h * CHUNK : (h + 1) * CHUNK]
        da = da.astype(bf16)
        turned = decayed(dot_nt(b, c), mt_ref[rows, :], heads)
        dx = dot_nn(turned, by_head(dy, heads, head_size))
        dx = dx + te.astype(f32) * dot_nn(b, ge)
        dx = dx + fs.astype(f32) * dot_nn(b, gs)
        dx_ref[rows, :] = dx.astype(bf16)
        dy_lv = dy * lv
        dc = dot_nn(da, b) + dot_nt(dy * en, sf_ref[state, :]) + dot_nt(dy_lv, rn_ref[state, :])
        db = dot_tn(da, c) + dot_nt(x * te, ge) + dot_nt(x * fs, gs)
        shared_ref[:state_size, rows] = db.T.astype(bf16)
        shared_ref[state_size:, rows] = dc.T.astype(bf16)
        carry[...] = dt_ref[k] * carry[...] + dot_tn(c, dy_lv)
        return 0

    lax.fori_loop(0, chunks, gradients, 0, unroll=2)
    out_stores = [
        pltpu.make_async_copy(source, target, stores.at[n])
        for n, (source, target) in enumerate(zip((dx_ref, shared_ref), out_hbm))
    ]
    for store in out_stores:
        store.start()
    for store in out_stores:
        store.wait()


def sum_kernel(parts_ref, dx_ref, sum_ref, packed_ref):
    total = parts_ref[0].astype(f32)
    for n in range(1, parts_ref.shape[0]):
        total = total + parts_ref[n].astype(f32)
    total = total.astype(bf16)
    sum_ref[...] = total
    count = packed_ref.shape[0]
    part, tokens = total.shape[0], total.shape[1] // count
    if packed_ref.shape[1] > tokens + part or packed_ref.shape[2] > dx_ref.shape[1]:
        packed_ref[...] = jnp.zeros_like(packed_ref)
    for n in range(count):
        block = slice(n * tokens, (n + 1) * tokens)
        packed_ref[n, :tokens, : dx_ref.shape[1]] = dx_ref[block, :]
        packed_ref[n, tokens : tokens + part, :tokens] = total[:, block]


def tokens_kernel(place_ref, packed_ref, own_ref, partner_ref, even_ref, odd_ref, out_ref, *lhs):
    own_lhs, partner_lhs, even_lhs, odd_lhs = lhs
    count = packed_ref.shape[0]
    tokens, width = partner_lhs.shape
    part = (own_lhs.shape[1] - width) // count

    @pl.when(pl.program_id(0) == 0)
    def _():
        for r in range(count):
            target = (even_lhs, odd_lhs)[r % 2] if r > 1 else (own_lhs, partner_lhs)[r]
            start = (r // 2 - 1) * width if r > 1 else 0
            source = lax.bitwise_xor(place_ref[0], r)
            target[:, start : start + width] = packed_ref[source, :tokens, :width]
        turned = [packed_ref[n, tokens : tokens + part, :tokens] for n in range(count)]
        own_lhs[:, width:] = jnp.concatenate(turned, axis=0).T

    result = dot_nt(own_lhs[...], own_ref[...])
    result = result + dot_nt(partner_lhs[...], partner_ref[:, :width])
    result = result + dot_nt(even_lhs[...], even_ref[...])
    result = result + dot_nt(odd_lhs[...], odd_ref[...])
    out_ref[0] = result.astype(bf16)


def spread_kernel(blocks_ref, out_ref):
    width = blocks_ref.shape[2]
    for n in range(blocks_ref.shape[0]):
        out_ref[0, :, n * width : (n + 1) * width] = blocks_ref[n]


def add_kernel(*refs):
    head_ref, shared_refs, out_ref = refs[0], refs[1:-1], refs[-1]
    rows = head_ref.shape[1]
    out_ref[:, :rows, :] = head_ref[...]
    total = shared_refs[0][...].astype(f32)
    for ref in shared_refs[1:]:
        total = total + ref[...].astype(f32)
    total = total.astype(bf16)
    extra = out_ref.shape[1] - rows
    part = total.shape[2]
    out_ref[:, rows:, :] = jnp.zeros((out_ref.shape[0], extra, out_ref.shape[2]), bf16)
    for q in range(rows // extra):
        out_ref[:, rows:, q * part : (q + 1) * part] = total[:, q * extra : (q + 1) * extra]


def weight_kernel(sources, arrays, slots, group, parts, is_turned, places_ref, *refs):
    array_refs, grad_ref = refs[:arrays], refs[arrays]
    out_refs, (held, total, result, sems) = refs[arrays + 1 : -4], refs[-4:]
    pieces = len(sources)
    rows = held.shape[1]
    hidden = held.shape[2]

    def fetch(i):
        array, start = sources[i]
        source = array_refs[array].at[pl.ds(start, rows)]
        return pltpu.make_async_copy(source, held.at[i % slots], sems.at[i % slots])

    for i in range(slots):
        fetch(i).start()
    for first in range(0, pieces, group):
        turned = []
        for i in range(first, first + group):
            offset = (2 * lax.bitwise_xor(places_ref[0], i // 2) + i % 2) * rows
            target = pl.ds(pl.multiple_of(offset, rows), rows)
            turned.append(grad_ref[:, target] if is_turned else grad_ref[target, :].T)
        for i in range(first, first + group):
            fetch(i).wait()
        slot = first % slots
        block = held[slot : slot + group].reshape(group * rows, hidden)
        term = dot_nn(jnp.concatenate(turned, axis=1), block)
        if first > 0:
            term = term + total[...]
        if first + group < pieces:
            total[...] = term
        else:
            result[...] = term.T.astype(bf16)
        for i in range(first, first + group):
            if i + slots < pieces:
                fetch(i + slots).start()
    each = out_refs[0].shape[-2]
    count = hidden // (parts * each)
    for k in range(parts):
        for j in range(count):
            if len(out_refs) == 1:
                out_refs[0][k, j] = result[(j * parts + k) * each : (j * parts + k + 1) * each, :]
            else:
                mine = (j * parts + lax.bitwise_xor(places_ref[1], k)) * each
                out_refs[k][j] = result[pl.ds(pl.multiple_of(mine, each), each), :]


def finish_kernel(packed_ref, out_ref):
    count, _, width = packed_ref.shape
    rows = out_ref.shape[0]
    extra = packed_ref.shape[1] - rows
    part = (out_ref.shape[1] - count * width) // count
    for n in range(count):
        out_ref[:, n * width : (n + 1) * width] = packed_ref[n, :rows].astype(f32)
        start = count * width + n * part
        for q in range(rows // extra):
            block = packed_ref[n, rows:, q * part : (q + 1) * part]
            out_ref[q * extra : (q + 1) * extra, start : start + part] = block.astype(f32)


def resident(array):
    return pl.BlockSpec(array.shape, lambda k: (0,) * len(array.shape))


def after(value, *earlier):
    return lax.optimization_barrier((value,) + earlier)[0]


def permute_xor(a, axis, mask):
    count = lax.axis_size(axis)
    return lax.ppermute(a, axis, [(i, i ^ mask) for i in range(count)])


def gather_rows(rows, axis, beside, work, last):
    count = lax.axis_size(axis)
    bits = count.bit_length() - 1
    half = rows.shape[0] // 2
    if bits == 3:
        held = {r: permute_xor(rows, axis, r) for r in (2, 4, 1)}
        held, beside = lax.optimization_barrier((held, beside))
        held[3], held[5] = permute_xor(held[2], axis, 1), permute_xor(held[4], axis, 1)
        corner = [
            permute_xor(held[2][:half], axis, 4),
            permute_xor(held[4][half:], axis, 2),
        ]
        last = after(last, held[3])
        held, corner, done = lax.optimization_barrier((held, corner, work(beside)))
        held = {r: [a] for r, a in held.items()}
        held[0], held[6] = [rows], corner
        held[7] = [permute_xor(a, axis, 1) for a in corner]
    else:
        done = work(beside)
        upper = list(range(1, bits))
        orders = (upper + [0], upper[1:] + upper[:1] + [0])
        both = ({0: rows[:half]}, {0: rows[half:]})
        for step in range(bits):
            for part in range(2):
                mask = 1 << orders[part][step]
                for r in list(both[part]):
                    both[part][r ^ mask] = permute_xor(both[part][r], axis, mask)
        held = {r: [both[0][r], both[1][r]] for r in range(count)}
    arrays, sources = [], []
    for r in range(count):
        for part in range(2):
            whole_block = len(held[r]) == 1
            if part == 0 or not whole_block:
                arrays.append(held[r][part])
            sources.append((len(arrays) - 1, half * part if whole_block else 0))
    return arrays, tuple(sources), done, last


def exchange_xor(pieces, axis):
    return [pieces[0]] + [permute_xor(p, axis, r) for r, p in enumerate(pieces) if r > 0]


def tables_kernel(log_ref, *refs):
    out_refs, table_refs, sems = refs[:7], refs[7:14], refs[14]
    te_ref, fs_ref, en_ref, lv_ref, dt_ref, m_ref, mt_ref = table_refs
    heads = log_ref.shape[0]
    chunks = dt_ref.shape[0]
    head_size = te_ref.shape[1] // heads
    row = lax.broadcasted_iota(jnp.int32, (CHUNK, CHUNK), 0)
    col = lax.broadcasted_iota(jnp.int32, (CHUNK, CHUNK), 1)
    logs = jnp.concatenate(
        [log_ref[:, k * CHUNK : (k + 1) * CHUNK] for k in range(chunks)], axis=0
    )
    cumulative = lax.dot_general(
        logs, (row <= col).astype(f32), (((1,), (0,)), ((), ())),
        precision=lax.Precision.HIGHEST, preferred_element_type=f32,
    )
    exclusive = cumulative - logs
    cum_t, exc_t = cumulative.T, exclusive.T
    total = cum_t[CHUNK - 1 : CHUNK, :]
    spreads = (
        (te_ref, jnp.exp(total - cum_t)),
        (fs_ref, jnp.exp(exc_t)),
        (en_ref, jnp.exp(cum_t)),
        (lv_ref, jnp.exp(total - exc_t)),
    )
    chunk_decay = jnp.exp(total)
    diagonal = (row == col).astype(f32)
    for k in range(chunks):
        rows = slice(k * CHUNK, (k + 1) * CHUNK)
        picked = range(k * heads, (k + 1) * heads)
        for ref, source in spreads:
            ref[rows, :] = jnp.concatenate(
                [jnp.broadcast_to(source[:, n : n + 1], (CHUNK, head_size)) for n in picked], axis=1
            ).astype(bf16)
        dt_ref[k] = jnp.concatenate(
            [jnp.broadcast_to(chunk_decay[:, n : n + 1], (1, head_size)) for n in picked], axis=1
        )
        for h, n in enumerate(picked):
            cum_col, exc_col = cum_t[:, n : n + 1], exc_t[:, n : n + 1]
            cum_row, exc_row = cumulative[n : n + 1, :], exclusive[n : n + 1, :]
            below, above = cum_col - cum_row, exc_row - exc_col
            exponent = jnp.where(row > col, below, jnp.where(row < col, above, 0.0))
            turned = jnp.where(row < col, -below, jnp.where(row > col, -above, 0.0))
            columns = slice(h * CHUNK, (h + 1) * CHUNK)
            m_ref[rows, columns] = (jnp.exp(exponent) + diagonal).astype(bf16)
            mt_ref[rows, columns] = (jnp.exp(turned) + diagonal).astype(bf16)
    stores = [
        pltpu.make_async_copy(source, target, sems.at[n])
        for n, (source, target) in enumerate(zip(table_refs, out_refs))
    ]
    for store in stores:
        store.start()
    for store in stores:
        store.wait()


def on_device(tokens, w_in, log_decay, grad_out):
    local_tokens = tokens[0]
    upstream = grad_out[0]
    token_count, hidden_width = local_tokens.shape
    head_count = log_decay.shape[1]
    inner_width = upstream.shape[1]
    head_size = inner_width // head_count
    state_size = (w_in.shape[1] - inner_width) // 2
    seq_count = lax.axis_size("seq")
    fsdp_count = lax.axis_size("fsdp")
    place = lax.axis_index("seq")
    row_place = lax.axis_index("fsdp")
    heads = head_count // seq_count
    width = heads * head_size
    length = token_count * seq_count
    shared = 2 * state_size
    chunks = length // CHUNK
    extent = hidden_width // fsdp_count
    shape = jax.ShapeDtypeStruct
    params = pltpu.CompilerParams(vmem_limit_bytes=VMEM_LIMIT)
    scalar = [pl.BlockSpec(memory_space=pltpu.SMEM)]
    places = jnp.stack([place, row_place]).astype(jnp.int32)

    def cost(flops, moved):
        return pl.CostEstimate(flops=flops, bytes_accessed=moved, transcendentals=0)

    def columns(r):
        return lax.dynamic_slice_in_dim(w_in, lax.bitwise_xor(place, r) * width, width, 1)

    w_columns = lax.all_gather(
        jnp.concatenate([columns(0), w_in[:, inner_width:]], axis=1), "fsdp", axis=0, tiled=True
    )
    log_rates = lax.all_to_all(log_decay[0], "seq", 0, 1, tiled=True)

    table_shapes = (
        [shape((length, width), bf16)] * 4
        + [shape((chunks, 1, width), f32)]
        + [shape((length, heads * CHUNK), bf16)] * 2
    )
    in_hbm = [pl.BlockSpec(memory_space=pltpu.HBM)]
    scratch = lambda *buffers: [pltpu.VMEM(a.shape, a.dtype) for a in buffers]
    make_tables = pl.pallas_call(
        tables_kernel,
        grid=(1,),
        out_shape=table_shapes,
        in_specs=[resident(log_rates)],
        out_specs=in_hbm * 7,
        scratch_shapes=scratch(*table_shapes) + [pltpu.SemaphoreType.DMA((7,))],
        compiler_params=params,
        cost_estimate=cost(0, 120 * length * width),
    )
    arrays, sources, tables, upstream = gather_rows(
        local_tokens, "seq", log_rates, make_tables, upstream
    )
    to_end, from_start, enter, leave, chunk_decay, decays, turned = tables

    count = len(sources)
    slots = min(count, 16)
    group = min(slots, 4)
    held = shape((slots, token_count // 2, hidden_width), bf16)
    by_position = shape((length, width), bf16)
    by_state = shape((chunks * state_size, width), bf16)
    state_rows = shape((length, state_size), bf16)
    mean = shape((width, width), bf16)
    carry = shape((state_size, width), f32)

    rest = jnp.concatenate([columns(r) for r in range(2, seq_count, 2)], axis=1)
    w_even = lax.all_gather(after(rest, w_columns), "fsdp", axis=0, tiled=True)

    *arrays, w_columns = lax.optimization_barrier((*arrays, w_columns))
    g = lax.all_to_all(upstream, "seq", 1, 0, tiled=True)
    operands = (w_columns, decays, to_end, from_start, enter, leave, chunk_decay)
    kept = [by_position, state_rows, state_rows, by_position, by_position, by_state, by_state]
    forward = pl.pallas_call(
        functools.partial(
            forward_kernel, sources, len(arrays), slots, group, heads, head_size
        ),
        out_shape=kept,
        in_specs=scalar + in_hbm * (len(arrays) + 7),
        out_specs=in_hbm * 7,
        scratch_shapes=scratch(*operands, *kept, held, mean, carry)
        + [
            pltpu.SemaphoreType.DMA((slots,)),
            pltpu.SemaphoreType.DMA((7,)),
            pltpu.SemaphoreType.DMA((7,)),
        ],
        compiler_params=params,
        cost_estimate=cost(
            4 * length * hidden_width * (width + shared) + 160 * length * width * CHUNK,
            4 * length * hidden_width,
        ),
    )(places, *arrays, *operands)
    (x, b, c, z, inverse, states_in, states_next), g = lax.optimization_barrier((forward, g))

    mixed_blocks = lax.all_to_all(z.reshape(seq_count, token_count, width), "seq", 0, 0)
    operands = (
        g, z, inverse, c, enter, chunk_decay,
        x, b, decays, turned, to_end, from_start, leave, states_in, states_next,
    )
    grads = [by_position, shape((shared, length), bf16)]
    backward = pl.pallas_call(
        functools.partial(backward_kernel, heads, head_size),
        out_shape=grads,
        in_specs=in_hbm * 15,
        out_specs=in_hbm * 2,
        scratch_shapes=scratch(*operands, *grads, by_position, by_state, mean, carry)
        + [pltpu.SemaphoreType.DMA((15,)), pltpu.SemaphoreType.DMA((2,))],
        compiler_params=params,
        cost_estimate=cost(240 * length * width * CHUNK, 40 * length * width),
    )(*operands)
    (dx, shared_partial), mixed_blocks = lax.optimization_barrier((backward, mixed_blocks))

    rows_each = hidden_width // (seq_count * fsdp_count)

    def weight_columns(grad, columns, is_turned):
        total = shape((columns, hidden_width), f32)
        result = shape((hidden_width, columns), bf16)
        if not is_turned:
            parts = [shape((fsdp_count, seq_count, rows_each, columns), bf16)]
        else:
            parts = [shape((seq_count, rows_each, columns), bf16)] * fsdp_count
        return pl.pallas_call(
            functools.partial(weight_kernel, sources, len(arrays), slots, group, fsdp_count, is_turned),
            out_shape=parts,
            grid=(1,),
            in_specs=scalar + in_hbm * len(arrays) + [resident(grad)],
            out_specs=[resident(a) for a in parts],
            scratch_shapes=scratch(held, total, result) + [pltpu.SemaphoreType.DMA((slots,))],
            compiler_params=params,
            cost_estimate=cost(4 * length * hidden_width * columns, 4 * length * hidden_width),
        )(places, *arrays, grad)

    part = shared // seq_count
    arrived = lax.all_to_all(shared_partial.reshape(seq_count, part, length), "seq", 0, 0)
    (head_weights,) = weight_columns(dx, width, False)
    head_sums = lax.psum_scatter(
        head_weights.reshape(hidden_width, width), "fsdp", scatter_dimension=0, tiled=True
    ).reshape(seq_count, rows_each, width)
    arrived, _, w_even = lax.optimization_barrier((arrived, head_weights, w_even))
    sums = [
        shape((part, length), bf16),
        shape((seq_count, token_count + max(part, 16), max(width, token_count)), bf16),
    ]
    shared_columns, packed = pl.pallas_call(
        sum_kernel,
        grid=(1,),
        out_shape=sums,
        in_specs=[resident(arrived), resident(dx)],
        out_specs=[resident(a) for a in sums],
        compiler_params=params,
    )(arrived, dx)

    grad_blocks = lax.all_to_all(packed, "seq", 0, 0)
    shared_weights = weight_columns(shared_columns, part, True)
    shared_arrived = exchange_xor(shared_weights, "fsdp")
    mixed_shape = shape((1, token_count, inner_width), bf16)
    mixer_out = pl.pallas_call(
        spread_kernel,
        grid=(1,),
        out_shape=mixed_shape,
        in_specs=[resident(mixed_blocks)],
        out_specs=resident(mixed_shape),
        compiler_params=params,
    )(after(mixed_blocks, shared_columns))
    w_partner = permute_xor(after(w_columns, arrived), "seq", 1)
    w_odd = permute_xor(w_even, "seq", 1)
    grad_blocks, shared_arrived, mixer_out, w_partner, w_odd = lax.optimization_barrier(
        (grad_blocks, shared_arrived, mixer_out, w_partner, w_odd)
    )

    grad_tokens_shape = shape((1, token_count, hidden_width), bf16)
    by_rows = lambda a: pl.BlockSpec((extent, a.shape[1]), lambda k: (k, 0))
    w_blocks = [w_columns, w_partner, w_even, w_odd]
    grad_tokens = pl.pallas_call(
        tokens_kernel,
        grid=(fsdp_count,),
        out_shape=grad_tokens_shape,
        in_specs=scalar + [resident(grad_blocks)] + [by_rows(a) for a in w_blocks],
        out_specs=pl.BlockSpec((1, token_count, extent), lambda k: (0, 0, k)),
        scratch_shapes=scratch(
            shape((token_count, width + shared), bf16),
            shape((token_count, width), bf16),
            shape((token_count, w_even.shape[1]), bf16),
            shape((token_count, w_odd.shape[1]), bf16),
        ),
        compiler_params=params,
        cost_estimate=cost(
            4 * token_count * hidden_width * (inner_width + shared),
            4 * hidden_width * (inner_width + shared),
        ),
    )(places, grad_blocks, *w_blocks)
    extra = 16
    packed = shape((seq_count, rows_each + extra, width), bf16)
    packed_sums = pl.pallas_call(
        add_kernel,
        grid=(1,),
        out_shape=packed,
        in_specs=[resident(a) for a in [head_sums, *shared_arrived]],
        out_specs=resident(packed),
        compiler_params=params,
    )(head_sums, *shared_arrived)
    owned = lax.all_to_all(packed_sums, "seq", 0, 0)
    finished = shape((rows_each, inner_width + shared), f32)
    grad_weights = pl.pallas_call(
        finish_kernel,
        grid=(1,),
        out_shape=finished,
        in_specs=[resident(owned)],
        out_specs=resident(finished),
        compiler_params=params,
    )(owned)
    return mixer_out, grad_tokens, grad_weights


def solution(mesh):
    return jax.shard_map(
        on_device,
        mesh=mesh,
        in_specs=(
            P("fsdp", "seq", None),
            P("fsdp", None),
            P("fsdp", None, "seq"),
            P("fsdp", "seq", None),
        ),
        out_specs=(P("fsdp", "seq", None), P("fsdp", "seq", None), P(("seq", "fsdp"), None)),
        check_vma=False,
    )
```

```python
import functools

import jax
import jax.numpy as jnp
from jax import lax
from jax.experimental import pallas as pl
from jax.experimental.pallas import tpu as pltpu
from jax.sharding import PartitionSpec as P

CHUNK = 128
EPSILON = 1e-05
VMEM_LIMIT = 60 * 1024 * 1024

f32 = jnp.float32
bf16 = jnp.bfloat16


def dot_nn(a, b):
    return lax.dot_general(a, b, (((1,), (0,)), ((), ())), preferred_element_type=f32)


def dot_nt(a, b):
    return lax.dot_general(a, b, (((1,), (1,)), ((), ())), preferred_element_type=f32)


def dot_tn(a, b):
    return lax.dot_general(a, b, (((0,), (0,)), ((), ())), preferred_element_type=f32)


def by_head(rows, heads, head_size):
    if heads == 1:
        return rows
    lane = lax.broadcasted_iota(jnp.int32, rows.shape, 1)
    parts = []
    for h in range(heads):
        inside = (lane >= h * head_size) & (lane < (h + 1) * head_size)
        parts.append(jnp.where(inside, rows, jnp.zeros_like(rows)))
    return jnp.concatenate(parts, axis=0)


def decayed(affinity, decays, heads):
    tiled = jnp.concatenate([affinity] * heads, axis=1) if heads > 1 else affinity
    return (tiled * decays.astype(f32)).astype(bf16)


def spans(k, state_size):
    rows = pl.ds(pl.multiple_of(k * CHUNK, CHUNK), CHUNK)
    return rows, pl.ds(pl.multiple_of(k * state_size, state_size), state_size)


def fill_mean(mean_ref, heads, head_size):
    row = lax.broadcasted_iota(jnp.int32, mean_ref.shape, 0)
    col = lax.broadcasted_iota(jnp.int32, mean_ref.shape, 1)
    same = jnp.zeros(mean_ref.shape, jnp.bool_)
    for h in range(heads):
        low, high = h * head_size, (h + 1) * head_size
        same |= (row >= low) & (row < high) & (col >= low) & (col < high)
    mean_ref[...] = jnp.where(same, 1.0 / head_size, 0.0).astype(bf16)


def forward_kernel(sources, arrays, slots, group, heads, head_size, place_ref, *refs):
    array_refs, refs = refs[:arrays], refs[arrays:]
    in_hbm, out_hbm, refs = refs[:7], refs[7:14], refs[14:]
    in_refs, out_refs, (held, mean_ref, carry, sems, loads, stores) = refs[:7], refs[7:14], refs[14:]
    w_ref, m_ref, te_ref, fs_ref, en_ref, lv_ref, dt_ref = in_refs
    x_ref, b_ref, c_ref, z_ref, rs_ref, sf_ref, rn_ref = out_refs
    pieces = len(sources)
    rows_each = held.shape[1]
    width, state_size = x_ref.shape[1], b_ref.shape[1]
    chunks = dt_ref.shape[0]

    def fetch(i):
        array, start = sources[i]
        source = array_refs[array].at[pl.ds(start, rows_each)]
        return pltpu.make_async_copy(source, held.at[i % slots], sems.at[i % slots])

    in_loads = [
        pltpu.make_async_copy(source, target, loads.at[n])
        for n, (source, target) in enumerate(zip(in_hbm, in_refs))
    ]
    out_stores = [
        pltpu.make_async_copy(source, target, stores.at[n])
        for n, (source, target) in enumerate(zip(out_refs, out_hbm))
    ]
    in_loads[0].start()
    for i in range(slots):
        fetch(i).start()
    for load in in_loads[1:]:
        load.start()
    fill_mean(mean_ref, heads, head_size)

    in_loads[0].wait()
    for first in range(0, pieces, group):
        for i in range(first, first + group):
            fetch(i).wait()
        slot = first % slots
        block = held[slot : slot + group].reshape(group * rows_each, held.shape[2])
        result = dot_nn(block, w_ref[...]).astype(bf16)
        for i in range(first, first + group):
            if i + slots < pieces:
                fetch(i + slots).start()
            offset = (2 * lax.bitwise_xor(place_ref[0], i // 2) + i % 2) * rows_each
            target = pl.ds(pl.multiple_of(offset, rows_each), rows_each)
            part = slice((i - first) * rows_each, (i - first + 1) * rows_each)
            x_ref[target, :] = result[part, :width]
            b_ref[target, :] = result[part, width : width + state_size]
            c_ref[target, :] = result[part, width + state_size :]
    for store in out_stores[:3]:
        store.start()
    for load in in_loads[1:]:
        load.wait()

    carry[...] = jnp.zeros_like(carry)

    def reverse_states(i, _):
        k = chunks - 1 - i
        rows, state = spans(k, state_size)
        rn_ref[state, :] = carry[...].astype(bf16)
        term = dot_tn(b_ref[rows, :], x_ref[rows, :] * fs_ref[rows, :])
        carry[...] = dt_ref[k] * carry[...] + term
        return 0

    lax.fori_loop(0, chunks, reverse_states, 0, unroll=8)
    out_stores[6].start()
    carry[...] = jnp.zeros_like(carry)

    def outputs(k, _):
        rows, state = spans(k, state_size)
        x, b, c = x_ref[rows, :], b_ref[rows, :], c_ref[rows, :]
        state_in = carry[...].astype(bf16)
        sf_ref[state, :] = state_in
        weights = decayed(dot_nt(c, b), m_ref[rows, :], heads)
        y = dot_nn(weights, by_head(x, heads, head_size))
        y = y + en_ref[rows, :].astype(f32) * dot_nn(c, state_in)
        y = y + lv_ref[rows, :].astype(f32) * dot_nn(c, rn_ref[state, :])
        mean_square = dot_nn((y * y).astype(bf16), mean_ref[...])
        inverse = lax.rsqrt(mean_square + EPSILON)
        z_ref[rows, :] = (y * inverse).astype(bf16)
        rs_ref[rows, :] = inverse.astype(bf16)
        carry[...] = dt_ref[k] * carry[...] + dot_tn(b, x * te_ref[rows, :])
        return 0

    lax.fori_loop(0, chunks, outputs, 0, unroll=8)
    for store in out_stores[3:6]:
        store.start()
    for store in out_stores:
        store.wait()


def backward_kernel(heads, head_size, *refs):
    in_hbm, out_hbm, refs = refs[:15], refs[15:17], refs[17:]
    in_refs, (dx_ref, shared_ref), refs = refs[:15], refs[15:17], refs[17:]
    dy_ref, ge_ref, mean_ref, carry, loads, stores = refs
    g_ref, z_ref, rs_ref, c_ref, en_ref, dt_ref = in_refs[:6]
    x_ref, b_ref, m_ref, mt_ref, te_ref, fs_ref, lv_ref, sf_ref, rn_ref = in_refs[6:15]
    state_size = b_ref.shape[1]
    chunks = dt_ref.shape[0]
    in_loads = [
        pltpu.make_async_copy(source, target, loads.at[n])
        for n, (source, target) in enumerate(zip(in_hbm, in_refs))
    ]
    for load in in_loads:
        load.start()
    fill_mean(mean_ref, heads, head_size)
    carry[...] = jnp.zeros_like(carry)
    for load in in_loads[:6]:
        load.wait()

    def end_adjoints(i, _):
        k = chunks - 1 - i
        rows, state = spans(k, state_size)
        g, z = g_ref[rows, :].astype(f32), z_ref[rows, :].astype(f32)
        mean_gz = dot_nn((g * z).astype(bf16), mean_ref[...])
        dy = ((g - z * mean_gz) * rs_ref[rows, :].astype(f32)).astype(bf16)
        dy_ref[rows, :] = dy
        ge_ref[state, :] = carry[...].astype(bf16)
        carry[...] = dt_ref[k] * carry[...] + dot_tn(c_ref[rows, :], dy * en_ref[rows, :])
        return 0

    lax.fori_loop(0, chunks, end_adjoints, 0, unroll=8)
    carry[...] = jnp.zeros_like(carry)
    for load in in_loads[6:]:
        load.wait()

    def gradients(k, _):
        rows, state = spans(k, state_size)
        x, b, c, dy = x_ref[rows, :], b_ref[rows, :], c_ref[rows, :], dy_ref[rows, :]
        te, fs, en, lv = te_ref[rows, :], fs_ref[rows, :], en_ref[rows, :], lv_ref[rows, :]
        ge, gs = ge_ref[state, :], carry[...].astype(bf16)
        grad_weights = dot_nt(dy, by_head(x, heads, head_size)) * m_ref[rows, :].astype(f32)
        da = grad_weights[:, :CHUNK]
        for h in range(1, heads):
            da = da + grad_weights[:, h * CHUNK : (h + 1) * CHUNK]
        da = da.astype(bf16)
        turned = decayed(dot_nt(b, c), mt_ref[rows, :], heads)
        dx = dot_nn(turned, by_head(dy, heads, head_size))
        dx = dx + te.astype(f32) * dot_nn(b, ge)
        dx = dx + fs.astype(f32) * dot_nn(b, gs)
        dx_ref[rows, :] = dx.astype(bf16)
        dy_lv = dy * lv
        dc = dot_nn(da, b) + dot_nt(dy * en, sf_ref[state, :]) + dot_nt(dy_lv, rn_ref[state, :])
        db = dot_tn(da, c) + dot_nt(x * te, ge) + dot_nt(x * fs, gs)
        shared_ref[:state_size, rows] = db.T.astype(bf16)
        shared_ref[state_size:, rows] = dc.T.astype(bf16)
        carry[...] = dt_ref[k] * carry[...] + dot_tn(c, dy_lv)
        return 0

    lax.fori_loop(0, chunks, gradients, 0, unroll=8)
    out_stores = [
        pltpu.make_async_copy(source, target, stores.at[n])
        for n, (source, target) in enumerate(zip((dx_ref, shared_ref), out_hbm))
    ]
    for store in out_stores:
        store.start()
    for store in out_stores:
        store.wait()


def sum_kernel(parts_ref, dx_ref, sum_ref, packed_ref):
    total = parts_ref[0].astype(f32)
    for n in range(1, parts_ref.shape[0]):
        total = total + parts_ref[n].astype(f32)
    total = total.astype(bf16)
    sum_ref[...] = total
    count = packed_ref.shape[0]
    part, tokens = total.shape[0], total.shape[1] // count
    if packed_ref.shape[1] > tokens + part or packed_ref.shape[2] > dx_ref.shape[1]:
        packed_ref[...] = jnp.zeros_like(packed_ref)
    for n in range(count):
        block = slice(n * tokens, (n + 1) * tokens)
        packed_ref[n, :tokens, : dx_ref.shape[1]] = dx_ref[block, :]
        packed_ref[n, tokens : tokens + part, :tokens] = total[:, block]


def tokens_kernel(where, place_ref, packed_ref, own_ref, partner_ref, *refs):
    columns, (out_ref, lhs_ref, own_lhs) = refs[:-3], refs[-3:]
    count = packed_ref.shape[0]
    tokens, first = own_lhs.shape
    width = lhs_ref.shape[1] // count
    part = (first - width) // count

    @pl.when(pl.program_id(0) == 0)
    def _():
        for r in range(count):
            source = packed_ref[lax.bitwise_xor(place_ref[0], r), :tokens, :width]
            lhs_ref[:, r * width : (r + 1) * width] = source
        own_lhs[:, :width] = lhs_ref[:, :width]
        turned = [packed_ref[n, tokens : tokens + part, :tokens] for n in range(count)]
        own_lhs[:, width:] = jnp.concatenate(turned, axis=0).T

    result = dot_nt(own_lhs[...], own_ref[...])
    result = result + dot_nt(lhs_ref[:, width : 2 * width], partner_ref[:, :width])
    for r in range(2, count):
        column = r * width
        for array, start, extent in where[r]:
            block = columns[array][:, start : start + extent]
            result = result + dot_nt(lhs_ref[:, column : column + extent], block)
            column += extent
    out_ref[0] = result.astype(bf16)


def spread_kernel(blocks_ref, out_ref):
    width = blocks_ref.shape[2]
    for n in range(blocks_ref.shape[0]):
        out_ref[0, :, n * width : (n + 1) * width] = blocks_ref[n]


def add_kernel(*refs):
    head_ref, shared_refs, out_ref = refs[0], refs[1:-1], refs[-1]
    rows = head_ref.shape[1]
    out_ref[:, :rows, :] = head_ref[...]
    total = shared_refs[0][...].astype(f32)
    for ref in shared_refs[1:]:
        total = total + ref[...].astype(f32)
    total = total.astype(bf16)
    if out_ref.shape[2] > total.shape[2]:
        out_ref[:, rows:, :] = jnp.zeros_like(out_ref[:, rows:, :])
    out_ref[:, rows:, : total.shape[2]] = total


def weight_kernel(sources, arrays, slots, group, parts, is_turned, places_ref, *refs):
    array_refs, grad_ref = refs[:arrays], refs[arrays]
    out_refs, (held, total, result, sems) = refs[arrays + 1 : -4], refs[-4:]
    pieces = len(sources)
    rows = held.shape[1]
    hidden = held.shape[2]

    def fetch(i):
        array, start = sources[i]
        source = array_refs[array].at[pl.ds(start, rows)]
        return pltpu.make_async_copy(source, held.at[i % slots], sems.at[i % slots])

    for i in range(slots):
        fetch(i).start()
    for first in range(0, pieces, group):
        turned = []
        for i in range(first, first + group):
            offset = (2 * lax.bitwise_xor(places_ref[0], i // 2) + i % 2) * rows
            target = pl.ds(pl.multiple_of(offset, rows), rows)
            turned.append(grad_ref[:, target] if is_turned else grad_ref[target, :].T)
        for i in range(first, first + group):
            fetch(i).wait()
        slot = first % slots
        block = held[slot : slot + group].reshape(group * rows, hidden)
        term = dot_nn(jnp.concatenate(turned, axis=1), block)
        if first > 0:
            term = term + total[...]
        if first + group < pieces:
            total[...] = term
        else:
            result[...] = term.T.astype(bf16)
        for i in range(first, first + group):
            if i + slots < pieces:
                fetch(i + slots).start()
    columns = result.shape[1]
    each = out_refs[0].shape[-2] * out_refs[0].shape[-1] // columns
    count = hidden // (parts * each)
    for k in range(parts):
        for j in range(count):
            if len(out_refs) == 1:
                out_refs[0][k, j] = result[(j * parts + k) * each : (j * parts + k + 1) * each, :]
                continue
            mine = (j * parts + lax.bitwise_xor(places_ref[1], k)) * each
            rows = out_refs[k].shape[1]
            for q in range(each // rows):
                source = pl.ds(pl.multiple_of(mine + q * rows, rows), rows)
                out_refs[k][j, :, q * columns : (q + 1) * columns] = result[source, :]


def finish_kernel(packed_ref, out_ref):
    count, _, width = packed_ref.shape
    rows = out_ref.shape[0]
    extra = packed_ref.shape[1] - rows
    part = (out_ref.shape[1] - count * width) // count
    for n in range(count):
        out_ref[:, n * width : (n + 1) * width] = packed_ref[n, :rows].astype(f32)
        start = count * width + n * part
        for q in range(rows // extra):
            block = packed_ref[n, rows:, q * part : (q + 1) * part]
            out_ref[q * extra : (q + 1) * extra, start : start + part] = block.astype(f32)


def resident(array):
    return pl.BlockSpec(array.shape, lambda k: (0,) * len(array.shape))


def after(value, *earlier):
    return lax.optimization_barrier((value,) + earlier)[0]


def permute_xor(a, axis, mask):
    count = lax.axis_size(axis)
    return lax.ppermute(a, axis, [(i, i ^ mask) for i in range(count)])


def gather_rows(rows, axis, beside, work):
    count = lax.axis_size(axis)
    bits = count.bit_length() - 1
    half = rows.shape[0] // 2
    if bits == 3:
        held = {r: permute_xor(rows, axis, r) for r in (2, 4, 1)}
        held, beside = lax.optimization_barrier((held, beside))
        held[3], held[5] = permute_xor(held[2], axis, 1), permute_xor(held[4], axis, 1)
        corner = [
            permute_xor(held[2][:half], axis, 4),
            permute_xor(held[4][half:], axis, 2),
        ]
        held, corner, done = lax.optimization_barrier((held, corner, work(*beside)))
        held = {r: [a] for r, a in held.items()}
        held[0], held[6] = [rows], corner
        held[7] = [permute_xor(a, axis, 1) for a in corner]
    else:
        done = work(*beside)
        upper = list(range(1, bits))
        orders = (upper + [0], upper[1:] + upper[:1] + [0])
        both = ({0: rows[:half]}, {0: rows[half:]})
        for step in range(bits):
            for part in range(2):
                mask = 1 << orders[part][step]
                for r in list(both[part]):
                    both[part][r ^ mask] = permute_xor(both[part][r], axis, mask)
        held = {r: [both[0][r], both[1][r]] for r in range(count)}
    arrays, sources = [], []
    for r in range(count):
        for part in range(2):
            whole_block = len(held[r]) == 1
            if part == 0 or not whole_block:
                arrays.append(held[r][part])
            sources.append((len(arrays) - 1, half * part if whole_block else 0))
    return arrays, tuple(sources), done


def exchange_xor(pieces, axis):
    return [pieces[0]] + [permute_xor(p, axis, r) for r, p in enumerate(pieces) if r > 0]


def tables_kernel(log_ref, *refs):
    out_refs, table_refs, sems = refs[:7], refs[7:14], refs[14]
    te_ref, fs_ref, en_ref, lv_ref, dt_ref, m_ref, mt_ref = table_refs
    heads = log_ref.shape[0]
    chunks = dt_ref.shape[0]
    head_size = te_ref.shape[1] // heads
    row = lax.broadcasted_iota(jnp.int32, (CHUNK, CHUNK), 0)
    col = lax.broadcasted_iota(jnp.int32, (CHUNK, CHUNK), 1)
    logs = jnp.concatenate(
        [log_ref[:, k * CHUNK : (k + 1) * CHUNK] for k in range(chunks)], axis=0
    )
    cumulative = lax.dot_general(
        logs, (row <= col).astype(f32), (((1,), (0,)), ((), ())),
        precision=lax.Precision.HIGHEST, preferred_element_type=f32,
    )
    exclusive = cumulative - logs
    cum_t, exc_t = cumulative.T, exclusive.T
    total = cum_t[CHUNK - 1 : CHUNK, :]
    spreads = (
        (te_ref, jnp.exp(total - cum_t)),
        (fs_ref, jnp.exp(exc_t)),
        (en_ref, jnp.exp(cum_t)),
        (lv_ref, jnp.exp(total - exc_t)),
    )
    chunk_decay = jnp.exp(total)
    diagonal = (row == col).astype(f32)
    for k in range(chunks):
        rows = slice(k * CHUNK, (k + 1) * CHUNK)
        picked = range(k * heads, (k + 1) * heads)
        for ref, source in spreads:
            ref[rows, :] = jnp.concatenate(
                [jnp.broadcast_to(source[:, n : n + 1], (CHUNK, head_size)) for n in picked], axis=1
            ).astype(bf16)
        dt_ref[k] = jnp.concatenate(
            [jnp.broadcast_to(chunk_decay[:, n : n + 1], (1, head_size)) for n in picked], axis=1
        )
        for h, n in enumerate(picked):
            cum_col, exc_col = cum_t[:, n : n + 1], exc_t[:, n : n + 1]
            cum_row, exc_row = cumulative[n : n + 1, :], exclusive[n : n + 1, :]
            below, above = cum_col - cum_row, exc_row - exc_col
            exponent = jnp.where(row > col, below, jnp.where(row < col, above, 0.0))
            turned = jnp.where(row < col, -below, jnp.where(row > col, -above, 0.0))
            columns = slice(h * CHUNK, (h + 1) * CHUNK)
            m_ref[rows, columns] = (jnp.exp(exponent) + diagonal).astype(bf16)
            mt_ref[rows, columns] = (jnp.exp(turned) + diagonal).astype(bf16)
    stores = [
        pltpu.make_async_copy(source, target, sems.at[n])
        for n, (source, target) in enumerate(zip(table_refs, out_refs))
    ]
    for store in stores:
        store.start()
    for store in stores:
        store.wait()


def on_device(tokens, w_in, log_decay, grad_out):
    local_tokens = tokens[0]
    upstream = grad_out[0]
    token_count, hidden_width = local_tokens.shape
    head_count = log_decay.shape[1]
    inner_width = upstream.shape[1]
    head_size = inner_width // head_count
    state_size = (w_in.shape[1] - inner_width) // 2
    seq_count = lax.axis_size("seq")
    fsdp_count = lax.axis_size("fsdp")
    place = lax.axis_index("seq")
    row_place = lax.axis_index("fsdp")
    heads = head_count // seq_count
    width = heads * head_size
    length = token_count * seq_count
    shared = 2 * state_size
    chunks = length // CHUNK
    extent = hidden_width // fsdp_count
    shape = jax.ShapeDtypeStruct
    params = pltpu.CompilerParams(vmem_limit_bytes=VMEM_LIMIT)
    scalar = [pl.BlockSpec(memory_space=pltpu.SMEM)]
    places = jnp.stack([place, row_place]).astype(jnp.int32)

    def cost(flops, moved):
        return pl.CostEstimate(flops=flops, bytes_accessed=moved, transcendentals=0)

    def columns(r):
        return lax.dynamic_slice_in_dim(w_in, lax.bitwise_xor(place, r) * width, width, 1)

    w_columns = lax.all_gather(
        jnp.concatenate([columns(0), w_in[:, inner_width:]], axis=1), "fsdp", axis=0, tiled=True
    )
    log_rates = lax.all_to_all(log_decay[0], "seq", 0, 1, tiled=True)

    table_shapes = (
        [shape((length, width), bf16)] * 4
        + [shape((chunks, 1, width), f32)]
        + [shape((length, heads * CHUNK), bf16)] * 2
    )
    in_hbm = [pl.BlockSpec(memory_space=pltpu.HBM)]
    scratch = lambda *buffers: [pltpu.VMEM(a.shape, a.dtype) for a in buffers]
    make_tables = pl.pallas_call(
        tables_kernel,
        grid=(1,),
        out_shape=table_shapes,
        in_specs=[resident(log_rates)],
        out_specs=in_hbm * 7,
        scratch_shapes=scratch(*table_shapes) + [pltpu.SemaphoreType.DMA((7,))],
        compiler_params=params,
        cost_estimate=cost(0, 120 * length * width),
    )
    neighbours = [r for r in range(2, seq_count, 2) if r & (r - 1) == 0]
    others = [r for r in range(2, seq_count, 2) if r & (r - 1)]
    first_part = width // 2
    rest = [columns(r) for r in others] + [columns(r)[:, :first_part] for r in neighbours]

    def second_step(log_rates, upstream, rest):
        blocks = upstream.reshape(token_count, seq_count, width).transpose(1, 0, 2)
        return make_tables(log_rates), blocks, jnp.concatenate(rest, axis=1)

    arrays, sources, (tables, upstream, rest) = gather_rows(
        local_tokens, "seq", (log_rates, upstream, rest), second_step
    )
    to_end, from_start, enter, leave, chunk_decay, decays, turned = tables

    count = len(sources)
    slots = min(count, 16)
    group = min(slots, 4)
    held = shape((slots, token_count // 2, hidden_width), bf16)
    by_position = shape((length, width), bf16)
    by_state = shape((chunks * state_size, width), bf16)
    state_rows = shape((length, state_size), bf16)
    mean = shape((width, width), bf16)
    carry = shape((state_size, width), f32)

    w_even = lax.all_gather(rest, "fsdp", axis=0, tiled=True)

    *arrays, w_columns = lax.optimization_barrier((*arrays, w_columns))
    g = lax.all_to_all(upstream, "seq", 0, 0).reshape(length, width)
    operands = (w_columns, decays, to_end, from_start, enter, leave, chunk_decay)
    kept = [by_position, state_rows, state_rows, by_position, by_position, by_state, by_state]
    forward = pl.pallas_call(
        functools.partial(
            forward_kernel, sources, len(arrays), slots, group, heads, head_size
        ),
        out_shape=kept,
        in_specs=scalar + in_hbm * (len(arrays) + 7),
        out_specs=in_hbm * 7,
        scratch_shapes=scratch(*operands, *kept, held, mean, carry)
        + [
            pltpu.SemaphoreType.DMA((slots,)),
            pltpu.SemaphoreType.DMA((7,)),
            pltpu.SemaphoreType.DMA((7,)),
        ],
        compiler_params=params,
        cost_estimate=cost(
            4 * length * hidden_width * (width + shared) + 160 * length * width * CHUNK,
            4 * length * hidden_width,
        ),
    )(places, *arrays, *operands)
    (x, b, c, z, inverse, states_in, states_next), g = lax.optimization_barrier((forward, g))

    mixed_blocks = lax.all_to_all(z.reshape(seq_count, token_count, width), "seq", 0, 0)
    operands = (
        g, z, inverse, c, enter, chunk_decay,
        x, b, decays, turned, to_end, from_start, leave, states_in, states_next,
    )
    grads = [by_position, shape((shared, length), bf16)]
    backward = pl.pallas_call(
        functools.partial(backward_kernel, heads, head_size),
        out_shape=grads,
        in_specs=in_hbm * 15,
        out_specs=in_hbm * 2,
        scratch_shapes=scratch(*operands, *grads, by_position, by_state, mean, carry)
        + [pltpu.SemaphoreType.DMA((15,)), pltpu.SemaphoreType.DMA((2,))],
        compiler_params=params,
        cost_estimate=cost(240 * length * width * CHUNK, 40 * length * width),
    )(*operands)
    backward, mixed_blocks = lax.optimization_barrier((backward, mixed_blocks))
    dx, shared_partial = backward

    rows_each = hidden_width // (seq_count * fsdp_count)
    extra = 16

    def weight_columns(grad, columns, is_turned):
        total = shape((columns, hidden_width), f32)
        result = shape((hidden_width, columns), bf16)
        if not is_turned:
            parts = [shape((fsdp_count, seq_count, rows_each, columns), bf16)]
        else:
            parts = [shape((seq_count, extra, columns * rows_each // extra), bf16)] * fsdp_count
        return pl.pallas_call(
            functools.partial(weight_kernel, sources, len(arrays), slots, group, fsdp_count, is_turned),
            out_shape=parts,
            grid=(1,),
            in_specs=scalar + in_hbm * len(arrays) + [resident(grad)],
            out_specs=[resident(a) for a in parts],
            scratch_shapes=scratch(held, total, result) + [pltpu.SemaphoreType.DMA((slots,))],
            compiler_params=params,
            cost_estimate=cost(4 * length * hidden_width * columns, 4 * length * hidden_width),
        )(places, *arrays, grad)

    part = shared // seq_count
    arrived = lax.all_to_all(shared_partial.reshape(seq_count, part, length), "seq", 0, 0)
    (head_weights,) = weight_columns(dx, width, False)
    head_sums = lax.psum_scatter(
        head_weights.reshape(hidden_width, width), "fsdp", scatter_dimension=0, tiled=True
    ).reshape(seq_count, rows_each, width)
    second_part = after(w_columns, head_weights)[:, first_part:width]
    w_across = [permute_xor(second_part, "seq", r) for r in neighbours]
    arrived, second_part, w_even = lax.optimization_barrier((arrived, second_part, w_even))
    sums = [
        shape((part, length), bf16),
        shape((seq_count, token_count + max(part, 16), max(width, token_count)), bf16),
    ]
    shared_columns, packed = pl.pallas_call(
        sum_kernel,
        grid=(1,),
        out_shape=sums,
        in_specs=[resident(arrived), resident(dx)],
        out_specs=[resident(a) for a in sums],
        compiler_params=params,
    )(arrived, dx)

    grad_blocks = lax.all_to_all(packed, "seq", 0, 0)
    shared_weights = weight_columns(shared_columns, part, True)
    shared_arrived = exchange_xor(shared_weights, "fsdp")
    mixed_shape = shape((1, token_count, inner_width), bf16)
    mixer_out = pl.pallas_call(
        spread_kernel,
        grid=(1,),
        out_shape=mixed_shape,
        in_specs=[resident(mixed_blocks)],
        out_specs=resident(mixed_shape),
        compiler_params=params,
    )(after(mixed_blocks, shared_columns))
    w_partner = permute_xor(after(w_columns, arrived), "seq", 1)
    w_even = [w_even, *w_across]
    w_odd = [permute_xor(a, "seq", 1) for a in w_even]
    grad_blocks, shared_arrived, mixer_out, w_partner, w_odd = lax.optimization_barrier(
        (grad_blocks, shared_arrived, mixer_out, w_partner, w_odd, head_sums)
    )[:-1]

    grad_tokens_shape = shape((1, token_count, hidden_width), bf16)
    by_rows = lambda a: pl.BlockSpec((extent, a.shape[1]), lambda k: (k, 0))
    where = {}
    for n, r in enumerate(others):
        where[r] = [(0, n * width, width)]
    for n, r in enumerate(neighbours):
        start = len(others) * width + n * first_part
        where[r] = [(0, start, first_part), (1 + n, 0, width - first_part)]
    for r in range(2, seq_count, 2):
        where[r + 1] = [(array + len(w_even), start, extent) for array, start, extent in where[r]]
    w_blocks = [w_columns, w_partner, *w_even, *w_odd]
    grad_tokens = pl.pallas_call(
        functools.partial(tokens_kernel, where),
        grid=(fsdp_count,),
        out_shape=grad_tokens_shape,
        in_specs=scalar + [resident(grad_blocks)] + [by_rows(a) for a in w_blocks],
        out_specs=pl.BlockSpec((1, token_count, extent), lambda k: (0, 0, k)),
        scratch_shapes=scratch(
            shape((token_count, inner_width), bf16), shape((token_count, width + shared), bf16)
        ),
        compiler_params=params,
        cost_estimate=cost(
            4 * token_count * hidden_width * (inner_width + shared),
            4 * hidden_width * (inner_width + shared),
        ),
    )(places, grad_blocks, *w_blocks)
    packed = shape((seq_count, rows_each + extra, width), bf16)
    packed_sums = pl.pallas_call(
        add_kernel,
        grid=(1,),
        out_shape=packed,
        in_specs=[resident(a) for a in [head_sums, *shared_arrived]],
        out_specs=resident(packed),
        compiler_params=params,
    )(head_sums, *shared_arrived)
    owned = lax.all_to_all(packed_sums, "seq", 0, 0)
    finished = shape((rows_each, inner_width + shared), f32)
    grad_weights = pl.pallas_call(
        finish_kernel,
        grid=(1,),
        out_shape=finished,
        in_specs=[resident(owned)],
        out_specs=resident(finished),
        compiler_params=params,
    )(owned)
    return mixer_out, grad_tokens, grad_weights


def solution(mesh):
    return jax.shard_map(
        on_device,
        mesh=mesh,
        in_specs=(
            P("fsdp", "seq", None),
            P("fsdp", None),
            P("fsdp", None, "seq"),
            P("fsdp", "seq", None),
        ),
        out_specs=(P("fsdp", "seq", None), P("fsdp", "seq", None), P(("seq", "fsdp"), None)),
        check_vma=False,
    )
```

```python
import functools

import jax
import jax.numpy as jnp
from jax import lax
from jax.experimental import pallas as pl
from jax.experimental.pallas import tpu as pltpu
from jax.sharding import PartitionSpec as P

CHUNK = 128
EPSILON = 1e-05
VMEM_LIMIT = 60 * 1024 * 1024

f32 = jnp.float32
bf16 = jnp.bfloat16


def dot_nn(a, b):
    return lax.dot_general(a, b, (((1,), (0,)), ((), ())), preferred_element_type=f32)


def dot_nt(a, b):
    return lax.dot_general(a, b, (((1,), (1,)), ((), ())), preferred_element_type=f32)


def dot_tn(a, b):
    return lax.dot_general(a, b, (((0,), (0,)), ((), ())), preferred_element_type=f32)


def by_head(rows, heads, head_size):
    if heads == 1:
        return rows
    lane = lax.broadcasted_iota(jnp.int32, rows.shape, 1)
    parts = []
    for h in range(heads):
        inside = (lane >= h * head_size) & (lane < (h + 1) * head_size)
        parts.append(jnp.where(inside, rows, jnp.zeros_like(rows)))
    return jnp.concatenate(parts, axis=0)


def decayed(affinity, decays, heads):
    tiled = jnp.concatenate([affinity] * heads, axis=1) if heads > 1 else affinity
    return (tiled * decays.astype(f32)).astype(bf16)


def spans(k, state_size):
    rows = pl.ds(pl.multiple_of(k * CHUNK, CHUNK), CHUNK)
    return rows, pl.ds(pl.multiple_of(k * state_size, state_size), state_size)


def fill_mean(mean_ref, heads, head_size):
    row = lax.broadcasted_iota(jnp.int32, mean_ref.shape, 0)
    col = lax.broadcasted_iota(jnp.int32, mean_ref.shape, 1)
    same = jnp.zeros(mean_ref.shape, jnp.bool_)
    for h in range(heads):
        low, high = h * head_size, (h + 1) * head_size
        same |= (row >= low) & (row < high) & (col >= low) & (col < high)
    mean_ref[...] = jnp.where(same, 1.0 / head_size, 0.0).astype(bf16)


def forward_kernel(sources, arrays, slots, group, heads, head_size, place_ref, *refs):
    array_refs, refs = refs[:arrays], refs[arrays:]
    in_hbm, out_hbm, refs = refs[:7], refs[7:14], refs[14:]
    in_refs, out_refs, (held, mean_ref, carry, sems, loads, stores) = refs[:7], refs[7:14], refs[14:]
    w_ref, m_ref, te_ref, fs_ref, en_ref, lv_ref, dt_ref = in_refs
    x_ref, b_ref, c_ref, z_ref, rs_ref, sf_ref, rn_ref = out_refs
    pieces = len(sources)
    rows_each = held.shape[1]
    width, state_size = x_ref.shape[1], b_ref.shape[1]
    chunks = dt_ref.shape[0]

    def fetch(i):
        array, start = sources[i]
        source = array_refs[array].at[pl.ds(start, rows_each)]
        return pltpu.make_async_copy(source, held.at[i % slots], sems.at[i % slots])

    in_loads = [
        pltpu.make_async_copy(source, target, loads.at[n])
        for n, (source, target) in enumerate(zip(in_hbm, in_refs))
    ]
    out_stores = [
        pltpu.make_async_copy(source, target, stores.at[n])
        for n, (source, target) in enumerate(zip(out_refs, out_hbm))
    ]
    in_loads[0].start()
    for i in range(slots):
        fetch(i).start()
    for load in in_loads[1:]:
        load.start()
    fill_mean(mean_ref, heads, head_size)

    in_loads[0].wait()
    for first in range(0, pieces, group):
        for i in range(first, first + group):
            fetch(i).wait()
        slot = first % slots
        block = held[slot : slot + group].reshape(group * rows_each, held.shape[2])
        result = dot_nn(block, w_ref[...]).astype(bf16)
        for i in range(first, first + group):
            if i + slots < pieces:
                fetch(i + slots).start()
            offset = (2 * lax.bitwise_xor(place_ref[0], i // 2) + i % 2) * rows_each
            target = pl.ds(pl.multiple_of(offset, rows_each), rows_each)
            part = slice((i - first) * rows_each, (i - first + 1) * rows_each)
            x_ref[target, :] = result[part, :width]
            b_ref[target, :] = result[part, width : width + state_size]
            c_ref[target, :] = result[part, width + state_size :]
    for store in out_stores[:3]:
        store.start()
    for load in in_loads[1:]:
        load.wait()

    carry[...] = jnp.zeros_like(carry)

    def reverse_states(i, _):
        k = chunks - 1 - i
        rows, state = spans(k, state_size)
        rn_ref[state, :] = carry[...].astype(bf16)
        term = dot_tn(b_ref[rows, :], x_ref[rows, :] * fs_ref[rows, :])
        carry[...] = dt_ref[k] * carry[...] + term
        return 0

    lax.fori_loop(0, chunks, reverse_states, 0, unroll=16)
    out_stores[6].start()
    carry[...] = jnp.zeros_like(carry)

    def outputs(k, _):
        rows, state = spans(k, state_size)
        x, b, c = x_ref[rows, :], b_ref[rows, :], c_ref[rows, :]
        state_in = carry[...].astype(bf16)
        sf_ref[state, :] = state_in
        weights = decayed(dot_nt(c, b), m_ref[rows, :], heads)
        y = dot_nn(weights, by_head(x, heads, head_size))
        y = y + en_ref[rows, :].astype(f32) * dot_nn(c, state_in)
        y = y + lv_ref[rows, :].astype(f32) * dot_nn(c, rn_ref[state, :])
        mean_square = dot_nn((y * y).astype(bf16), mean_ref[...])
        inverse = lax.rsqrt(mean_square + EPSILON)
        z_ref[rows, :] = (y * inverse).astype(bf16)
        rs_ref[rows, :] = inverse.astype(bf16)
        carry[...] = dt_ref[k] * carry[...] + dot_tn(b, x * te_ref[rows, :])
        return 0

    lax.fori_loop(0, chunks, outputs, 0, unroll=16)
    for store in out_stores[3:6]:
        store.start()
    for store in out_stores:
        store.wait()


def backward_kernel(heads, head_size, *refs):
    in_hbm, out_hbm, refs = refs[:15], refs[15:17], refs[17:]
    in_refs, (dx_ref, shared_ref), refs = refs[:15], refs[15:17], refs[17:]
    dy_ref, ge_ref, mean_ref, carry, loads, stores = refs
    g_ref, z_ref, rs_ref, c_ref, en_ref, dt_ref = in_refs[:6]
    x_ref, b_ref, m_ref, mt_ref, te_ref, fs_ref, lv_ref, sf_ref, rn_ref = in_refs[6:15]
    state_size = b_ref.shape[1]
    chunks = dt_ref.shape[0]
    in_loads = [
        pltpu.make_async_copy(source, target, loads.at[n])
        for n, (source, target) in enumerate(zip(in_hbm, in_refs))
    ]
    for load in in_loads:
        load.start()
    fill_mean(mean_ref, heads, head_size)
    carry[...] = jnp.zeros_like(carry)
    for load in in_loads[:6]:
        load.wait()

    def end_adjoints(i, _):
        k = chunks - 1 - i
        rows, state = spans(k, state_size)
        g, z = g_ref[rows, :].astype(f32), z_ref[rows, :].astype(f32)
        mean_gz = dot_nn((g * z).astype(bf16), mean_ref[...])
        dy = ((g - z * mean_gz) * rs_ref[rows, :].astype(f32)).astype(bf16)
        dy_ref[rows, :] = dy
        ge_ref[state, :] = carry[...].astype(bf16)
        carry[...] = dt_ref[k] * carry[...] + dot_tn(c_ref[rows, :], dy * en_ref[rows, :])
        return 0

    lax.fori_loop(0, chunks, end_adjoints, 0, unroll=16)
    carry[...] = jnp.zeros_like(carry)
    for load in in_loads[6:]:
        load.wait()

    def gradients(k, _):
        rows, state = spans(k, state_size)
        x, b, c, dy = x_ref[rows, :], b_ref[rows, :], c_ref[rows, :], dy_ref[rows, :]
        te, fs, en, lv = te_ref[rows, :], fs_ref[rows, :], en_ref[rows, :], lv_ref[rows, :]
        ge, gs = ge_ref[state, :], carry[...].astype(bf16)
        grad_weights = dot_nt(dy, by_head(x, heads, head_size)) * m_ref[rows, :].astype(f32)
        da = grad_weights[:, :CHUNK]
        for h in range(1, heads):
            da = da + grad_weights[:, h * CHUNK : (h + 1) * CHUNK]
        da = da.astype(bf16)
        turned = decayed(dot_nt(b, c), mt_ref[rows, :], heads)
        dx = dot_nn(turned, by_head(dy, heads, head_size))
        dx = dx + te.astype(f32) * dot_nn(b, ge)
        dx = dx + fs.astype(f32) * dot_nn(b, gs)
        dx_ref[rows, :] = dx.astype(bf16)
        dy_lv = dy * lv
        dc = dot_nn(da, b) + dot_nt(dy * en, sf_ref[state, :]) + dot_nt(dy_lv, rn_ref[state, :])
        db = dot_tn(da, c) + dot_nt(x * te, ge) + dot_nt(x * fs, gs)
        shared_ref[:state_size, rows] = db.T.astype(bf16)
        shared_ref[state_size:, rows] = dc.T.astype(bf16)
        carry[...] = dt_ref[k] * carry[...] + dot_tn(c, dy_lv)
        return 0

    lax.fori_loop(0, chunks, gradients, 0, unroll=16)
    out_stores = [
        pltpu.make_async_copy(source, target, stores.at[n])
        for n, (source, target) in enumerate(zip((dx_ref, shared_ref), out_hbm))
    ]
    for store in out_stores:
        store.start()
    for store in out_stores:
        store.wait()


def sum_kernel(parts_ref, dx_ref, sum_ref, packed_ref):
    total = parts_ref[0].astype(f32)
    for n in range(1, parts_ref.shape[0]):
        total = total + parts_ref[n].astype(f32)
    total = total.astype(bf16)
    sum_ref[...] = total
    count = packed_ref.shape[0]
    part, tokens = total.shape[0], total.shape[1] // count
    if packed_ref.shape[1] > tokens + part or packed_ref.shape[2] > dx_ref.shape[1]:
        packed_ref[...] = jnp.zeros_like(packed_ref)
    for n in range(count):
        block = slice(n * tokens, (n + 1) * tokens)
        packed_ref[n, :tokens, : dx_ref.shape[1]] = dx_ref[block, :]
        packed_ref[n, tokens : tokens + part, :tokens] = total[:, block]


def tokens_kernel(layout, place_ref, packed_ref, *refs):
    arrays = len(layout)
    column_refs, out_ref, lhs_refs = refs[:arrays], refs[arrays], refs[arrays + 1 :]
    count = packed_ref.shape[0]
    tokens = out_ref.shape[1]

    @pl.when(pl.program_id(0) == 0)
    def _():
        for lhs_ref, parts in zip(lhs_refs, layout):
            column = 0
            for r, start, extent in parts:
                source = lax.bitwise_xor(place_ref[0], r)
                block = packed_ref[source, :tokens, start : start + extent]
                lhs_ref[:, column : column + extent] = block
                column += extent
        width = layout[0][0][2]
        rows = (lhs_refs[0].shape[1] - width) // count
        turned = [packed_ref[n, tokens : tokens + rows, :tokens] for n in range(count)]
        lhs_refs[0][:, width:] = jnp.concatenate(turned, axis=0).T

    result = dot_nt(lhs_refs[0][...], column_refs[0][...])
    for lhs_ref, column_ref in zip(lhs_refs[1:], column_refs[1:]):
        result = result + dot_nt(lhs_ref[...], column_ref[:, : lhs_ref.shape[1]])
    out_ref[0] = result.astype(bf16)


def spread_kernel(blocks_ref, out_ref):
    width = blocks_ref.shape[2]
    for n in range(blocks_ref.shape[0]):
        out_ref[0, :, n * width : (n + 1) * width] = blocks_ref[n]


def add_kernel(*refs):
    head_ref, shared_refs, out_ref = refs[0], refs[1:-1], refs[-1]
    rows = head_ref.shape[1]
    out_ref[:, :rows, :] = head_ref[...]
    total = shared_refs[0][...].astype(f32)
    for ref in shared_refs[1:]:
        total = total + ref[...].astype(f32)
    total = total.astype(bf16)
    if out_ref.shape[2] > total.shape[2]:
        out_ref[:, rows:, :] = jnp.zeros_like(out_ref[:, rows:, :])
    out_ref[:, rows:, : total.shape[2]] = total


def weight_kernel(sources, arrays, slots, group, parts, is_turned, places_ref, *refs):
    array_refs, grad_ref = refs[:arrays], refs[arrays]
    out_refs, (held, total, result, sems) = refs[arrays + 1 : -4], refs[-4:]
    pieces = len(sources)
    rows = held.shape[1]
    hidden = held.shape[2]

    def fetch(i):
        array, start = sources[i]
        source = array_refs[array].at[pl.ds(start, rows)]
        return pltpu.make_async_copy(source, held.at[i % slots], sems.at[i % slots])

    for i in range(slots):
        fetch(i).start()
    for first in range(0, pieces, group):
        turned = []
        for i in range(first, first + group):
            offset = (2 * lax.bitwise_xor(places_ref[0], i // 2) + i % 2) * rows
            target = pl.ds(pl.multiple_of(offset, rows), rows)
            turned.append(grad_ref[:, target] if is_turned else grad_ref[target, :].T)
        for i in range(first, first + group):
            fetch(i).wait()
        slot = first % slots
        block = held[slot : slot + group].reshape(group * rows, hidden)
        term = dot_nn(jnp.concatenate(turned, axis=1), block)
        if first > 0:
            term = term + total[...]
        if first + group < pieces:
            total[...] = term
        else:
            result[...] = term.T.astype(bf16)
        for i in range(first, first + group):
            if i + slots < pieces:
                fetch(i + slots).start()
    columns = result.shape[1]
    each = out_refs[0].shape[-2] * out_refs[0].shape[-1] // columns
    count = hidden // (parts * each)
    for k in range(parts):
        for j in range(count):
            if len(out_refs) == 1:
                out_refs[0][k, j] = result[(j * parts + k) * each : (j * parts + k + 1) * each, :]
                continue
            mine = (j * parts + lax.bitwise_xor(places_ref[1], k)) * each
            rows = out_refs[k].shape[1]
            for q in range(each // rows):
                source = pl.ds(pl.multiple_of(mine + q * rows, rows), rows)
                out_refs[k][j, :, q * columns : (q + 1) * columns] = result[source, :]


def finish_kernel(packed_ref, out_ref):
    count, _, width = packed_ref.shape
    rows = out_ref.shape[0]
    extra = packed_ref.shape[1] - rows
    part = (out_ref.shape[1] - count * width) // count
    for n in range(count):
        out_ref[:, n * width : (n + 1) * width] = packed_ref[n, :rows].astype(f32)
        start = count * width + n * part
        for q in range(rows // extra):
            block = packed_ref[n, rows:, q * part : (q + 1) * part]
            out_ref[q * extra : (q + 1) * extra, start : start + part] = block.astype(f32)


def resident(array):
    return pl.BlockSpec(array.shape, lambda k: (0,) * len(array.shape))


def after(value, *earlier):
    return lax.optimization_barrier((value,) + earlier)[0]


def permute_xor(a, axis, mask):
    count = lax.axis_size(axis)
    return lax.ppermute(a, axis, [(i, i ^ mask) for i in range(count)])


def gather_rows(rows, axis, beside, work):
    count = lax.axis_size(axis)
    bits = count.bit_length() - 1
    half = rows.shape[0] // 2
    if bits == 3:
        held = {r: permute_xor(rows, axis, r) for r in (2, 4, 1)}
        held, beside = lax.optimization_barrier((held, beside))
        held[3], held[5] = permute_xor(held[2], axis, 1), permute_xor(held[4], axis, 1)
        corner = [
            permute_xor(held[2][:half], axis, 4),
            permute_xor(held[4][half:], axis, 2),
        ]
        held, corner, done = lax.optimization_barrier((held, corner, work(*beside)))
        held = {r: [a] for r, a in held.items()}
        held[0], held[6] = [rows], corner
        held[7] = [permute_xor(a, axis, 1) for a in corner]
    else:
        done = work(*beside)
        upper = list(range(1, bits))
        orders = (upper + [0], upper[1:] + upper[:1] + [0])
        both = ({0: rows[:half]}, {0: rows[half:]})
        for step in range(bits):
            for part in range(2):
                mask = 1 << orders[part][step]
                for r in list(both[part]):
                    both[part][r ^ mask] = permute_xor(both[part][r], axis, mask)
        held = {r: [both[0][r], both[1][r]] for r in range(count)}
    arrays, sources = [], []
    for r in range(count):
        for part in range(2):
            whole_block = len(held[r]) == 1
            if part == 0 or not whole_block:
                arrays.append(held[r][part])
            sources.append((len(arrays) - 1, half * part if whole_block else 0))
    return arrays, tuple(sources), done


def exchange_xor(pieces, axis):
    return [pieces[0]] + [permute_xor(p, axis, r) for r, p in enumerate(pieces) if r > 0]


def tables_kernel(log_ref, *refs):
    out_refs, table_refs, sems = refs[:7], refs[7:14], refs[14]
    te_ref, fs_ref, en_ref, lv_ref, dt_ref, m_ref, mt_ref = table_refs
    heads = log_ref.shape[0]
    chunks = dt_ref.shape[0]
    head_size = te_ref.shape[1] // heads
    row = lax.broadcasted_iota(jnp.int32, (CHUNK, CHUNK), 0)
    col = lax.broadcasted_iota(jnp.int32, (CHUNK, CHUNK), 1)
    logs = jnp.concatenate(
        [log_ref[:, k * CHUNK : (k + 1) * CHUNK] for k in range(chunks)], axis=0
    )
    cumulative = lax.dot_general(
        logs, (row <= col).astype(f32), (((1,), (0,)), ((), ())),
        precision=lax.Precision.HIGHEST, preferred_element_type=f32,
    )
    exclusive = cumulative - logs
    cum_t, exc_t = cumulative.T, exclusive.T
    total = cum_t[CHUNK - 1 : CHUNK, :]
    spreads = (
        (te_ref, jnp.exp(total - cum_t)),
        (fs_ref, jnp.exp(exc_t)),
        (en_ref, jnp.exp(cum_t)),
        (lv_ref, jnp.exp(total - exc_t)),
    )
    chunk_decay = jnp.exp(total)
    diagonal = (row == col).astype(f32)
    for k in range(chunks):
        rows = slice(k * CHUNK, (k + 1) * CHUNK)
        picked = range(k * heads, (k + 1) * heads)
        for ref, source in spreads:
            ref[rows, :] = jnp.concatenate(
                [jnp.broadcast_to(source[:, n : n + 1], (CHUNK, head_size)) for n in picked], axis=1
            ).astype(bf16)
        dt_ref[k] = jnp.concatenate(
            [jnp.broadcast_to(chunk_decay[:, n : n + 1], (1, head_size)) for n in picked], axis=1
        )
        for h, n in enumerate(picked):
            cum_col, exc_col = cum_t[:, n : n + 1], exc_t[:, n : n + 1]
            cum_row, exc_row = cumulative[n : n + 1, :], exclusive[n : n + 1, :]
            below, above = cum_col - cum_row, exc_row - exc_col
            exponent = jnp.where(row > col, below, jnp.where(row < col, above, 0.0))
            turned = jnp.where(row < col, -below, jnp.where(row > col, -above, 0.0))
            columns = slice(h * CHUNK, (h + 1) * CHUNK)
            m_ref[rows, columns] = (jnp.exp(exponent) + diagonal).astype(bf16)
            mt_ref[rows, columns] = (jnp.exp(turned) + diagonal).astype(bf16)
    stores = [
        pltpu.make_async_copy(source, target, sems.at[n])
        for n, (source, target) in enumerate(zip(table_refs, out_refs))
    ]
    for store in stores:
        store.start()
    for store in stores:
        store.wait()


def on_device(tokens, w_in, log_decay, grad_out):
    local_tokens = tokens[0]
    upstream = grad_out[0]
    token_count, hidden_width = local_tokens.shape
    head_count = log_decay.shape[1]
    inner_width = upstream.shape[1]
    head_size = inner_width // head_count
    state_size = (w_in.shape[1] - inner_width) // 2
    seq_count = lax.axis_size("seq")
    fsdp_count = lax.axis_size("fsdp")
    place = lax.axis_index("seq")
    row_place = lax.axis_index("fsdp")
    heads = head_count // seq_count
    width = heads * head_size
    length = token_count * seq_count
    shared = 2 * state_size
    chunks = length // CHUNK
    shape = jax.ShapeDtypeStruct
    params = pltpu.CompilerParams(vmem_limit_bytes=VMEM_LIMIT)
    scalar = [pl.BlockSpec(memory_space=pltpu.SMEM)]
    places = jnp.stack([place, row_place]).astype(jnp.int32)

    def cost(flops, moved):
        return pl.CostEstimate(flops=flops, bytes_accessed=moved, transcendentals=0)

    def columns(r):
        return lax.dynamic_slice_in_dim(w_in, lax.bitwise_xor(place, r) * width, width, 1)

    w_columns = lax.all_gather(
        jnp.concatenate([columns(0), w_in[:, inner_width:]], axis=1), "fsdp", axis=0, tiled=True
    )
    log_rates = lax.all_to_all(log_decay[0], "seq", 0, 1, tiled=True)

    table_shapes = (
        [shape((length, width), bf16)] * 4
        + [shape((chunks, 1, width), f32)]
        + [shape((length, heads * CHUNK), bf16)] * 2
    )
    in_hbm = [pl.BlockSpec(memory_space=pltpu.HBM)]
    scratch = lambda *buffers: [pltpu.VMEM(a.shape, a.dtype) for a in buffers]
    make_tables = pl.pallas_call(
        tables_kernel,
        grid=(1,),
        out_shape=table_shapes,
        in_specs=[resident(log_rates)],
        out_specs=in_hbm * 7,
        scratch_shapes=scratch(*table_shapes) + [pltpu.SemaphoreType.DMA((7,))],
        compiler_params=params,
        cost_estimate=cost(0, 120 * length * width),
    )
    neighbours = [r for r in range(2, seq_count, 2) if r & (r - 1) == 0]
    others = [r for r in range(2, seq_count, 2) if r & (r - 1)]
    first_part = width // 2
    rest = [columns(r) for r in others] + [columns(r)[:, :first_part] for r in neighbours]

    blocks = upstream.reshape(token_count, seq_count, width).transpose(1, 0, 2)
    rest = jnp.concatenate(rest, axis=1)
    arrays, sources, (tables, upstream, rest, places) = gather_rows(
        local_tokens,
        "seq",
        (log_rates, blocks, rest, places),
        lambda log_rates, *others: (make_tables(log_rates), *others),
    )
    to_end, from_start, enter, leave, chunk_decay, decays, turned = tables

    count = len(sources)
    slots = min(count, 16)
    group = min(slots, 4)
    held = shape((slots, token_count // 2, hidden_width), bf16)
    by_position = shape((length, width), bf16)
    by_state = shape((chunks * state_size, width), bf16)
    state_rows = shape((length, state_size), bf16)
    mean = shape((width, width), bf16)
    carry = shape((state_size, width), f32)

    w_even = lax.all_gather(rest, "fsdp", axis=0, tiled=True)
    upstream = after(upstream, w_columns)

    *arrays, w_columns = lax.optimization_barrier((*arrays, w_columns))
    g = lax.all_to_all(upstream, "seq", 0, 0).reshape(length, width)
    operands = (w_columns, decays, to_end, from_start, enter, leave, chunk_decay)
    kept = [by_position, state_rows, state_rows, by_position, by_position, by_state, by_state]
    forward = pl.pallas_call(
        functools.partial(
            forward_kernel, sources, len(arrays), slots, group, heads, head_size
        ),
        out_shape=kept,
        in_specs=scalar + in_hbm * (len(arrays) + 7),
        out_specs=in_hbm * 7,
        scratch_shapes=scratch(*operands, *kept, held, mean, carry)
        + [
            pltpu.SemaphoreType.DMA((slots,)),
            pltpu.SemaphoreType.DMA((7,)),
            pltpu.SemaphoreType.DMA((7,)),
        ],
        compiler_params=params,
        cost_estimate=cost(
            4 * length * hidden_width * (width + shared) + 160 * length * width * CHUNK,
            4 * length * hidden_width,
        ),
    )(places, *arrays, *operands)
    w_partner = permute_xor(w_columns, "seq", 1)
    forward, g, w_partner = lax.optimization_barrier((forward, g, w_partner))
    x, b, c, z, inverse, states_in, states_next = forward

    mixed_blocks = lax.all_to_all(z.reshape(seq_count, token_count, width), "seq", 0, 0)
    operands = (
        g, z, inverse, c, enter, chunk_decay,
        x, b, decays, turned, to_end, from_start, leave, states_in, states_next,
    )
    grads = [by_position, shape((shared, length), bf16)]
    backward = pl.pallas_call(
        functools.partial(backward_kernel, heads, head_size),
        out_shape=grads,
        in_specs=in_hbm * 15,
        out_specs=in_hbm * 2,
        scratch_shapes=scratch(*operands, *grads, by_position, by_state, mean, carry)
        + [pltpu.SemaphoreType.DMA((15,)), pltpu.SemaphoreType.DMA((2,))],
        compiler_params=params,
        cost_estimate=cost(240 * length * width * CHUNK, 40 * length * width),
    )(*operands)
    backward, mixed_blocks = lax.optimization_barrier((backward, mixed_blocks))
    dx, shared_partial = backward

    rows_each = hidden_width // (seq_count * fsdp_count)
    extra = 16

    def weight_columns(grad, columns, is_turned):
        total = shape((columns, hidden_width), f32)
        result = shape((hidden_width, columns), bf16)
        if not is_turned:
            parts = [shape((fsdp_count, seq_count, rows_each, columns), bf16)]
        else:
            parts = [shape((seq_count, extra, columns * rows_each // extra), bf16)] * fsdp_count
        return pl.pallas_call(
            functools.partial(weight_kernel, sources, len(arrays), slots, group, fsdp_count, is_turned),
            out_shape=parts,
            grid=(1,),
            in_specs=scalar + in_hbm * len(arrays) + [resident(grad)],
            out_specs=[resident(a) for a in parts],
            scratch_shapes=scratch(held, total, result) + [pltpu.SemaphoreType.DMA((slots,))],
            compiler_params=params,
            cost_estimate=cost(4 * length * hidden_width * columns, 4 * length * hidden_width),
        )(places, *arrays, grad)

    part = shared // seq_count
    arrived = lax.all_to_all(shared_partial.reshape(seq_count, part, length), "seq", 0, 0)
    (head_weights,) = weight_columns(dx, width, False)
    head_sums = lax.psum_scatter(
        head_weights.reshape(hidden_width, width), "fsdp", scatter_dimension=0, tiled=True
    ).reshape(seq_count, rows_each, width)
    second_part = after(w_columns, head_weights)[:, first_part:width]
    w_across = [permute_xor(second_part, "seq", r) for r in neighbours]
    arrived, second_part, w_even = lax.optimization_barrier((arrived, second_part, w_even))
    sums = [
        shape((part, length), bf16),
        shape((seq_count, token_count + max(part, 16), max(width, token_count)), bf16),
    ]
    shared_columns, packed = pl.pallas_call(
        sum_kernel,
        grid=(1,),
        out_shape=sums,
        in_specs=[resident(arrived), resident(dx)],
        out_specs=[resident(a) for a in sums],
        compiler_params=params,
    )(arrived, dx)

    grad_blocks = lax.all_to_all(packed, "seq", 0, 0)
    shared_weights = weight_columns(shared_columns, part, True)
    shared_arrived = exchange_xor(shared_weights, "fsdp")
    mixed_shape = shape((1, token_count, inner_width), bf16)
    mixer_out = pl.pallas_call(
        spread_kernel,
        grid=(1,),
        out_shape=mixed_shape,
        in_specs=[resident(mixed_blocks)],
        out_specs=resident(mixed_shape),
        compiler_params=params,
    )(after(mixed_blocks, shared_columns))
    w_even = [w_even, *(after(a, shared_weights[0]) for a in w_across)]
    w_odd = [permute_xor(a, "seq", 1) for a in w_even]
    shared_arrived, mixer_out, w_odd, head_sums = lax.optimization_barrier(
        (shared_arrived, mixer_out, w_odd, head_sums)
    )

    grad_tokens_shape = shape((1, token_count, hidden_width), bf16)
    steps = 2
    rows = hidden_width // steps
    by_rows = lambda a: pl.BlockSpec((rows, a.shape[1]), lambda k: (k, 0))
    layout = [[(r, 0, width) for r in others] + [(r, 0, first_part) for r in neighbours]]
    layout += [[(r, first_part, width - first_part)] for r in neighbours]
    odd_layout = [[(r + 1, start, extent) for r, start, extent in parts] for parts in layout]
    layout = [[(0, 0, width)], [(1, 0, width)]] + layout + odd_layout
    lhs_shapes = [
        shape((token_count, sum(part[2] for part in parts) + (shared if n == 0 else 0)), bf16)
        for n, parts in enumerate(layout)
    ]
    w_blocks = [w_columns, w_partner, *w_even, *w_odd]
    grad_tokens = pl.pallas_call(
        functools.partial(tokens_kernel, layout),
        grid=(steps,),
        out_shape=grad_tokens_shape,
        in_specs=scalar + [resident(grad_blocks)] + [by_rows(a) for a in w_blocks],
        out_specs=pl.BlockSpec((1, token_count, rows), lambda k: (0, 0, k)),
        scratch_shapes=scratch(*lhs_shapes),
        compiler_params=params,
        cost_estimate=cost(
            4 * token_count * hidden_width * (inner_width + shared),
            4 * hidden_width * (inner_width + shared),
        ),
    )(places, grad_blocks, *w_blocks)
    packed = shape((seq_count, rows_each + extra, width), bf16)
    packed_sums = pl.pallas_call(
        add_kernel,
        grid=(1,),
        out_shape=packed,
        in_specs=[resident(a) for a in [head_sums, *shared_arrived]],
        out_specs=resident(packed),
        compiler_params=params,
    )(head_sums, *shared_arrived)
    owned = lax.all_to_all(after(packed_sums, grad_blocks), "seq", 0, 0)
    finished = shape((rows_each, inner_width + shared), f32)
    grad_weights = pl.pallas_call(
        finish_kernel,
        grid=(1,),
        out_shape=finished,
        in_specs=[resident(owned)],
        out_specs=resident(finished),
        compiler_params=params,
    )(owned)
    return mixer_out, grad_tokens, grad_weights


def solution(mesh):
    return jax.shard_map(
        on_device,
        mesh=mesh,
        in_specs=(
            P("fsdp", "seq", None),
            P("fsdp", None),
            P("fsdp", None, "seq"),
            P("fsdp", "seq", None),
        ),
        out_specs=(P("fsdp", "seq", None), P("fsdp", "seq", None), P(("seq", "fsdp"), None)),
        check_vma=False,
    )
```

```python
import functools

import jax
import jax.numpy as jnp
from jax import lax
from jax.experimental import pallas as pl
from jax.experimental.pallas import tpu as pltpu
from jax.sharding import PartitionSpec as P

CHUNK = 128
EPSILON = 1e-05
VMEM_LIMIT = 60 * 1024 * 1024

f32 = jnp.float32
bf16 = jnp.bfloat16


def dot_nn(a, b):
    return lax.dot_general(a, b, (((1,), (0,)), ((), ())), preferred_element_type=f32)


def dot_nt(a, b):
    return lax.dot_general(a, b, (((1,), (1,)), ((), ())), preferred_element_type=f32)


def dot_tn(a, b):
    return lax.dot_general(a, b, (((0,), (0,)), ((), ())), preferred_element_type=f32)


def by_head(rows, heads, head_size):
    if heads == 1:
        return rows
    lane = lax.broadcasted_iota(jnp.int32, rows.shape, 1)
    parts = []
    for h in range(heads):
        inside = (lane >= h * head_size) & (lane < (h + 1) * head_size)
        parts.append(jnp.where(inside, rows, jnp.zeros_like(rows)))
    return jnp.concatenate(parts, axis=0)


def decayed(affinity, decays, heads):
    tiled = jnp.concatenate([affinity] * heads, axis=1) if heads > 1 else affinity
    return (tiled * decays.astype(f32)).astype(bf16)


def spans(k, state_size):
    rows = pl.ds(pl.multiple_of(k * CHUNK, CHUNK), CHUNK)
    return rows, pl.ds(pl.multiple_of(k * state_size, state_size), state_size)


def fill_mean(mean_ref, heads, head_size):
    row = lax.broadcasted_iota(jnp.int32, mean_ref.shape, 0)
    col = lax.broadcasted_iota(jnp.int32, mean_ref.shape, 1)
    same = jnp.zeros(mean_ref.shape, jnp.bool_)
    for h in range(heads):
        low, high = h * head_size, (h + 1) * head_size
        same |= (row >= low) & (row < high) & (col >= low) & (col < high)
    mean_ref[...] = jnp.where(same, 1.0 / head_size, 0.0).astype(bf16)


def forward_kernel(sources, arrays, slots, group, heads, head_size, place_ref, *refs):
    array_refs, refs = refs[:arrays], refs[arrays:]
    in_hbm, out_hbm, refs = refs[:7], refs[7:14], refs[14:]
    in_refs, out_refs, refs = refs[:7], refs[7:14], refs[14:]
    held, mean_ref, carry, y_ref, sems, loads, stores, y_sems = refs
    w_ref, m_ref, te_ref, fs_ref, en_ref, lv_ref, dt_ref = in_refs
    x_ref, b_ref, c_ref, z_ref, rs_ref, sf_ref, rn_ref = out_refs
    pieces = len(sources)
    rows_each = held.shape[1]
    width, state_size = x_ref.shape[1], b_ref.shape[1]
    chunks = dt_ref.shape[0]

    def fetch(i):
        array, start = sources[i]
        source = array_refs[array].at[pl.ds(start, rows_each)]
        return pltpu.make_async_copy(source, held.at[i % slots], sems.at[i % slots])

    in_loads = [
        pltpu.make_async_copy(source, target, loads.at[n])
        for n, (source, target) in enumerate(zip(in_hbm, in_refs))
    ]
    out_stores = [
        pltpu.make_async_copy(source, target, stores.at[n])
        for n, (source, target) in enumerate(zip(out_refs, out_hbm))
    ]
    in_loads[0].start()
    for i in range(slots):
        fetch(i).start()
    for load in in_loads[1:]:
        load.start()
    fill_mean(mean_ref, heads, head_size)

    in_loads[0].wait()
    for first in range(0, pieces, group):
        for i in range(first, first + group):
            fetch(i).wait()
        slot = first % slots
        block = held[slot : slot + group].reshape(group * rows_each, held.shape[2])
        result = dot_nn(block, w_ref[...]).astype(bf16)
        for i in range(first, first + group):
            if i + slots < pieces:
                fetch(i + slots).start()
            offset = (2 * lax.bitwise_xor(place_ref[0], i // 2) + i % 2) * rows_each
            target = pl.ds(pl.multiple_of(offset, rows_each), rows_each)
            part = slice((i - first) * rows_each, (i - first + 1) * rows_each)
            x_ref[target, :] = result[part, :width]
            b_ref[target, :] = result[part, width : width + state_size]
            c_ref[target, :] = result[part, width + state_size :]
    for store in out_stores[:3]:
        store.start()
    for load in in_loads[1:]:
        load.wait()

    carry[...] = jnp.zeros_like(carry)

    def reverse_states(i, _):
        k = chunks - 1 - i
        rows, state = spans(k, state_size)
        rn_ref[state, :] = carry[...].astype(bf16)
        term = dot_tn(b_ref[rows, :], x_ref[rows, :] * fs_ref[rows, :])
        carry[...] = dt_ref[k] * carry[...] + term
        return 0

    lax.fori_loop(0, chunks, reverse_states, 0, unroll=16)
    out_stores[6].start()
    carry[...] = jnp.zeros_like(carry)

    def outputs(k, _):
        rows, state = spans(k, state_size)
        x, b, c = x_ref[rows, :], b_ref[rows, :], c_ref[rows, :]
        state_in = carry[...].astype(bf16)
        sf_ref[state, :] = state_in
        weights = decayed(dot_nt(c, b), m_ref[rows, :], heads)
        y = dot_nn(weights, by_head(x, heads, head_size))
        y = y + en_ref[rows, :].astype(f32) * dot_nn(c, state_in)
        y = y + lv_ref[rows, :].astype(f32) * dot_nn(c, rn_ref[state, :])
        y_ref[rows, :] = y
        carry[...] = dt_ref[k] * carry[...] + dot_tn(b, x * te_ref[rows, :])
        return 0

    lax.fori_loop(0, chunks, outputs, 0, unroll=16)
    out_stores[5].start()
    block_stores = []
    block = y_ref.shape[0] // (y_sems.shape[0] // 2)
    for n in range(y_sems.shape[0] // 2):
        rows = pl.ds(n * block, block)
        y = y_ref[rows, :]
        mean_square = dot_nn((y * y).astype(bf16), mean_ref[...])
        inverse = lax.rsqrt(mean_square + EPSILON)
        z_ref[rows, :] = (y * inverse).astype(bf16)
        rs_ref[rows, :] = inverse.astype(bf16)
        for m in (3, 4):
            source, target = out_refs[m].at[rows], out_hbm[m].at[rows]
            store = pltpu.make_async_copy(source, target, y_sems.at[2 * n + m - 3])
            store.start()
            block_stores.append(store)
    for store in out_stores[:3] + out_stores[5:] + block_stores:
        store.wait()


def backward_kernel(heads, head_size, *refs):
    in_hbm, out_hbm, refs = refs[:15], refs[15:17], refs[17:]
    in_refs, (dx_ref, shared_ref), refs = refs[:15], refs[15:17], refs[17:]
    dy_ref, ge_ref, mean_ref, carry, loads, stores = refs
    g_ref, z_ref, rs_ref, c_ref, en_ref, dt_ref = in_refs[:6]
    x_ref, b_ref, m_ref, mt_ref, te_ref, fs_ref, lv_ref, sf_ref, rn_ref = in_refs[6:15]
    state_size = b_ref.shape[1]
    chunks = dt_ref.shape[0]
    in_loads = [
        pltpu.make_async_copy(source, target, loads.at[n])
        for n, (source, target) in enumerate(zip(in_hbm, in_refs))
    ]
    for load in in_loads:
        load.start()
    fill_mean(mean_ref, heads, head_size)
    carry[...] = jnp.zeros_like(carry)
    for load in in_loads[:6]:
        load.wait()

    def end_adjoints(i, _):
        k = chunks - 1 - i
        rows, state = spans(k, state_size)
        g, z = g_ref[rows, :].astype(f32), z_ref[rows, :].astype(f32)
        mean_gz = dot_nn((g * z).astype(bf16), mean_ref[...])
        dy = ((g - z * mean_gz) * rs_ref[rows, :].astype(f32)).astype(bf16)
        dy_ref[rows, :] = dy
        ge_ref[state, :] = carry[...].astype(bf16)
        carry[...] = dt_ref[k] * carry[...] + dot_tn(c_ref[rows, :], dy * en_ref[rows, :])
        return 0

    lax.fori_loop(0, chunks, end_adjoints, 0, unroll=16)
    carry[...] = jnp.zeros_like(carry)
    for load in in_loads[6:]:
        load.wait()

    def gradients(k, _):
        rows, state = spans(k, state_size)
        x, b, c, dy = x_ref[rows, :], b_ref[rows, :], c_ref[rows, :], dy_ref[rows, :]
        te, fs, en, lv = te_ref[rows, :], fs_ref[rows, :], en_ref[rows, :], lv_ref[rows, :]
        ge, gs = ge_ref[state, :], carry[...].astype(bf16)
        grad_weights = dot_nt(dy, by_head(x, heads, head_size)) * m_ref[rows, :].astype(f32)
        da = grad_weights[:, :CHUNK]
        for h in range(1, heads):
            da = da + grad_weights[:, h * CHUNK : (h + 1) * CHUNK]
        da = da.astype(bf16)
        turned = decayed(dot_nt(b, c), mt_ref[rows, :], heads)
        dx = dot_nn(turned, by_head(dy, heads, head_size))
        dx = dx + te.astype(f32) * dot_nn(b, ge)
        dx = dx + fs.astype(f32) * dot_nn(b, gs)
        dx_ref[rows, :] = dx.astype(bf16)
        dy_lv = dy * lv
        dc = dot_nn(da, b) + dot_nt(dy * en, sf_ref[state, :]) + dot_nt(dy_lv, rn_ref[state, :])
        db = dot_tn(da, c) + dot_nt(x * te, ge) + dot_nt(x * fs, gs)
        shared_ref[:state_size, rows] = db.T.astype(bf16)
        shared_ref[state_size:, rows] = dc.T.astype(bf16)
        carry[...] = dt_ref[k] * carry[...] + dot_tn(c, dy_lv)
        return 0

    lax.fori_loop(0, chunks, gradients, 0, unroll=16)
    out_stores = [
        pltpu.make_async_copy(source, target, stores.at[n])
        for n, (source, target) in enumerate(zip((dx_ref, shared_ref), out_hbm))
    ]
    for store in out_stores:
        store.start()
    for store in out_stores:
        store.wait()


def sum_kernel(parts_ref, dx_ref, sum_ref, packed_ref):
    total = parts_ref[0].astype(f32)
    for n in range(1, parts_ref.shape[0]):
        total = total + parts_ref[n].astype(f32)
    total = total.astype(bf16)
    sum_ref[...] = total
    count = packed_ref.shape[0]
    part, tokens = total.shape[0], total.shape[1] // count
    if packed_ref.shape[1] > tokens + part or packed_ref.shape[2] > dx_ref.shape[1]:
        packed_ref[...] = jnp.zeros_like(packed_ref)
    for n in range(count):
        block = slice(n * tokens, (n + 1) * tokens)
        packed_ref[n, :tokens, : dx_ref.shape[1]] = dx_ref[block, :]
        packed_ref[n, tokens : tokens + part, :tokens] = total[:, block]


def tokens_kernel(layout, place_ref, packed_ref, *refs):
    arrays = len(layout)
    column_refs, out_ref, lhs_refs = refs[:arrays], refs[arrays], refs[arrays + 1 :]
    count = packed_ref.shape[0]
    tokens = out_ref.shape[1]

    @pl.when(pl.program_id(0) == 0)
    def _():
        for lhs_ref, parts in zip(lhs_refs, layout):
            column = 0
            for r, start, extent in parts:
                source = lax.bitwise_xor(place_ref[0], r)
                block = packed_ref[source, :tokens, start : start + extent]
                lhs_ref[:, column : column + extent] = block
                column += extent
        width = layout[0][0][2]
        rows = (lhs_refs[0].shape[1] - width) // count
        turned = [packed_ref[n, tokens : tokens + rows, :tokens] for n in range(count)]
        lhs_refs[0][:, width:] = jnp.concatenate(turned, axis=0).T

    result = dot_nt(lhs_refs[0][...], column_refs[0][...])
    for lhs_ref, column_ref in zip(lhs_refs[1:], column_refs[1:]):
        result = result + dot_nt(lhs_ref[...], column_ref[:, : lhs_ref.shape[1]])
    out_ref[0] = result.astype(bf16)


def joined_tokens_kernel(layout, steps, place_ref, packed_ref, *refs):
    arrays = len(layout)
    column_refs, out_ref, joined_ref, lhs_ref, sems = refs[:arrays], *refs[arrays:]
    count = packed_ref.shape[0]
    tokens = out_ref.shape[1]
    rows = joined_ref.shape[1]
    width = layout[0][0][2]
    part = (joined_ref.shape[2] - count * width) // count
    loads = []
    for step in range(steps):
        column = 0
        for n, parts in enumerate(layout):
            extent = sum(p[2] for p in parts) + (count * part if n == 0 else 0)
            source = column_refs[n].at[pl.ds(step * rows, rows), pl.ds(0, extent)]
            target = joined_ref.at[step, :, pl.ds(column, extent)]
            loads.append(pltpu.make_async_copy(source, target, sems.at[step * arrays + n]))
            loads[-1].start()
            column += extent

    column = 0
    for n, parts in enumerate(layout):
        for r, start, extent in parts:
            source = lax.bitwise_xor(place_ref[0], r)
            block = packed_ref[source, :tokens, start : start + extent]
            lhs_ref[:, column : column + extent] = block
            column += extent
        if n == 0:
            turned = [packed_ref[m, tokens : tokens + part, :tokens] for m in range(count)]
            lhs_ref[:, column : column + count * part] = jnp.concatenate(turned, axis=0).T
            column += count * part
    for step in range(steps):
        for load in loads[step * arrays : (step + 1) * arrays]:
            load.wait()
        result = dot_nt(lhs_ref[...], joined_ref[step])
        out_ref[0, :, step * rows : (step + 1) * rows] = result.astype(bf16)


def spread_kernel(blocks_ref, out_ref):
    width = blocks_ref.shape[2]
    for n in range(blocks_ref.shape[0]):
        out_ref[0, :, n * width : (n + 1) * width] = blocks_ref[n]


def add_kernel(*refs):
    head_ref, shared_refs, out_ref = refs[0], refs[1:-1], refs[-1]
    rows = head_ref.shape[1]
    out_ref[:, :rows, :] = head_ref[...]
    total = shared_refs[0][...].astype(f32)
    for ref in shared_refs[1:]:
        total = total + ref[...].astype(f32)
    total = total.astype(bf16)
    if out_ref.shape[2] > total.shape[2]:
        out_ref[:, rows:, :] = jnp.zeros_like(out_ref[:, rows:, :])
    out_ref[:, rows:, : total.shape[2]] = total


def weight_kernel(sources, arrays, slots, group, parts, is_turned, places_ref, *refs):
    array_refs, grad_ref = refs[:arrays], refs[arrays]
    out_refs, (held, total, result, sems) = refs[arrays + 1 : -4], refs[-4:]
    pieces = len(sources)
    rows = held.shape[1]
    hidden = held.shape[2]

    def fetch(i):
        array, start = sources[i]
        source = array_refs[array].at[pl.ds(start, rows)]
        return pltpu.make_async_copy(source, held.at[i % slots], sems.at[i % slots])

    for i in range(slots):
        fetch(i).start()
    for first in range(0, pieces, group):
        turned = []
        for i in range(first, first + group):
            offset = (2 * lax.bitwise_xor(places_ref[0], i // 2) + i % 2) * rows
            target = pl.ds(pl.multiple_of(offset, rows), rows)
            turned.append(grad_ref[:, target] if is_turned else grad_ref[target, :].T)
        for i in range(first, first + group):
            fetch(i).wait()
        slot = first % slots
        block = held[slot : slot + group].reshape(group * rows, hidden)
        term = dot_nn(jnp.concatenate(turned, axis=1), block)
        if first > 0:
            term = term + total[...]
        if first + group < pieces:
            total[...] = term
        else:
            result[...] = term.T.astype(bf16)
        for i in range(first, first + group):
            if i + slots < pieces:
                fetch(i + slots).start()
    columns = result.shape[1]
    each = out_refs[0].shape[-2] * out_refs[0].shape[-1] // columns
    count = hidden // (parts * each)
    for k in range(parts):
        for j in range(count):
            if len(out_refs) == 1:
                out_refs[0][k, j] = result[(j * parts + k) * each : (j * parts + k + 1) * each, :]
                continue
            mine = (j * parts + lax.bitwise_xor(places_ref[1], k)) * each
            rows = out_refs[k].shape[1]
            for q in range(each // rows):
                source = pl.ds(pl.multiple_of(mine + q * rows, rows), rows)
                out_refs[k][j, :, q * columns : (q + 1) * columns] = result[source, :]


def finish_kernel(packed_ref, out_ref):
    count, _, width = packed_ref.shape
    rows = out_ref.shape[0]
    extra = packed_ref.shape[1] - rows
    part = (out_ref.shape[1] - count * width) // count
    for n in range(count):
        out_ref[:, n * width : (n + 1) * width] = packed_ref[n, :rows].astype(f32)
        start = count * width + n * part
        for q in range(rows // extra):
            block = packed_ref[n, rows:, q * part : (q + 1) * part]
            out_ref[q * extra : (q + 1) * extra, start : start + part] = block.astype(f32)


def resident(array):
    return pl.BlockSpec(array.shape, lambda k: (0,) * len(array.shape))


def after(value, *earlier):
    return lax.optimization_barrier((value,) + earlier)[0]


def permute_xor(a, axis, mask):
    count = lax.axis_size(axis)
    return lax.ppermute(a, axis, [(i, i ^ mask) for i in range(count)])


def gather_rows(rows, axis, beside, work):
    count = lax.axis_size(axis)
    bits = count.bit_length() - 1
    half = rows.shape[0] // 2
    if bits == 3:
        held = {r: permute_xor(rows, axis, r) for r in (2, 4, 1)}
        held, beside = lax.optimization_barrier((held, beside))
        held[3], held[5] = permute_xor(held[2], axis, 1), permute_xor(held[4], axis, 1)
        corner = [
            permute_xor(held[2][:half], axis, 4),
            permute_xor(held[4][half:], axis, 2),
        ]
        held, corner, done = lax.optimization_barrier((held, corner, work(*beside)))
        held = {r: [a] for r, a in held.items()}
        held[0], held[6] = [rows], corner
        held[7] = [permute_xor(a, axis, 1) for a in corner]
    else:
        done = work(*beside)
        upper = list(range(1, bits))
        orders = (upper + [0], upper[1:] + upper[:1] + [0])
        both = ({0: rows[:half]}, {0: rows[half:]})
        for step in range(bits):
            for part in range(2):
                mask = 1 << orders[part][step]
                for r in list(both[part]):
                    both[part][r ^ mask] = permute_xor(both[part][r], axis, mask)
        held = {r: [both[0][r], both[1][r]] for r in range(count)}
    arrays, sources = [], []
    for r in range(count):
        for part in range(2):
            whole_block = len(held[r]) == 1
            if part == 0 or not whole_block:
                arrays.append(held[r][part])
            sources.append((len(arrays) - 1, half * part if whole_block else 0))
    return arrays, tuple(sources), done


def exchange_xor(pieces, axis):
    return [pieces[0]] + [permute_xor(p, axis, r) for r, p in enumerate(pieces) if r > 0]


def tables_kernel(log_ref, *refs):
    out_refs, table_refs, sems = refs[:7], refs[7:14], refs[14]
    te_ref, fs_ref, en_ref, lv_ref, dt_ref, m_ref, mt_ref = table_refs
    heads = log_ref.shape[0]
    chunks = dt_ref.shape[0]
    head_size = te_ref.shape[1] // heads
    row = lax.broadcasted_iota(jnp.int32, (CHUNK, CHUNK), 0)
    col = lax.broadcasted_iota(jnp.int32, (CHUNK, CHUNK), 1)
    logs = jnp.concatenate(
        [log_ref[:, k * CHUNK : (k + 1) * CHUNK] for k in range(chunks)], axis=0
    )
    cumulative = lax.dot_general(
        logs, (row <= col).astype(f32), (((1,), (0,)), ((), ())),
        precision=lax.Precision.HIGHEST, preferred_element_type=f32,
    )
    exclusive = cumulative - logs
    cum_t, exc_t = cumulative.T, exclusive.T
    total = cum_t[CHUNK - 1 : CHUNK, :]
    spreads = (
        (te_ref, jnp.exp(total - cum_t)),
        (fs_ref, jnp.exp(exc_t)),
        (en_ref, jnp.exp(cum_t)),
        (lv_ref, jnp.exp(total - exc_t)),
    )
    chunk_decay = jnp.exp(total)
    diagonal = (row == col).astype(f32)
    for k in range(chunks):
        rows = slice(k * CHUNK, (k + 1) * CHUNK)
        picked = range(k * heads, (k + 1) * heads)
        for ref, source in spreads:
            ref[rows, :] = jnp.concatenate(
                [jnp.broadcast_to(source[:, n : n + 1], (CHUNK, head_size)) for n in picked], axis=1
            ).astype(bf16)
        dt_ref[k] = jnp.concatenate(
            [jnp.broadcast_to(chunk_decay[:, n : n + 1], (1, head_size)) for n in picked], axis=1
        )
        for h, n in enumerate(picked):
            cum_col, exc_col = cum_t[:, n : n + 1], exc_t[:, n : n + 1]
            cum_row, exc_row = cumulative[n : n + 1, :], exclusive[n : n + 1, :]
            below, above = cum_col - cum_row, exc_row - exc_col
            exponent = jnp.where(row > col, below, jnp.where(row < col, above, 0.0))
            turned = jnp.where(row < col, -below, jnp.where(row > col, -above, 0.0))
            columns = slice(h * CHUNK, (h + 1) * CHUNK)
            m_ref[rows, columns] = (jnp.exp(exponent) + diagonal).astype(bf16)
            mt_ref[rows, columns] = (jnp.exp(turned) + diagonal).astype(bf16)
    stores = [
        pltpu.make_async_copy(source, target, sems.at[n])
        for n, (source, target) in enumerate(zip(table_refs, out_refs))
    ]
    for store in stores:
        store.start()
    for store in stores:
        store.wait()


def on_device(tokens, w_in, log_decay, grad_out):
    local_tokens = tokens[0]
    upstream = grad_out[0]
    token_count, hidden_width = local_tokens.shape
    head_count = log_decay.shape[1]
    inner_width = upstream.shape[1]
    head_size = inner_width // head_count
    state_size = (w_in.shape[1] - inner_width) // 2
    seq_count = lax.axis_size("seq")
    fsdp_count = lax.axis_size("fsdp")
    place = lax.axis_index("seq")
    row_place = lax.axis_index("fsdp")
    heads = head_count // seq_count
    width = heads * head_size
    length = token_count * seq_count
    shared = 2 * state_size
    chunks = length // CHUNK
    shape = jax.ShapeDtypeStruct
    params = pltpu.CompilerParams(vmem_limit_bytes=VMEM_LIMIT)
    scalar = [pl.BlockSpec(memory_space=pltpu.SMEM)]
    places = jnp.stack([place, row_place]).astype(jnp.int32)

    def cost(flops, moved):
        return pl.CostEstimate(flops=flops, bytes_accessed=moved, transcendentals=0)

    def columns(r):
        return lax.dynamic_slice_in_dim(w_in, lax.bitwise_xor(place, r) * width, width, 1)

    w_columns = lax.all_gather(
        jnp.concatenate([columns(0), w_in[:, inner_width:]], axis=1), "fsdp", axis=0, tiled=True
    )
    log_rates = lax.all_to_all(log_decay[0], "seq", 0, 1, tiled=True)

    table_shapes = (
        [shape((length, width), bf16)] * 4
        + [shape((chunks, 1, width), f32)]
        + [shape((length, heads * CHUNK), bf16)] * 2
    )
    in_hbm = [pl.BlockSpec(memory_space=pltpu.HBM)]
    scratch = lambda *buffers: [pltpu.VMEM(a.shape, a.dtype) for a in buffers]
    make_tables = pl.pallas_call(
        tables_kernel,
        grid=(1,),
        out_shape=table_shapes,
        in_specs=[resident(log_rates)],
        out_specs=in_hbm * 7,
        scratch_shapes=scratch(*table_shapes) + [pltpu.SemaphoreType.DMA((7,))],
        compiler_params=params,
        cost_estimate=cost(0, 120 * length * width),
    )
    neighbours = [r for r in range(2, seq_count, 2) if r & (r - 1) == 0]
    others = [r for r in range(2, seq_count, 2) if r & (r - 1)]
    first_part = width // 2
    rest = [columns(r) for r in others] + [columns(r)[:, :first_part] for r in neighbours]

    blocks = upstream.reshape(token_count, seq_count, width).transpose(1, 0, 2)
    rest = jnp.concatenate(rest, axis=1)
    arrays, sources, (tables, upstream, rest, places) = gather_rows(
        local_tokens,
        "seq",
        (log_rates, blocks, rest, places),
        lambda log_rates, *others: (make_tables(log_rates), *others),
    )
    to_end, from_start, enter, leave, chunk_decay, decays, turned = tables

    count = len(sources)
    slots = min(count, 16)
    group = min(slots, 4)
    held = shape((slots, token_count // 2, hidden_width), bf16)
    by_position = shape((length, width), bf16)
    by_state = shape((chunks * state_size, width), bf16)
    state_rows = shape((length, state_size), bf16)
    mean = shape((width, width), bf16)
    carry = shape((state_size, width), f32)

    w_even = lax.all_gather(rest, "fsdp", axis=0, tiled=True)
    upstream = after(upstream, w_columns)

    *arrays, w_columns = lax.optimization_barrier((*arrays, w_columns))
    g = lax.all_to_all(upstream, "seq", 0, 0).reshape(length, width)
    operands = (w_columns, decays, to_end, from_start, enter, leave, chunk_decay)
    kept = [by_position, state_rows, state_rows, by_position, by_position, by_state, by_state]
    forward = pl.pallas_call(
        functools.partial(
            forward_kernel, sources, len(arrays), slots, group, heads, head_size
        ),
        out_shape=kept,
        in_specs=scalar + in_hbm * (len(arrays) + 7),
        out_specs=in_hbm * 7,
        scratch_shapes=scratch(*operands, *kept, held, mean, carry, shape((length, width), f32))
        + [
            pltpu.SemaphoreType.DMA((slots,)),
            pltpu.SemaphoreType.DMA((7,)),
            pltpu.SemaphoreType.DMA((7,)),
            pltpu.SemaphoreType.DMA((8,)),
        ],
        compiler_params=params,
        cost_estimate=cost(
            4 * length * hidden_width * (width + shared) + 160 * length * width * CHUNK,
            4 * length * hidden_width,
        ),
    )(places, *arrays, *operands)
    w_partner = permute_xor(w_columns, "seq", 1)
    forward, g, w_partner = lax.optimization_barrier((forward, g, w_partner))
    x, b, c, z, inverse, states_in, states_next = forward

    mixed_blocks = lax.all_to_all(z.reshape(seq_count, token_count, width), "seq", 0, 0)
    operands = (
        g, z, inverse, c, enter, chunk_decay,
        x, b, decays, turned, to_end, from_start, leave, states_in, states_next,
    )
    grads = [by_position, shape((shared, length), bf16)]
    backward = pl.pallas_call(
        functools.partial(backward_kernel, heads, head_size),
        out_shape=grads,
        in_specs=in_hbm * 15,
        out_specs=in_hbm * 2,
        scratch_shapes=scratch(*operands, *grads, by_position, by_state, mean, carry)
        + [pltpu.SemaphoreType.DMA((15,)), pltpu.SemaphoreType.DMA((2,))],
        compiler_params=params,
        cost_estimate=cost(240 * length * width * CHUNK, 40 * length * width),
    )(*operands)
    backward, mixed_blocks = lax.optimization_barrier((backward, mixed_blocks))
    dx, shared_partial = backward

    rows_each = hidden_width // (seq_count * fsdp_count)
    extra = 16

    def weight_columns(grad, columns, is_turned):
        total = shape((columns, hidden_width), f32)
        result = shape((hidden_width, columns), bf16)
        if not is_turned:
            parts = [shape((fsdp_count, seq_count, rows_each, columns), bf16)]
        else:
            parts = [shape((seq_count, extra, columns * rows_each // extra), bf16)] * fsdp_count
        return pl.pallas_call(
            functools.partial(weight_kernel, sources, len(arrays), slots, group, fsdp_count, is_turned),
            out_shape=parts,
            grid=(1,),
            in_specs=scalar + in_hbm * len(arrays) + [resident(grad)],
            out_specs=[resident(a) for a in parts],
            scratch_shapes=scratch(held, total, result) + [pltpu.SemaphoreType.DMA((slots,))],
            compiler_params=params,
            cost_estimate=cost(4 * length * hidden_width * columns, 4 * length * hidden_width),
        )(places, *arrays, grad)

    part = shared // seq_count
    arrived = lax.all_to_all(shared_partial.reshape(seq_count, part, length), "seq", 0, 0)
    (head_weights,) = weight_columns(dx, width, False)
    head_sums = lax.psum_scatter(
        head_weights.reshape(hidden_width, width), "fsdp", scatter_dimension=0, tiled=True
    ).reshape(seq_count, rows_each, width)
    second_part = after(w_columns, head_weights)[:, first_part:width]
    w_across = [permute_xor(second_part, "seq", r) for r in neighbours]
    arrived, second_part, w_even = lax.optimization_barrier((arrived, second_part, w_even))
    sums = [
        shape((part, length), bf16),
        shape((seq_count, token_count + max(part, 16), max(width, token_count)), bf16),
    ]
    shared_columns, packed = pl.pallas_call(
        sum_kernel,
        grid=(1,),
        out_shape=sums,
        in_specs=[resident(arrived), resident(dx)],
        out_specs=[resident(a) for a in sums],
        compiler_params=params,
    )(arrived, dx)

    grad_blocks = lax.all_to_all(packed, "seq", 0, 0)
    shared_weights = weight_columns(shared_columns, part, True)
    shared_arrived = exchange_xor(shared_weights, "fsdp")
    mixed_shape = shape((1, token_count, inner_width), bf16)
    mixer_out = pl.pallas_call(
        spread_kernel,
        grid=(1,),
        out_shape=mixed_shape,
        in_specs=[resident(mixed_blocks)],
        out_specs=resident(mixed_shape),
        compiler_params=params,
    )(after(mixed_blocks, shared_columns))
    w_even = [w_even, *(after(a, shared_weights[0]) for a in w_across)]
    w_odd = [permute_xor(a, "seq", 1) for a in w_even]
    shared_arrived, mixer_out, w_odd, head_sums = lax.optimization_barrier(
        (shared_arrived, mixer_out, w_odd, head_sums)
    )

    grad_tokens_shape = shape((1, token_count, hidden_width), bf16)
    layout = [[(r, 0, width) for r in others] + [(r, 0, first_part) for r in neighbours]]
    layout += [[(r, first_part, width - first_part)] for r in neighbours]
    odd_layout = [[(r + 1, start, extent) for r, start, extent in parts] for parts in layout]
    layout = [[(0, 0, width)], [(1, 0, width)]] + layout + odd_layout
    lhs_shapes = [
        shape((token_count, sum(part[2] for part in parts) + (shared if n == 0 else 0)), bf16)
        for n, parts in enumerate(layout)
    ]
    w_blocks = [w_columns, w_partner, *w_even, *w_odd]
    tokens_cost = cost(
        4 * token_count * hidden_width * (inner_width + shared),
        4 * hidden_width * (inner_width + shared),
    )
    if all(extent % 128 == 0 for parts in layout for _, _, extent in parts):
        steps = 4
        joined = shape((steps, hidden_width // steps, inner_width + shared), bf16)
        grad_tokens = pl.pallas_call(
            functools.partial(joined_tokens_kernel, layout, steps),
            grid=(1,),
            out_shape=grad_tokens_shape,
            in_specs=scalar + [resident(grad_blocks)] + in_hbm * len(w_blocks),
            out_specs=resident(grad_tokens_shape),
            scratch_shapes=scratch(joined, shape((token_count, inner_width + shared), bf16))
            + [pltpu.SemaphoreType.DMA((steps * len(w_blocks),))],
            compiler_params=params,
            cost_estimate=tokens_cost,
        )(places, grad_blocks, *w_blocks)
    else:
        steps = 2
        rows = hidden_width // steps
        by_rows = lambda a: pl.BlockSpec((rows, a.shape[1]), lambda k: (k, 0))
        grad_tokens = pl.pallas_call(
            functools.partial(tokens_kernel, layout),
            grid=(steps,),
            out_shape=grad_tokens_shape,
            in_specs=scalar + [resident(grad_blocks)] + [by_rows(a) for a in w_blocks],
            out_specs=pl.BlockSpec((1, token_count, rows), lambda k: (0, 0, k)),
            scratch_shapes=scratch(*lhs_shapes),
            compiler_params=params,
            cost_estimate=tokens_cost,
        )(places, grad_blocks, *w_blocks)
    packed = shape((seq_count, rows_each + extra, width), bf16)
    packed_sums = pl.pallas_call(
        add_kernel,
        grid=(1,),
        out_shape=packed,
        in_specs=[resident(a) for a in [head_sums, *shared_arrived]],
        out_specs=resident(packed),
        compiler_params=params,
    )(head_sums, *shared_arrived)
    owned = lax.all_to_all(after(packed_sums, grad_blocks), "seq", 0, 0)
    finished = shape((rows_each, inner_width + shared), f32)
    grad_weights = pl.pallas_call(
        finish_kernel,
        grid=(1,),
        out_shape=finished,
        in_specs=[resident(owned)],
        out_specs=resident(finished),
        compiler_params=params,
    )(owned)
    return mixer_out, grad_tokens, grad_weights


def solution(mesh):
    return jax.shard_map(
        on_device,
        mesh=mesh,
        in_specs=(
            P("fsdp", "seq", None),
            P("fsdp", None),
            P("fsdp", None, "seq"),
            P("fsdp", "seq", None),
        ),
        out_specs=(P("fsdp", "seq", None), P("fsdp", "seq", None), P(("seq", "fsdp"), None)),
        check_vma=False,
    )
```

```python
import functools

import jax
import jax.numpy as jnp
from jax import lax
from jax.experimental import pallas as pl
from jax.experimental.pallas import tpu as pltpu
from jax.sharding import PartitionSpec as P

CHUNK = 128
EPSILON = 1e-05
VMEM_LIMIT = 60 * 1024 * 1024

f32 = jnp.float32
bf16 = jnp.bfloat16


def dot_nn(a, b):
    return lax.dot_general(a, b, (((1,), (0,)), ((), ())), preferred_element_type=f32)


def dot_nt(a, b):
    return lax.dot_general(a, b, (((1,), (1,)), ((), ())), preferred_element_type=f32)


def dot_tn(a, b):
    return lax.dot_general(a, b, (((0,), (0,)), ((), ())), preferred_element_type=f32)


def by_head(rows, heads, head_size):
    if heads == 1:
        return rows
    lane = lax.broadcasted_iota(jnp.int32, rows.shape, 1)
    parts = []
    for h in range(heads):
        inside = (lane >= h * head_size) & (lane < (h + 1) * head_size)
        parts.append(jnp.where(inside, rows, jnp.zeros_like(rows)))
    return jnp.concatenate(parts, axis=0)


def decayed(affinity, decays, heads):
    tiled = jnp.concatenate([affinity] * heads, axis=1) if heads > 1 else affinity
    return (tiled * decays.astype(f32)).astype(bf16)


def spans(k, state_size):
    rows = pl.ds(pl.multiple_of(k * CHUNK, CHUNK), CHUNK)
    return rows, pl.ds(pl.multiple_of(k * state_size, state_size), state_size)


def fill_mean(mean_ref, heads, head_size):
    row = lax.broadcasted_iota(jnp.int32, mean_ref.shape, 0)
    col = lax.broadcasted_iota(jnp.int32, mean_ref.shape, 1)
    same = jnp.zeros(mean_ref.shape, jnp.bool_)
    for h in range(heads):
        low, high = h * head_size, (h + 1) * head_size
        same |= (row >= low) & (row < high) & (col >= low) & (col < high)
    mean_ref[...] = jnp.where(same, 1.0 / head_size, 0.0).astype(bf16)


def forward_kernel(sources, arrays, slots, group, heads, head_size, place_ref, *refs):
    array_refs, refs = refs[:arrays], refs[arrays:]
    in_hbm, out_hbm, refs = refs[:7], refs[7:14], refs[14:]
    in_refs, out_refs, refs = refs[:7], refs[7:14], refs[14:]
    held, mean_ref, carry, y_ref, sems, loads, stores, y_sems = refs
    w_ref, m_ref, te_ref, fs_ref, en_ref, lv_ref, dt_ref = in_refs
    x_ref, b_ref, c_ref, z_ref, rs_ref, sf_ref, rn_ref = out_refs
    pieces = len(sources)
    rows_each = held.shape[1]
    width, state_size = x_ref.shape[1], b_ref.shape[1]
    chunks = dt_ref.shape[0]

    def fetch(i):
        array, start = sources[i]
        source = array_refs[array].at[pl.ds(start, rows_each)]
        return pltpu.make_async_copy(source, held.at[i % slots], sems.at[i % slots])

    in_loads = [
        pltpu.make_async_copy(source, target, loads.at[n])
        for n, (source, target) in enumerate(zip(in_hbm, in_refs))
    ]
    out_stores = [
        pltpu.make_async_copy(source, target, stores.at[n])
        for n, (source, target) in enumerate(zip(out_refs, out_hbm))
    ]
    in_loads[0].start()
    for i in range(slots):
        fetch(i).start()
    for load in in_loads[1:]:
        load.start()
    fill_mean(mean_ref, heads, head_size)

    in_loads[0].wait()
    for first in range(0, pieces, group):
        for i in range(first, first + group):
            fetch(i).wait()
        slot = first % slots
        block = held[slot : slot + group].reshape(group * rows_each, held.shape[2])
        result = dot_nn(block, w_ref[...]).astype(bf16)
        for i in range(first, first + group):
            if i + slots < pieces:
                fetch(i + slots).start()
            offset = (2 * lax.bitwise_xor(place_ref[0], i // 2) + i % 2) * rows_each
            target = pl.ds(pl.multiple_of(offset, rows_each), rows_each)
            part = slice((i - first) * rows_each, (i - first + 1) * rows_each)
            x_ref[target, :] = result[part, :width]
            b_ref[target, :] = result[part, width : width + state_size]
            c_ref[target, :] = result[part, width + state_size :]
    for store in out_stores[:3]:
        store.start()
    for load in in_loads[1:]:
        load.wait()

    carry[...] = jnp.zeros_like(carry)

    def reverse_states(i, _):
        k = chunks - 1 - i
        rows, state = spans(k, state_size)
        rn_ref[state, :] = carry[...].astype(bf16)
        term = dot_tn(b_ref[rows, :], x_ref[rows, :] * fs_ref[rows, :])
        carry[...] = dt_ref[k] * carry[...] + term
        return 0

    lax.fori_loop(0, chunks, reverse_states, 0, unroll=16)
    out_stores[6].start()
    carry[...] = jnp.zeros_like(carry)

    def outputs(k, _):
        rows, state = spans(k, state_size)
        x, b, c = x_ref[rows, :], b_ref[rows, :], c_ref[rows, :]
        state_in = carry[...].astype(bf16)
        sf_ref[state, :] = state_in
        weights = decayed(dot_nt(c, b), m_ref[rows, :], heads)
        y = dot_nn(weights, by_head(x, heads, head_size))
        y = y + en_ref[rows, :].astype(f32) * dot_nn(c, state_in)
        y = y + lv_ref[rows, :].astype(f32) * dot_nn(c, rn_ref[state, :])
        y_ref[rows, :] = y
        carry[...] = dt_ref[k] * carry[...] + dot_tn(b, x * te_ref[rows, :])
        return 0

    lax.fori_loop(0, chunks, outputs, 0, unroll=16)
    out_stores[5].start()
    block_stores = []
    block = y_ref.shape[0] // (y_sems.shape[0] // 2)
    for n in range(y_sems.shape[0] // 2):
        rows = pl.ds(n * block, block)
        y = y_ref[rows, :]
        mean_square = dot_nn((y * y).astype(bf16), mean_ref[...])
        inverse = lax.rsqrt(mean_square + EPSILON)
        z_ref[rows, :] = (y * inverse).astype(bf16)
        rs_ref[rows, :] = inverse.astype(bf16)
        for m in (3, 4):
            source, target = out_refs[m].at[rows], out_hbm[m].at[rows]
            store = pltpu.make_async_copy(source, target, y_sems.at[2 * n + m - 3])
            store.start()
            block_stores.append(store)
    for store in out_stores[:3] + out_stores[5:] + block_stores:
        store.wait()


def backward_kernel(heads, head_size, *refs):
    in_hbm, out_hbm, refs = refs[:15], refs[15:17], refs[17:]
    in_refs, (dx_ref, shared_ref), refs = refs[:15], refs[15:17], refs[17:]
    dy_ref, ge_ref, mean_ref, carry, loads, stores = refs
    g_ref, z_ref, rs_ref, c_ref, en_ref, dt_ref = in_refs[:6]
    x_ref, b_ref, m_ref, mt_ref, te_ref, fs_ref, lv_ref, sf_ref, rn_ref = in_refs[6:15]
    state_size = b_ref.shape[1]
    chunks = dt_ref.shape[0]
    in_loads = [
        pltpu.make_async_copy(source, target, loads.at[n])
        for n, (source, target) in enumerate(zip(in_hbm, in_refs))
    ]
    for load in in_loads:
        load.start()
    fill_mean(mean_ref, heads, head_size)
    carry[...] = jnp.zeros_like(carry)
    for load in in_loads[:6]:
        load.wait()

    def end_adjoints(i, _):
        k = chunks - 1 - i
        rows, state = spans(k, state_size)
        g, z = g_ref[rows, :].astype(f32), z_ref[rows, :].astype(f32)
        mean_gz = dot_nn((g * z).astype(bf16), mean_ref[...])
        dy = ((g - z * mean_gz) * rs_ref[rows, :].astype(f32)).astype(bf16)
        dy_ref[rows, :] = dy
        ge_ref[state, :] = carry[...].astype(bf16)
        carry[...] = dt_ref[k] * carry[...] + dot_tn(c_ref[rows, :], dy * en_ref[rows, :])
        return 0

    lax.fori_loop(0, chunks, end_adjoints, 0, unroll=16)
    carry[...] = jnp.zeros_like(carry)
    for load in in_loads[6:]:
        load.wait()

    def gradients(k, _):
        rows, state = spans(k, state_size)
        x, b, c, dy = x_ref[rows, :], b_ref[rows, :], c_ref[rows, :], dy_ref[rows, :]
        te, fs, en, lv = te_ref[rows, :], fs_ref[rows, :], en_ref[rows, :], lv_ref[rows, :]
        ge, gs = ge_ref[state, :], carry[...].astype(bf16)
        grad_weights = dot_nt(dy, by_head(x, heads, head_size)) * m_ref[rows, :].astype(f32)
        da = grad_weights[:, :CHUNK]
        for h in range(1, heads):
            da = da + grad_weights[:, h * CHUNK : (h + 1) * CHUNK]
        da = da.astype(bf16)
        turned = decayed(dot_nt(b, c), mt_ref[rows, :], heads)
        dx = dot_nn(turned, by_head(dy, heads, head_size))
        dx = dx + te.astype(f32) * dot_nn(b, ge)
        dx = dx + fs.astype(f32) * dot_nn(b, gs)
        dx_ref[rows, :] = dx.astype(bf16)
        dy_lv = dy * lv
        dc = dot_nn(da, b) + dot_nt(dy * en, sf_ref[state, :]) + dot_nt(dy_lv, rn_ref[state, :])
        db = dot_tn(da, c) + dot_nt(x * te, ge) + dot_nt(x * fs, gs)
        shared_ref[:state_size, rows] = db.T.astype(bf16)
        shared_ref[state_size:, rows] = dc.T.astype(bf16)
        carry[...] = dt_ref[k] * carry[...] + dot_tn(c, dy_lv)
        return 0

    lax.fori_loop(0, chunks, gradients, 0, unroll=16)
    out_stores = [
        pltpu.make_async_copy(source, target, stores.at[n])
        for n, (source, target) in enumerate(zip((dx_ref, shared_ref), out_hbm))
    ]
    for store in out_stores:
        store.start()
    for store in out_stores:
        store.wait()


def sum_kernel(parts_ref, dx_ref, sum_ref, packed_ref):
    total = parts_ref[0].astype(f32)
    for n in range(1, parts_ref.shape[0]):
        total = total + parts_ref[n].astype(f32)
    total = total.astype(bf16)
    sum_ref[...] = total
    count = packed_ref.shape[0]
    part, tokens = total.shape[0], total.shape[1] // count
    if packed_ref.shape[1] > tokens + part or packed_ref.shape[2] > dx_ref.shape[1]:
        packed_ref[...] = jnp.zeros_like(packed_ref)
    for n in range(count):
        block = slice(n * tokens, (n + 1) * tokens)
        packed_ref[n, :tokens, : dx_ref.shape[1]] = dx_ref[block, :]
        packed_ref[n, tokens : tokens + part, :tokens] = total[:, block]


def tokens_kernel(layout, place_ref, packed_ref, *refs):
    arrays = len(layout)
    column_refs, out_ref, lhs_refs = refs[:arrays], refs[arrays], refs[arrays + 1 :]
    count = packed_ref.shape[0]
    tokens = out_ref.shape[1]

    @pl.when(pl.program_id(0) == 0)
    def _():
        for lhs_ref, parts in zip(lhs_refs, layout):
            column = 0
            for r, start, extent in parts:
                source = lax.bitwise_xor(place_ref[0], r)
                block = packed_ref[source, :tokens, start : start + extent]
                lhs_ref[:, column : column + extent] = block
                column += extent
        width = layout[0][0][2]
        rows = (lhs_refs[0].shape[1] - width) // count
        turned = [packed_ref[n, tokens : tokens + rows, :tokens] for n in range(count)]
        lhs_refs[0][:, width:] = jnp.concatenate(turned, axis=0).T

    result = dot_nt(lhs_refs[0][...], column_refs[0][...])
    for lhs_ref, column_ref in zip(lhs_refs[1:], column_refs[1:]):
        result = result + dot_nt(lhs_ref[...], column_ref[:, : lhs_ref.shape[1]])
    out_ref[0] = result.astype(bf16)


def joined_tokens_kernel(layout, steps, place_ref, packed_ref, *refs):
    arrays = len(layout)
    column_refs, out_ref, joined_ref, lhs_ref, sems = refs[:arrays], *refs[arrays:]
    count = packed_ref.shape[0]
    tokens = out_ref.shape[1]
    rows = joined_ref.shape[1]
    width = layout[0][0][2]
    part = (joined_ref.shape[2] - count * width) // count
    loads = []
    for step in range(steps):
        column = 0
        for n, parts in enumerate(layout):
            extent = sum(p[2] for p in parts) + (count * part if n == 0 else 0)
            source = column_refs[n].at[pl.ds(step * rows, rows), pl.ds(0, extent)]
            target = joined_ref.at[step, :, pl.ds(column, extent)]
            loads.append(pltpu.make_async_copy(source, target, sems.at[step * arrays + n]))
            loads[-1].start()
            column += extent

    column = 0
    for n, parts in enumerate(layout):
        for r, start, extent in parts:
            source = lax.bitwise_xor(place_ref[0], r)
            block = packed_ref[source, :tokens, start : start + extent]
            lhs_ref[:, column : column + extent] = block
            column += extent
        if n == 0:
            turned = [packed_ref[m, tokens : tokens + part, :tokens] for m in range(count)]
            lhs_ref[:, column : column + count * part] = jnp.concatenate(turned, axis=0).T
            column += count * part
    for step in range(steps):
        for load in loads[step * arrays : (step + 1) * arrays]:
            load.wait()
        result = dot_nt(lhs_ref[...], joined_ref[step])
        out_ref[0, :, step * rows : (step + 1) * rows] = result.astype(bf16)


def spread_kernel(blocks_ref, out_ref):
    width = blocks_ref.shape[2]
    for n in range(blocks_ref.shape[0]):
        out_ref[0, :, n * width : (n + 1) * width] = blocks_ref[n]


def add_kernel(*refs):
    head_ref, shared_refs, out_ref = refs[0], refs[1:-1], refs[-1]
    rows = head_ref.shape[1]
    out_ref[:, :rows, :] = head_ref[...]
    total = shared_refs[0][...].astype(f32)
    for ref in shared_refs[1:]:
        total = total + ref[...].astype(f32)
    total = total.astype(bf16)
    if out_ref.shape[2] > total.shape[2]:
        out_ref[:, rows:, :] = jnp.zeros_like(out_ref[:, rows:, :])
    out_ref[:, rows:, : total.shape[2]] = total


def weight_kernel(sources, arrays, slots, group, parts, is_turned, places_ref, *refs):
    array_refs, grad_ref = refs[:arrays], refs[arrays]
    out_refs, (held, total, result, sems) = refs[arrays + 1 : -4], refs[-4:]
    pieces = len(sources)
    rows = held.shape[1]
    hidden = held.shape[2]

    def fetch(i):
        array, start = sources[i]
        source = array_refs[array].at[pl.ds(start, rows)]
        return pltpu.make_async_copy(source, held.at[i % slots], sems.at[i % slots])

    for i in range(slots):
        fetch(i).start()
    for first in range(0, pieces, group):
        turned = []
        for i in range(first, first + group):
            offset = (2 * lax.bitwise_xor(places_ref[0], i // 2) + i % 2) * rows
            target = pl.ds(pl.multiple_of(offset, rows), rows)
            turned.append(grad_ref[:, target] if is_turned else grad_ref[target, :].T)
        for i in range(first, first + group):
            fetch(i).wait()
        slot = first % slots
        block = held[slot : slot + group].reshape(group * rows, hidden)
        term = dot_nn(jnp.concatenate(turned, axis=1), block)
        if first > 0:
            term = term + total[...]
        if first + group < pieces:
            total[...] = term
        else:
            result[...] = term.T.astype(bf16)
        for i in range(first, first + group):
            if i + slots < pieces:
                fetch(i + slots).start()
    columns = result.shape[1]
    each = out_refs[0].shape[-2] * out_refs[0].shape[-1] // columns
    count = hidden // (parts * each)
    for k in range(parts):
        for j in range(count):
            if len(out_refs) == 1:
                out_refs[0][k, j] = result[(j * parts + k) * each : (j * parts + k + 1) * each, :]
                continue
            mine = (j * parts + lax.bitwise_xor(places_ref[1], k)) * each
            rows = out_refs[k].shape[1]
            for q in range(each // rows):
                source = pl.ds(pl.multiple_of(mine + q * rows, rows), rows)
                out_refs[k][j, :, q * columns : (q + 1) * columns] = result[source, :]


def finish_kernel(packed_ref, out_ref):
    count, _, width = packed_ref.shape
    rows = out_ref.shape[0]
    extra = packed_ref.shape[1] - rows
    part = (out_ref.shape[1] - count * width) // count
    for n in range(count):
        out_ref[:, n * width : (n + 1) * width] = packed_ref[n, :rows].astype(f32)
        start = count * width + n * part
        for q in range(rows // extra):
            block = packed_ref[n, rows:, q * part : (q + 1) * part]
            out_ref[q * extra : (q + 1) * extra, start : start + part] = block.astype(f32)


def resident(array):
    return pl.BlockSpec(array.shape, lambda k: (0,) * len(array.shape))


def after(value, *earlier):
    return lax.optimization_barrier((value,) + earlier)[0]


def permute_xor(a, axis, mask):
    count = lax.axis_size(axis)
    return lax.ppermute(a, axis, [(i, i ^ mask) for i in range(count)])


def gather_rows(rows, axis, beside, work):
    count = lax.axis_size(axis)
    bits = count.bit_length() - 1
    half = rows.shape[0] // 2
    if bits == 3:
        held = {r: permute_xor(rows, axis, r) for r in (2, 4, 1)}
        held, beside = lax.optimization_barrier((held, beside))
        held[3], held[5] = permute_xor(held[2], axis, 1), permute_xor(held[4], axis, 1)
        corner = [
            permute_xor(held[2][:half], axis, 4),
            permute_xor(held[4][half:], axis, 2),
        ]
        held, corner, done = lax.optimization_barrier((held, corner, work(*beside)))
        held = {r: [a] for r, a in held.items()}
        held[0], held[6] = [rows], corner
        held[7] = [permute_xor(a, axis, 1) for a in corner]
    else:
        done = work(*beside)
        upper = list(range(1, bits))
        orders = (upper + [0], upper[1:] + upper[:1] + [0])
        both = ({0: rows[:half]}, {0: rows[half:]})
        for step in range(bits):
            for part in range(2):
                mask = 1 << orders[part][step]
                for r in list(both[part]):
                    both[part][r ^ mask] = permute_xor(both[part][r], axis, mask)
        held = {r: [both[0][r], both[1][r]] for r in range(count)}
    arrays, sources = [], []
    for r in range(count):
        for part in range(2):
            whole_block = len(held[r]) == 1
            if part == 0 or not whole_block:
                arrays.append(held[r][part])
            sources.append((len(arrays) - 1, half * part if whole_block else 0))
    return arrays, tuple(sources), done


def exchange_xor(pieces, axis):
    return [pieces[0]] + [permute_xor(p, axis, r) for r, p in enumerate(pieces) if r > 0]


def tables_kernel(log_ref, *refs):
    out_refs, table_refs, sems = refs[:7], refs[7:14], refs[14]
    te_ref, fs_ref, en_ref, lv_ref, dt_ref, m_ref, mt_ref = table_refs
    heads = log_ref.shape[0]
    chunks = dt_ref.shape[0]
    head_size = te_ref.shape[1] // heads
    row = lax.broadcasted_iota(jnp.int32, (CHUNK, CHUNK), 0)
    col = lax.broadcasted_iota(jnp.int32, (CHUNK, CHUNK), 1)
    logs = jnp.concatenate(
        [log_ref[:, k * CHUNK : (k + 1) * CHUNK] for k in range(chunks)], axis=0
    )
    cumulative = lax.dot_general(
        logs, (row <= col).astype(f32), (((1,), (0,)), ((), ())),
        precision=lax.Precision.HIGHEST, preferred_element_type=f32,
    )
    exclusive = cumulative - logs
    cum_t, exc_t = cumulative.T, exclusive.T
    total = cum_t[CHUNK - 1 : CHUNK, :]
    spreads = (
        (te_ref, jnp.exp(total - cum_t)),
        (fs_ref, jnp.exp(exc_t)),
        (en_ref, jnp.exp(cum_t)),
        (lv_ref, jnp.exp(total - exc_t)),
    )
    chunk_decay = jnp.exp(total)
    diagonal = (row == col).astype(f32)
    for k in range(chunks):
        rows = slice(k * CHUNK, (k + 1) * CHUNK)
        picked = range(k * heads, (k + 1) * heads)
        for ref, source in spreads:
            ref[rows, :] = jnp.concatenate(
                [jnp.broadcast_to(source[:, n : n + 1], (CHUNK, head_size)) for n in picked], axis=1
            ).astype(bf16)
        dt_ref[k] = jnp.concatenate(
            [jnp.broadcast_to(chunk_decay[:, n : n + 1], (1, head_size)) for n in picked], axis=1
        )
        for h, n in enumerate(picked):
            cum_col, exc_col = cum_t[:, n : n + 1], exc_t[:, n : n + 1]
            cum_row, exc_row = cumulative[n : n + 1, :], exclusive[n : n + 1, :]
            below, above = cum_col - cum_row, exc_row - exc_col
            exponent = jnp.where(row > col, below, jnp.where(row < col, above, 0.0))
            turned = jnp.where(row < col, -below, jnp.where(row > col, -above, 0.0))
            columns = slice(h * CHUNK, (h + 1) * CHUNK)
            m_ref[rows, columns] = (jnp.exp(exponent) + diagonal).astype(bf16)
            mt_ref[rows, columns] = (jnp.exp(turned) + diagonal).astype(bf16)
    stores = [
        pltpu.make_async_copy(source, target, sems.at[n])
        for n, (source, target) in enumerate(zip(table_refs, out_refs))
    ]
    for store in stores:
        store.start()
    for store in stores:
        store.wait()


def on_device(tokens, w_in, log_decay, grad_out):
    local_tokens = tokens[0]
    upstream = grad_out[0]
    token_count, hidden_width = local_tokens.shape
    head_count = log_decay.shape[1]
    inner_width = upstream.shape[1]
    head_size = inner_width // head_count
    state_size = (w_in.shape[1] - inner_width) // 2
    seq_count = lax.axis_size("seq")
    fsdp_count = lax.axis_size("fsdp")
    place = lax.axis_index("seq")
    row_place = lax.axis_index("fsdp")
    heads = head_count // seq_count
    width = heads * head_size
    length = token_count * seq_count
    shared = 2 * state_size
    chunks = length // CHUNK
    shape = jax.ShapeDtypeStruct
    params = pltpu.CompilerParams(vmem_limit_bytes=VMEM_LIMIT)
    scalar = [pl.BlockSpec(memory_space=pltpu.SMEM)]
    places = jnp.stack([place, row_place]).astype(jnp.int32)

    def cost(flops, moved):
        return pl.CostEstimate(flops=flops, bytes_accessed=moved, transcendentals=0)

    def columns(r):
        return lax.dynamic_slice_in_dim(w_in, lax.bitwise_xor(place, r) * width, width, 1)

    w_columns = lax.all_gather(
        jnp.concatenate([columns(0), w_in[:, inner_width:]], axis=1), "fsdp", axis=0, tiled=True
    )
    log_rates = lax.all_to_all(log_decay[0], "seq", 0, 1, tiled=True)

    table_shapes = (
        [shape((length, width), bf16)] * 4
        + [shape((chunks, 1, width), f32)]
        + [shape((length, heads * CHUNK), bf16)] * 2
    )
    in_hbm = [pl.BlockSpec(memory_space=pltpu.HBM)]
    scratch = lambda *buffers: [pltpu.VMEM(a.shape, a.dtype) for a in buffers]
    make_tables = pl.pallas_call(
        tables_kernel,
        grid=(1,),
        out_shape=table_shapes,
        in_specs=[resident(log_rates)],
        out_specs=in_hbm * 7,
        scratch_shapes=scratch(*table_shapes) + [pltpu.SemaphoreType.DMA((7,))],
        compiler_params=params,
        cost_estimate=cost(0, 120 * length * width),
    )
    neighbours = [r for r in range(2, seq_count, 2) if r & (r - 1) == 0]
    others = [r for r in range(2, seq_count, 2) if r & (r - 1)]
    first_part = width // 2
    rest = [columns(r) for r in others] + [columns(r)[:, :first_part] for r in neighbours]

    blocks = upstream.reshape(token_count, seq_count, width).transpose(1, 0, 2)
    rest = jnp.concatenate(rest, axis=1)
    arrays, sources, (tables, upstream, rest, places) = gather_rows(
        local_tokens,
        "seq",
        (log_rates, blocks, rest, places),
        lambda log_rates, *others: (make_tables(log_rates), *others),
    )
    to_end, from_start, enter, leave, chunk_decay, decays, turned = tables

    count = len(sources)
    slots = min(count, 16)
    group = min(slots, 4)
    held = shape((slots, token_count // 2, hidden_width), bf16)
    by_position = shape((length, width), bf16)
    by_state = shape((chunks * state_size, width), bf16)
    state_rows = shape((length, state_size), bf16)
    mean = shape((width, width), bf16)
    carry = shape((state_size, width), f32)

    w_even = lax.all_gather(rest, "fsdp", axis=0, tiled=True)
    upstream = after(upstream, w_columns)

    *arrays, w_columns = lax.optimization_barrier((*arrays, w_columns))
    g = lax.all_to_all(upstream, "seq", 0, 0).reshape(length, width)
    operands = (w_columns, decays, to_end, from_start, enter, leave, chunk_decay)
    kept = [by_position, state_rows, state_rows, by_position, by_position, by_state, by_state]
    forward = pl.pallas_call(
        functools.partial(
            forward_kernel, sources, len(arrays), slots, group, heads, head_size
        ),
        out_shape=kept,
        in_specs=scalar + in_hbm * (len(arrays) + 7),
        out_specs=in_hbm * 7,
        scratch_shapes=scratch(*operands, *kept, held, mean, carry, shape((length, width), f32))
        + [
            pltpu.SemaphoreType.DMA((slots,)),
            pltpu.SemaphoreType.DMA((7,)),
            pltpu.SemaphoreType.DMA((7,)),
            pltpu.SemaphoreType.DMA((8,)),
        ],
        compiler_params=params,
        cost_estimate=cost(
            4 * length * hidden_width * (width + shared) + 160 * length * width * CHUNK,
            4 * length * hidden_width,
        ),
    )(places, *arrays, *operands)
    w_partner = permute_xor(w_columns, "seq", 1)
    forward, g, w_partner = lax.optimization_barrier((forward, g, w_partner))
    x, b, c, z, inverse, states_in, states_next = forward

    mixed_blocks = lax.all_to_all(z.reshape(seq_count, token_count, width), "seq", 0, 0)
    operands = (
        g, z, inverse, c, enter, chunk_decay,
        x, b, decays, turned, to_end, from_start, leave, states_in, states_next,
    )
    grads = [by_position, shape((shared, length), bf16)]
    backward = pl.pallas_call(
        functools.partial(backward_kernel, heads, head_size),
        out_shape=grads,
        in_specs=in_hbm * 15,
        out_specs=in_hbm * 2,
        scratch_shapes=scratch(*operands, *grads, by_position, by_state, mean, carry)
        + [pltpu.SemaphoreType.DMA((15,)), pltpu.SemaphoreType.DMA((2,))],
        compiler_params=params,
        cost_estimate=cost(240 * length * width * CHUNK, 40 * length * width),
    )(*operands)
    backward, mixed_blocks = lax.optimization_barrier((backward, mixed_blocks))
    dx, shared_partial = backward

    rows_each = hidden_width // (seq_count * fsdp_count)
    extra = 16

    def weight_columns(grad, columns, is_turned):
        total = shape((columns, hidden_width), f32)
        result = shape((hidden_width, columns), bf16)
        if not is_turned:
            parts = [shape((fsdp_count, seq_count, rows_each, columns), bf16)]
        else:
            parts = [shape((seq_count, extra, columns * rows_each // extra), bf16)] * fsdp_count
        return pl.pallas_call(
            functools.partial(weight_kernel, sources, len(arrays), slots, min(slots, 2), fsdp_count, is_turned),
            out_shape=parts,
            grid=(1,),
            in_specs=scalar + in_hbm * len(arrays) + [resident(grad)],
            out_specs=[resident(a) for a in parts],
            scratch_shapes=scratch(held, total, result) + [pltpu.SemaphoreType.DMA((slots,))],
            compiler_params=params,
            cost_estimate=cost(4 * length * hidden_width * columns, 4 * length * hidden_width),
        )(places, *arrays, grad)

    part = shared // seq_count
    arrived = lax.all_to_all(shared_partial.reshape(seq_count, part, length), "seq", 0, 0)
    (head_weights,) = weight_columns(dx, width, False)
    head_sums = lax.psum_scatter(
        head_weights.reshape(hidden_width, width), "fsdp", scatter_dimension=0, tiled=True
    ).reshape(seq_count, rows_each, width)
    second_part = after(w_columns, head_weights)[:, first_part:width]
    w_across = [permute_xor(second_part, "seq", r) for r in neighbours]
    arrived, second_part, w_even = lax.optimization_barrier((arrived, second_part, w_even))
    sums = [
        shape((part, length), bf16),
        shape((seq_count, token_count + max(part, 16), max(width, token_count)), bf16),
    ]
    shared_columns, packed = pl.pallas_call(
        sum_kernel,
        grid=(1,),
        out_shape=sums,
        in_specs=[resident(arrived), resident(dx)],
        out_specs=[resident(a) for a in sums],
        compiler_params=params,
    )(arrived, dx)

    grad_blocks = lax.all_to_all(packed, "seq", 0, 0)
    shared_weights = weight_columns(shared_columns, part, True)
    shared_arrived = exchange_xor(shared_weights, "fsdp")
    mixed_shape = shape((1, token_count, inner_width), bf16)
    mixer_out = pl.pallas_call(
        spread_kernel,
        grid=(1,),
        out_shape=mixed_shape,
        in_specs=[resident(mixed_blocks)],
        out_specs=resident(mixed_shape),
        compiler_params=params,
    )(after(mixed_blocks, shared_columns))
    w_even = [w_even, *(after(a, shared_weights[0]) for a in w_across)]
    w_odd = [permute_xor(a, "seq", 1) for a in w_even]
    shared_arrived, mixer_out, w_odd, head_sums = lax.optimization_barrier(
        (shared_arrived, mixer_out, w_odd, head_sums)
    )

    grad_tokens_shape = shape((1, token_count, hidden_width), bf16)
    layout = [[(r, 0, width) for r in others] + [(r, 0, first_part) for r in neighbours]]
    layout += [[(r, first_part, width - first_part)] for r in neighbours]
    odd_layout = [[(r + 1, start, extent) for r, start, extent in parts] for parts in layout]
    layout = [[(0, 0, width)], [(1, 0, width)]] + layout + odd_layout
    lhs_shapes = [
        shape((token_count, sum(part[2] for part in parts) + (shared if n == 0 else 0)), bf16)
        for n, parts in enumerate(layout)
    ]
    w_blocks = [w_columns, w_partner, *w_even, *w_odd]
    tokens_cost = cost(
        4 * token_count * hidden_width * (inner_width + shared),
        4 * hidden_width * (inner_width + shared),
    )
    if all(extent % 128 == 0 for parts in layout for _, _, extent in parts):
        steps = 4
        joined = shape((steps, hidden_width // steps, inner_width + shared), bf16)
        grad_tokens = pl.pallas_call(
            functools.partial(joined_tokens_kernel, layout, steps),
            grid=(1,),
            out_shape=grad_tokens_shape,
            in_specs=scalar + [resident(grad_blocks)] + in_hbm * len(w_blocks),
            out_specs=resident(grad_tokens_shape),
            scratch_shapes=scratch(joined, shape((token_count, inner_width + shared), bf16))
            + [pltpu.SemaphoreType.DMA((steps * len(w_blocks),))],
            compiler_params=params,
            cost_estimate=tokens_cost,
        )(places, grad_blocks, *w_blocks)
    else:
        steps = 2
        rows = hidden_width // steps
        by_rows = lambda a: pl.BlockSpec((rows, a.shape[1]), lambda k: (k, 0))
        grad_tokens = pl.pallas_call(
            functools.partial(tokens_kernel, layout),
            grid=(steps,),
            out_shape=grad_tokens_shape,
            in_specs=scalar + [resident(grad_blocks)] + [by_rows(a) for a in w_blocks],
            out_specs=pl.BlockSpec((1, token_count, rows), lambda k: (0, 0, k)),
            scratch_shapes=scratch(*lhs_shapes),
            compiler_params=params,
            cost_estimate=tokens_cost,
        )(places, grad_blocks, *w_blocks)
    packed = shape((seq_count, rows_each + extra, width), bf16)
    packed_sums = pl.pallas_call(
        add_kernel,
        grid=(1,),
        out_shape=packed,
        in_specs=[resident(a) for a in [head_sums, *shared_arrived]],
        out_specs=resident(packed),
        compiler_params=params,
    )(head_sums, *shared_arrived)
    owned = lax.all_to_all(after(packed_sums, grad_blocks), "seq", 0, 0)
    finished = shape((rows_each, inner_width + shared), f32)
    grad_weights = pl.pallas_call(
        finish_kernel,
        grid=(1,),
        out_shape=finished,
        in_specs=[resident(owned)],
        out_specs=resident(finished),
        compiler_params=params,
    )(owned)
    return mixer_out, grad_tokens, grad_weights


def solution(mesh):
    return jax.shard_map(
        on_device,
        mesh=mesh,
        in_specs=(
            P("fsdp", "seq", None),
            P("fsdp", None),
            P("fsdp", None, "seq"),
            P("fsdp", "seq", None),
        ),
        out_specs=(P("fsdp", "seq", None), P("fsdp", "seq", None), P(("seq", "fsdp"), None)),
        check_vma=False,
    )
```

```python
import functools

import jax
import jax.numpy as jnp
from jax import lax
from jax.experimental import pallas as pl
from jax.experimental.pallas import tpu as pltpu
from jax.sharding import PartitionSpec as P

CHUNK = 128
EPSILON = 1e-05
VMEM_LIMIT = 60 * 1024 * 1024

f32 = jnp.float32
bf16 = jnp.bfloat16


def dot_nn(a, b):
    return lax.dot_general(a, b, (((1,), (0,)), ((), ())), preferred_element_type=f32)


def dot_nt(a, b):
    return lax.dot_general(a, b, (((1,), (1,)), ((), ())), preferred_element_type=f32)


def dot_tn(a, b):
    return lax.dot_general(a, b, (((0,), (0,)), ((), ())), preferred_element_type=f32)


def by_head(rows, heads, head_size):
    if heads == 1:
        return rows
    lane = lax.broadcasted_iota(jnp.int32, rows.shape, 1)
    parts = []
    for h in range(heads):
        inside = (lane >= h * head_size) & (lane < (h + 1) * head_size)
        parts.append(jnp.where(inside, rows, jnp.zeros_like(rows)))
    return jnp.concatenate(parts, axis=0)


def decayed(affinity, decays, heads):
    tiled = jnp.concatenate([affinity] * heads, axis=1) if heads > 1 else affinity
    return (tiled * decays.astype(f32)).astype(bf16)


def spans(k, state_size):
    rows = pl.ds(pl.multiple_of(k * CHUNK, CHUNK), CHUNK)
    return rows, pl.ds(pl.multiple_of(k * state_size, state_size), state_size)


def fill_mean(mean_ref, heads, head_size):
    row = lax.broadcasted_iota(jnp.int32, mean_ref.shape, 0)
    col = lax.broadcasted_iota(jnp.int32, mean_ref.shape, 1)
    same = jnp.zeros(mean_ref.shape, jnp.bool_)
    for h in range(heads):
        low, high = h * head_size, (h + 1) * head_size
        same |= (row >= low) & (row < high) & (col >= low) & (col < high)
    mean_ref[...] = jnp.where(same, 1.0 / head_size, 0.0).astype(bf16)


def forward_kernel(sources, arrays, slots, group, heads, head_size, place_ref, *refs):
    array_refs, refs = refs[:arrays], refs[arrays:]
    in_hbm, out_hbm, refs = refs[:7], refs[7:14], refs[14:]
    in_refs, out_refs, refs = refs[:7], refs[7:14], refs[14:]
    held, mean_ref, carry, y_ref, sems, loads, stores, y_sems = refs
    w_ref, m_ref, te_ref, fs_ref, en_ref, lv_ref, dt_ref = in_refs
    x_ref, b_ref, c_ref, z_ref, rs_ref, sf_ref, rn_ref = out_refs
    pieces = len(sources)
    rows_each = held.shape[1]
    width, state_size = x_ref.shape[1], b_ref.shape[1]
    chunks = dt_ref.shape[0]

    def fetch(i):
        array, start = sources[i]
        source = array_refs[array].at[pl.ds(start, rows_each)]
        return pltpu.make_async_copy(source, held.at[i % slots], sems.at[i % slots])

    in_loads = [
        pltpu.make_async_copy(source, target, loads.at[n])
        for n, (source, target) in enumerate(zip(in_hbm, in_refs))
    ]
    out_stores = [
        pltpu.make_async_copy(source, target, stores.at[n])
        for n, (source, target) in enumerate(zip(out_refs, out_hbm))
    ]
    in_loads[0].start()
    for i in range(slots):
        fetch(i).start()
    for load in in_loads[1:]:
        load.start()
    fill_mean(mean_ref, heads, head_size)

    in_loads[0].wait()
    for first in range(0, pieces, group):
        for i in range(first, first + group):
            fetch(i).wait()
        slot = first % slots
        block = held[slot : slot + group].reshape(group * rows_each, held.shape[2])
        result = dot_nn(block, w_ref[...]).astype(bf16)
        for i in range(first, first + group):
            if i + slots < pieces:
                fetch(i + slots).start()
            offset = (2 * lax.bitwise_xor(place_ref[0], i // 2) + i % 2) * rows_each
            target = pl.ds(pl.multiple_of(offset, rows_each), rows_each)
            part = slice((i - first) * rows_each, (i - first + 1) * rows_each)
            x_ref[target, :] = result[part, :width]
            b_ref[target, :] = result[part, width : width + state_size]
            c_ref[target, :] = result[part, width + state_size :]
    for store in out_stores[:3]:
        store.start()
    for load in in_loads[1:]:
        load.wait()

    carry[...] = jnp.zeros_like(carry)

    def reverse_states(i, _):
        k = chunks - 1 - i
        rows, state = spans(k, state_size)
        rn_ref[state, :] = carry[...].astype(bf16)
        term = dot_tn(b_ref[rows, :], x_ref[rows, :] * fs_ref[rows, :])
        carry[...] = dt_ref[k] * carry[...] + term
        return 0

    lax.fori_loop(0, chunks, reverse_states, 0, unroll=16)
    out_stores[6].start()
    carry[...] = jnp.zeros_like(carry)

    def outputs(k, _):
        rows, state = spans(k, state_size)
        x, b, c = x_ref[rows, :], b_ref[rows, :], c_ref[rows, :]
        state_in = carry[...].astype(bf16)
        sf_ref[state, :] = state_in
        weights = decayed(dot_nt(c, b), m_ref[rows, :], heads)
        y = dot_nn(weights, by_head(x, heads, head_size))
        y = y + en_ref[rows, :].astype(f32) * dot_nn(c, state_in)
        y = y + lv_ref[rows, :].astype(f32) * dot_nn(c, rn_ref[state, :])
        y_ref[rows, :] = y
        carry[...] = dt_ref[k] * carry[...] + dot_tn(b, x * te_ref[rows, :])
        return 0

    lax.fori_loop(0, chunks, outputs, 0, unroll=16)
    out_stores[5].start()
    block_stores = []
    block = y_ref.shape[0] // (y_sems.shape[0] // 2)
    for n in range(y_sems.shape[0] // 2):
        rows = pl.ds(n * block, block)
        y = y_ref[rows, :]
        mean_square = dot_nn((y * y).astype(bf16), mean_ref[...])
        inverse = lax.rsqrt(mean_square + EPSILON)
        z_ref[rows, :] = (y * inverse).astype(bf16)
        rs_ref[rows, :] = inverse.astype(bf16)
        for m in (3, 4):
            source, target = out_refs[m].at[rows], out_hbm[m].at[rows]
            store = pltpu.make_async_copy(source, target, y_sems.at[2 * n + m - 3])
            store.start()
            block_stores.append(store)
    for store in out_stores[:3] + out_stores[5:] + block_stores:
        store.wait()


def backward_kernel(heads, head_size, *refs):
    in_hbm, out_hbm, refs = refs[:15], refs[15:17], refs[17:]
    in_refs, (dx_ref, shared_ref), refs = refs[:15], refs[15:17], refs[17:]
    dy_ref, ge_ref, mean_ref, carry, loads, stores = refs
    g_ref, z_ref, rs_ref, c_ref, en_ref, dt_ref = in_refs[:6]
    x_ref, b_ref, m_ref, mt_ref, te_ref, fs_ref, lv_ref, sf_ref, rn_ref = in_refs[6:15]
    state_size = b_ref.shape[1]
    chunks = dt_ref.shape[0]
    in_loads = [
        pltpu.make_async_copy(source, target, loads.at[n])
        for n, (source, target) in enumerate(zip(in_hbm, in_refs))
    ]
    for load in in_loads:
        load.start()
    fill_mean(mean_ref, heads, head_size)
    carry[...] = jnp.zeros_like(carry)
    for load in in_loads[:6]:
        load.wait()

    def end_adjoints(i, _):
        k = chunks - 1 - i
        rows, state = spans(k, state_size)
        g, z = g_ref[rows, :].astype(f32), z_ref[rows, :].astype(f32)
        mean_gz = dot_nn((g * z).astype(bf16), mean_ref[...])
        dy = ((g - z * mean_gz) * rs_ref[rows, :].astype(f32)).astype(bf16)
        dy_ref[rows, :] = dy
        ge_ref[state, :] = carry[...].astype(bf16)
        carry[...] = dt_ref[k] * carry[...] + dot_tn(c_ref[rows, :], dy * en_ref[rows, :])
        return 0

    lax.fori_loop(0, chunks, end_adjoints, 0, unroll=16)
    carry[...] = jnp.zeros_like(carry)
    for load in in_loads[6:]:
        load.wait()

    def gradients(k, _):
        rows, state = spans(k, state_size)
        x, b, c, dy = x_ref[rows, :], b_ref[rows, :], c_ref[rows, :], dy_ref[rows, :]
        te, fs, en, lv = te_ref[rows, :], fs_ref[rows, :], en_ref[rows, :], lv_ref[rows, :]
        ge, gs = ge_ref[state, :], carry[...].astype(bf16)
        grad_weights = dot_nt(dy, by_head(x, heads, head_size)) * m_ref[rows, :].astype(f32)
        da = grad_weights[:, :CHUNK]
        for h in range(1, heads):
            da = da + grad_weights[:, h * CHUNK : (h + 1) * CHUNK]
        da = da.astype(bf16)
        turned = decayed(dot_nt(b, c), mt_ref[rows, :], heads)
        dx = dot_nn(turned, by_head(dy, heads, head_size))
        dx = dx + te.astype(f32) * dot_nn(b, ge)
        dx = dx + fs.astype(f32) * dot_nn(b, gs)
        dx_ref[rows, :] = dx.astype(bf16)
        dy_lv = dy * lv
        dc = dot_nn(da, b) + dot_nt(dy * en, sf_ref[state, :]) + dot_nt(dy_lv, rn_ref[state, :])
        db = dot_tn(da, c) + dot_nt(x * te, ge) + dot_nt(x * fs, gs)
        shared_ref[:state_size, rows] = db.T.astype(bf16)
        shared_ref[state_size:, rows] = dc.T.astype(bf16)
        carry[...] = dt_ref[k] * carry[...] + dot_tn(c, dy_lv)
        return 0

    lax.fori_loop(0, chunks, gradients, 0, unroll=16)
    out_stores = [
        pltpu.make_async_copy(source, target, stores.at[n])
        for n, (source, target) in enumerate(zip((dx_ref, shared_ref), out_hbm))
    ]
    for store in out_stores:
        store.start()
    for store in out_stores:
        store.wait()


def sum_kernel(parts_ref, dx_ref, sum_ref, packed_ref):
    total = parts_ref[0].astype(f32)
    for n in range(1, parts_ref.shape[0]):
        total = total + parts_ref[n].astype(f32)
    total = total.astype(bf16)
    sum_ref[...] = total
    count = packed_ref.shape[0]
    part, tokens = total.shape[0], total.shape[1] // count
    if packed_ref.shape[1] > tokens + part or packed_ref.shape[2] > dx_ref.shape[1]:
        packed_ref[...] = jnp.zeros_like(packed_ref)
    for n in range(count):
        block = slice(n * tokens, (n + 1) * tokens)
        packed_ref[n, :tokens, : dx_ref.shape[1]] = dx_ref[block, :]
        packed_ref[n, tokens : tokens + part, :tokens] = total[:, block]


def tokens_kernel(layout, place_ref, packed_ref, *refs):
    arrays = len(layout)
    column_refs, out_ref, lhs_refs = refs[:arrays], refs[arrays], refs[arrays + 1 :]
    count = packed_ref.shape[0]
    tokens = out_ref.shape[1]

    @pl.when(pl.program_id(0) == 0)
    def _():
        for lhs_ref, parts in zip(lhs_refs, layout):
            column = 0
            for r, start, extent in parts:
                source = lax.bitwise_xor(place_ref[0], r)
                block = packed_ref[source, :tokens, start : start + extent]
                lhs_ref[:, column : column + extent] = block
                column += extent
        width = layout[0][0][2]
        rows = (lhs_refs[0].shape[1] - width) // count
        turned = [packed_ref[n, tokens : tokens + rows, :tokens] for n in range(count)]
        lhs_refs[0][:, width:] = jnp.concatenate(turned, axis=0).T

    result = dot_nt(lhs_refs[0][...], column_refs[0][...])
    for lhs_ref, column_ref in zip(lhs_refs[1:], column_refs[1:]):
        result = result + dot_nt(lhs_ref[...], column_ref[:, : lhs_ref.shape[1]])
    out_ref[0] = result.astype(bf16)


def joined_tokens_kernel(layout, steps, place_ref, packed_ref, *refs):
    arrays = len(layout)
    column_refs, out_ref, joined_ref, lhs_ref, sems = refs[:arrays], *refs[arrays:]
    count = packed_ref.shape[0]
    tokens = out_ref.shape[1]
    rows = joined_ref.shape[1]
    width = layout[0][0][2]
    part = (joined_ref.shape[2] - count * width) // count
    loads = []
    for step in range(steps):
        column = 0
        for n, parts in enumerate(layout):
            extent = sum(p[2] for p in parts) + (count * part if n == 0 else 0)
            source = column_refs[n].at[pl.ds(step * rows, rows), pl.ds(0, extent)]
            target = joined_ref.at[step, :, pl.ds(column, extent)]
            loads.append(pltpu.make_async_copy(source, target, sems.at[step * arrays + n]))
            loads[-1].start()
            column += extent

    column = 0
    for n, parts in enumerate(layout):
        for r, start, extent in parts:
            source = lax.bitwise_xor(place_ref[0], r)
            block = packed_ref[source, :tokens, start : start + extent]
            lhs_ref[:, column : column + extent] = block
            column += extent
        if n == 0:
            turned = [packed_ref[m, tokens : tokens + part, :tokens] for m in range(count)]
            lhs_ref[:, column : column + count * part] = jnp.concatenate(turned, axis=0).T
            column += count * part
    for step in range(steps):
        for load in loads[step * arrays : (step + 1) * arrays]:
            load.wait()
        result = dot_nt(lhs_ref[...], joined_ref[step])
        out_ref[0, :, step * rows : (step + 1) * rows] = result.astype(bf16)


def spread_kernel(blocks_ref, out_ref):
    width = blocks_ref.shape[2]
    for n in range(blocks_ref.shape[0]):
        out_ref[0, :, n * width : (n + 1) * width] = blocks_ref[n]


def add_kernel(*refs):
    head_ref, shared_refs, out_ref = refs[0], refs[1:-1], refs[-1]
    rows = head_ref.shape[1]
    out_ref[:, :rows, :] = head_ref[...]
    total = shared_refs[0][...].astype(f32)
    for ref in shared_refs[1:]:
        total = total + ref[...].astype(f32)
    total = total.astype(bf16)
    if out_ref.shape[2] > total.shape[2]:
        out_ref[:, rows:, :] = jnp.zeros_like(out_ref[:, rows:, :])
    out_ref[:, rows:, : total.shape[2]] = total


def weight_kernel(sources, arrays, slots, group, parts, is_turned, places_ref, *refs):
    array_refs, grad_ref = refs[:arrays], refs[arrays]
    out_refs, (held, total, result, sems) = refs[arrays + 1 : -4], refs[-4:]
    pieces = len(sources)
    rows = held.shape[1]
    hidden = held.shape[2]

    def fetch(i):
        array, start = sources[i]
        source = array_refs[array].at[pl.ds(start, rows)]
        return pltpu.make_async_copy(source, held.at[i % slots], sems.at[i % slots])

    for i in range(slots):
        fetch(i).start()
    for first in range(0, pieces, group):
        turned = []
        for i in range(first, first + group):
            offset = (2 * lax.bitwise_xor(places_ref[0], i // 2) + i % 2) * rows
            target = pl.ds(pl.multiple_of(offset, rows), rows)
            turned.append(grad_ref[:, target] if is_turned else grad_ref[target, :].T)
        for i in range(first, first + group):
            fetch(i).wait()
        slot = first % slots
        block = held[slot : slot + group].reshape(group * rows, hidden)
        term = dot_nn(jnp.concatenate(turned, axis=1), block)
        if first > 0:
            term = term + total[...]
        if first + group < pieces:
            total[...] = term
        else:
            result[...] = term.T.astype(bf16)
        for i in range(first, first + group):
            if i + slots < pieces:
                fetch(i + slots).start()
    columns = result.shape[1]
    each = out_refs[0].shape[-2] * out_refs[0].shape[-1] // columns
    count = hidden // (parts * each)
    for k in range(parts):
        for j in range(count):
            if len(out_refs) == 1:
                out_refs[0][k, j] = result[(j * parts + k) * each : (j * parts + k + 1) * each, :]
                continue
            mine = (j * parts + lax.bitwise_xor(places_ref[1], k)) * each
            rows = out_refs[k].shape[1]
            for q in range(each // rows):
                source = pl.ds(pl.multiple_of(mine + q * rows, rows), rows)
                out_refs[k][j, :, q * columns : (q + 1) * columns] = result[source, :]


def finish_kernel(packed_ref, out_ref):
    count, _, width = packed_ref.shape
    rows = out_ref.shape[0]
    extra = packed_ref.shape[1] - rows
    part = (out_ref.shape[1] - count * width) // count
    for n in range(count):
        out_ref[:, n * width : (n + 1) * width] = packed_ref[n, :rows].astype(f32)
        start = count * width + n * part
        for q in range(rows // extra):
            block = packed_ref[n, rows:, q * part : (q + 1) * part]
            out_ref[q * extra : (q + 1) * extra, start : start + part] = block.astype(f32)


def resident(array):
    return pl.BlockSpec(array.shape, lambda k: (0,) * len(array.shape))


def after(value, *earlier):
    return lax.optimization_barrier((value,) + earlier)[0]


def permute_xor(a, axis, mask):
    count = lax.axis_size(axis)
    return lax.ppermute(a, axis, [(i, i ^ mask) for i in range(count)])


def gather_rows(rows, axis, beside, work):
    count = lax.axis_size(axis)
    bits = count.bit_length() - 1
    half = rows.shape[0] // 2
    if bits == 3:
        held = {r: permute_xor(rows, axis, r) for r in (2, 4, 1)}
        held, beside = lax.optimization_barrier((held, beside))
        held[3], held[5] = permute_xor(held[2], axis, 1), permute_xor(held[4], axis, 1)
        corner = [
            permute_xor(held[2][:half], axis, 4),
            permute_xor(held[4][half:], axis, 2),
        ]
        held, corner, done = lax.optimization_barrier((held, corner, work(*beside)))
        held = {r: [a] for r, a in held.items()}
        held[0], held[6] = [rows], corner
        held[7] = [permute_xor(a, axis, 1) for a in corner]
    else:
        done = work(*beside)
        upper = list(range(1, bits))
        orders = (upper + [0], upper[1:] + upper[:1] + [0])
        both = ({0: rows[:half]}, {0: rows[half:]})
        for step in range(bits):
            for part in range(2):
                mask = 1 << orders[part][step]
                for r in list(both[part]):
                    both[part][r ^ mask] = permute_xor(both[part][r], axis, mask)
        held = {r: [both[0][r], both[1][r]] for r in range(count)}
    arrays, sources = [], []
    for r in range(count):
        for part in range(2):
            whole_block = len(held[r]) == 1
            if part == 0 or not whole_block:
                arrays.append(held[r][part])
            sources.append((len(arrays) - 1, half * part if whole_block else 0))
    return arrays, tuple(sources), done


def exchange_xor(pieces, axis):
    return [pieces[0]] + [permute_xor(p, axis, r) for r, p in enumerate(pieces) if r > 0]


def tables_kernel(log_ref, *refs):
    out_refs, table_refs, sems = refs[:7], refs[7:14], refs[14]
    te_ref, fs_ref, en_ref, lv_ref, dt_ref, m_ref, mt_ref = table_refs
    heads = log_ref.shape[0]
    chunks = dt_ref.shape[0]
    head_size = te_ref.shape[1] // heads
    row = lax.broadcasted_iota(jnp.int32, (CHUNK, CHUNK), 0)
    col = lax.broadcasted_iota(jnp.int32, (CHUNK, CHUNK), 1)
    logs = jnp.concatenate(
        [log_ref[:, k * CHUNK : (k + 1) * CHUNK] for k in range(chunks)], axis=0
    )
    cumulative = lax.dot_general(
        logs, (row <= col).astype(f32), (((1,), (0,)), ((), ())),
        precision=lax.Precision.HIGHEST, preferred_element_type=f32,
    )
    exclusive = cumulative - logs
    cum_t, exc_t = cumulative.T, exclusive.T
    total = cum_t[CHUNK - 1 : CHUNK, :]
    spreads = (
        (te_ref, jnp.exp(total - cum_t)),
        (fs_ref, jnp.exp(exc_t)),
        (en_ref, jnp.exp(cum_t)),
        (lv_ref, jnp.exp(total - exc_t)),
    )
    chunk_decay = jnp.exp(total)
    diagonal = (row == col).astype(f32)
    for k in range(chunks):
        rows = slice(k * CHUNK, (k + 1) * CHUNK)
        picked = range(k * heads, (k + 1) * heads)
        for ref, source in spreads:
            ref[rows, :] = jnp.concatenate(
                [jnp.broadcast_to(source[:, n : n + 1], (CHUNK, head_size)) for n in picked], axis=1
            ).astype(bf16)
        dt_ref[k] = jnp.concatenate(
            [jnp.broadcast_to(chunk_decay[:, n : n + 1], (1, head_size)) for n in picked], axis=1
        )
        for h, n in enumerate(picked):
            cum_col, exc_col = cum_t[:, n : n + 1], exc_t[:, n : n + 1]
            cum_row, exc_row = cumulative[n : n + 1, :], exclusive[n : n + 1, :]
            below, above = cum_col - cum_row, exc_row - exc_col
            exponent = jnp.where(row > col, below, jnp.where(row < col, above, 0.0))
            turned = jnp.where(row < col, -below, jnp.where(row > col, -above, 0.0))
            columns = slice(h * CHUNK, (h + 1) * CHUNK)
            m_ref[rows, columns] = (jnp.exp(exponent) + diagonal).astype(bf16)
            mt_ref[rows, columns] = (jnp.exp(turned) + diagonal).astype(bf16)
    stores = [
        pltpu.make_async_copy(source, target, sems.at[n])
        for n, (source, target) in enumerate(zip(table_refs, out_refs))
    ]
    for store in stores:
        store.start()
    for store in stores:
        store.wait()


def on_device(tokens, w_in, log_decay, grad_out):
    local_tokens = tokens[0]
    upstream = grad_out[0]
    token_count, hidden_width = local_tokens.shape
    head_count = log_decay.shape[1]
    inner_width = upstream.shape[1]
    head_size = inner_width // head_count
    state_size = (w_in.shape[1] - inner_width) // 2
    seq_count = lax.axis_size("seq")
    fsdp_count = lax.axis_size("fsdp")
    place = lax.axis_index("seq")
    row_place = lax.axis_index("fsdp")
    heads = head_count // seq_count
    width = heads * head_size
    length = token_count * seq_count
    shared = 2 * state_size
    chunks = length // CHUNK
    shape = jax.ShapeDtypeStruct
    params = pltpu.CompilerParams(vmem_limit_bytes=VMEM_LIMIT)
    scalar = [pl.BlockSpec(memory_space=pltpu.SMEM)]
    places = jnp.stack([place, row_place]).astype(jnp.int32)

    def cost(flops, moved):
        return pl.CostEstimate(flops=flops, bytes_accessed=moved, transcendentals=0)

    def columns(r):
        return lax.dynamic_slice_in_dim(w_in, lax.bitwise_xor(place, r) * width, width, 1)

    w_columns = lax.all_gather(
        jnp.concatenate([columns(0), w_in[:, inner_width:]], axis=1), "fsdp", axis=0, tiled=True
    )
    log_rates = lax.all_to_all(log_decay[0], "seq", 0, 1, tiled=True)

    table_shapes = (
        [shape((length, width), bf16)] * 4
        + [shape((chunks, 1, width), f32)]
        + [shape((length, heads * CHUNK), bf16)] * 2
    )
    in_hbm = [pl.BlockSpec(memory_space=pltpu.HBM)]
    scratch = lambda *buffers: [pltpu.VMEM(a.shape, a.dtype) for a in buffers]
    make_tables = pl.pallas_call(
        tables_kernel,
        grid=(1,),
        out_shape=table_shapes,
        in_specs=[resident(log_rates)],
        out_specs=in_hbm * 7,
        scratch_shapes=scratch(*table_shapes) + [pltpu.SemaphoreType.DMA((7,))],
        compiler_params=params,
        cost_estimate=cost(0, 120 * length * width),
    )
    neighbours = [r for r in range(2, seq_count, 2) if r & (r - 1) == 0]
    others = [r for r in range(2, seq_count, 2) if r & (r - 1)]
    first_part = width // 2
    rest = [columns(r) for r in others] + [columns(r)[:, :first_part] for r in neighbours]

    blocks = upstream.reshape(token_count, seq_count, width).transpose(1, 0, 2)
    rest = jnp.concatenate(rest, axis=1)
    arrays, sources, (tables, upstream, rest, places) = gather_rows(
        local_tokens,
        "seq",
        (log_rates, blocks, rest, places),
        lambda log_rates, *others: (make_tables(log_rates), *others),
    )
    to_end, from_start, enter, leave, chunk_decay, decays, turned = tables

    count = len(sources)
    slots = min(count, 16)
    group = min(slots, 4)
    held = shape((slots, token_count // 2, hidden_width), bf16)
    by_position = shape((length, width), bf16)
    by_state = shape((chunks * state_size, width), bf16)
    state_rows = shape((length, state_size), bf16)
    mean = shape((width, width), bf16)
    carry = shape((state_size, width), f32)

    w_even = lax.all_gather(rest, "fsdp", axis=0, tiled=True)
    upstream = after(upstream, w_columns)

    *arrays, w_columns = lax.optimization_barrier((*arrays, w_columns))
    g = lax.all_to_all(upstream, "seq", 0, 0).reshape(length, width)
    operands = (w_columns, decays, to_end, from_start, enter, leave, chunk_decay)
    kept = [by_position, state_rows, state_rows, by_position, by_position, by_state, by_state]
    forward = pl.pallas_call(
        functools.partial(
            forward_kernel, sources, len(arrays), slots, group, heads, head_size
        ),
        out_shape=kept,
        in_specs=scalar + in_hbm * (len(arrays) + 7),
        out_specs=in_hbm * 7,
        scratch_shapes=scratch(*operands, *kept, held, mean, carry, shape((length, width), f32))
        + [
            pltpu.SemaphoreType.DMA((slots,)),
            pltpu.SemaphoreType.DMA((7,)),
            pltpu.SemaphoreType.DMA((7,)),
            pltpu.SemaphoreType.DMA((8,)),
        ],
        compiler_params=params,
        cost_estimate=cost(
            4 * length * hidden_width * (width + shared) + 160 * length * width * CHUNK,
            4 * length * hidden_width,
        ),
    )(places, *arrays, *operands)
    w_partner = permute_xor(w_columns, "seq", 1)
    forward, g, w_partner = lax.optimization_barrier((forward, g, w_partner))
    x, b, c, z, inverse, states_in, states_next = forward

    mixed_blocks = lax.all_to_all(z.reshape(seq_count, token_count, width), "seq", 0, 0)
    operands = (
        g, z, inverse, c, enter, chunk_decay,
        x, b, decays, turned, to_end, from_start, leave, states_in, states_next,
    )
    grads = [by_position, shape((shared, length), bf16)]
    backward = pl.pallas_call(
        functools.partial(backward_kernel, heads, head_size),
        out_shape=grads,
        in_specs=in_hbm * 15,
        out_specs=in_hbm * 2,
        scratch_shapes=scratch(*operands, *grads, by_position, by_state, mean, carry)
        + [pltpu.SemaphoreType.DMA((15,)), pltpu.SemaphoreType.DMA((2,))],
        compiler_params=params,
        cost_estimate=cost(240 * length * width * CHUNK, 40 * length * width),
    )(*operands)
    backward, mixed_blocks = lax.optimization_barrier((backward, mixed_blocks))
    dx, shared_partial = backward

    rows_each = hidden_width // (seq_count * fsdp_count)
    extra = 16

    def weight_columns(grad, columns, is_turned):
        total = shape((columns, hidden_width), f32)
        result = shape((hidden_width, columns), bf16)
        if not is_turned:
            parts = [shape((fsdp_count, seq_count, rows_each, columns), bf16)]
        else:
            parts = [shape((seq_count, extra, columns * rows_each // extra), bf16)] * fsdp_count
        return pl.pallas_call(
            functools.partial(weight_kernel, sources, len(arrays), slots, min(slots, 2), fsdp_count, is_turned),
            out_shape=parts,
            grid=(1,),
            in_specs=scalar + in_hbm * len(arrays) + [resident(grad)],
            out_specs=[resident(a) for a in parts],
            scratch_shapes=scratch(held, total, result) + [pltpu.SemaphoreType.DMA((slots,))],
            compiler_params=params,
            cost_estimate=cost(4 * length * hidden_width * columns, 4 * length * hidden_width),
        )(places, *arrays, grad)

    part = shared // seq_count
    arrived = lax.all_to_all(shared_partial.reshape(seq_count, part, length), "seq", 0, 0)
    (head_weights,) = weight_columns(dx, width, False)
    head_sums = lax.psum_scatter(
        head_weights.reshape(hidden_width, width), "fsdp", scatter_dimension=0, tiled=True
    ).reshape(seq_count, rows_each, width)
    second_part = after(w_columns, head_weights)[:, first_part:width]
    w_across = [permute_xor(second_part, "seq", r) for r in neighbours]
    arrived, second_part, w_even = lax.optimization_barrier((arrived, second_part, w_even))
    sums = [
        shape((part, length), bf16),
        shape((seq_count, token_count + max(part, 16), max(width, token_count)), bf16),
    ]
    shared_columns, packed = pl.pallas_call(
        sum_kernel,
        grid=(1,),
        out_shape=sums,
        in_specs=[resident(arrived), resident(dx)],
        out_specs=[resident(a) for a in sums],
        compiler_params=params,
    )(arrived, dx)

    grad_blocks = lax.all_to_all(packed, "seq", 0, 0)
    shared_weights = weight_columns(shared_columns, part, True)
    shared_arrived = exchange_xor(shared_weights, "fsdp")
    mixed_shape = shape((1, token_count, inner_width), bf16)
    mixer_out = pl.pallas_call(
        spread_kernel,
        grid=(1,),
        out_shape=mixed_shape,
        in_specs=[resident(mixed_blocks)],
        out_specs=resident(mixed_shape),
        compiler_params=params,
    )(after(mixed_blocks, second_part))
    w_even = [w_even, *(after(a, shared_weights[0]) for a in w_across)]
    w_odd = [permute_xor(a, "seq", 1) for a in w_even]
    shared_arrived, mixer_out, w_odd, head_sums = lax.optimization_barrier(
        (shared_arrived, mixer_out, w_odd, head_sums)
    )

    grad_tokens_shape = shape((1, token_count, hidden_width), bf16)
    layout = [[(r, 0, width) for r in others] + [(r, 0, first_part) for r in neighbours]]
    layout += [[(r, first_part, width - first_part)] for r in neighbours]
    odd_layout = [[(r + 1, start, extent) for r, start, extent in parts] for parts in layout]
    layout = [[(0, 0, width)], [(1, 0, width)]] + layout + odd_layout
    lhs_shapes = [
        shape((token_count, sum(part[2] for part in parts) + (shared if n == 0 else 0)), bf16)
        for n, parts in enumerate(layout)
    ]
    w_blocks = [w_columns, w_partner, *w_even, *w_odd]
    tokens_cost = cost(
        4 * token_count * hidden_width * (inner_width + shared),
        4 * hidden_width * (inner_width + shared),
    )
    if all(extent % 128 == 0 for parts in layout for _, _, extent in parts):
        steps = 4
        joined = shape((steps, hidden_width // steps, inner_width + shared), bf16)
        grad_tokens = pl.pallas_call(
            functools.partial(joined_tokens_kernel, layout, steps),
            grid=(1,),
            out_shape=grad_tokens_shape,
            in_specs=scalar + [resident(grad_blocks)] + in_hbm * len(w_blocks),
            out_specs=resident(grad_tokens_shape),
            scratch_shapes=scratch(joined, shape((token_count, inner_width + shared), bf16))
            + [pltpu.SemaphoreType.DMA((steps * len(w_blocks),))],
            compiler_params=params,
            cost_estimate=tokens_cost,
        )(places, grad_blocks, *w_blocks)
    else:
        steps = 2
        rows = hidden_width // steps
        by_rows = lambda a: pl.BlockSpec((rows, a.shape[1]), lambda k: (k, 0))
        grad_tokens = pl.pallas_call(
            functools.partial(tokens_kernel, layout),
            grid=(steps,),
            out_shape=grad_tokens_shape,
            in_specs=scalar + [resident(grad_blocks)] + [by_rows(a) for a in w_blocks],
            out_specs=pl.BlockSpec((1, token_count, rows), lambda k: (0, 0, k)),
            scratch_shapes=scratch(*lhs_shapes),
            compiler_params=params,
            cost_estimate=tokens_cost,
        )(places, grad_blocks, *w_blocks)
    packed = shape((seq_count, rows_each + extra, width), bf16)
    packed_sums = pl.pallas_call(
        add_kernel,
        grid=(1,),
        out_shape=packed,
        in_specs=[resident(a) for a in [head_sums, *shared_arrived]],
        out_specs=resident(packed),
        compiler_params=params,
    )(head_sums, *shared_arrived)
    owned = lax.all_to_all(after(packed_sums, grad_blocks), "seq", 0, 0)
    finished = shape((rows_each, inner_width + shared), f32)
    grad_weights = pl.pallas_call(
        finish_kernel,
        grid=(1,),
        out_shape=finished,
        in_specs=[resident(owned)],
        out_specs=resident(finished),
        compiler_params=params,
    )(owned)
    return mixer_out, grad_tokens, grad_weights


def solution(mesh):
    return jax.shard_map(
        on_device,
        mesh=mesh,
        in_specs=(
            P("fsdp", "seq", None),
            P("fsdp", None),
            P("fsdp", None, "seq"),
            P("fsdp", "seq", None),
        ),
        out_specs=(P("fsdp", "seq", None), P("fsdp", "seq", None), P(("seq", "fsdp"), None)),
        check_vma=False,
    )
```
